32 devices in a mesh: grp: 2 (over core), aux: 4 (over y, x), orb: 4 (over z).
Axes of the slice: x: 2, y: 2, z: 4, core: 2. Of those that a mesh axis runs over, the one named last changes fastest.
Arguments:
- fitted_tensor: bfloat16 [4, 8192, 8192], P('grp', 'aux', 'orb'), may hold values from -0.23925781 to 0.23925781
- block_mask: int32 [2, 64, 64], P('grp'), may hold values 0 or 1
- orbitals: bfloat16 [8192, 256], P('aux'), may hold values from -0.0625 to 0.0625
- nuclear: float32 [8192], replicated, may hold values from 0.5 to 1.5
- centres: float32 [3, 8192], replicated, may hold values from 0 to 8
- mm_positions: float32 [3, 32768], P(None, ('grp', 'aux', 'orb')), may hold values from 0 to 8
- mm_charges: float32 [32768], P(('grp', 'aux', 'orb')), may hold values from -0.12 to 0.12
- neighbours: int32 [32, 2], P(('grp', 'aux', 'orb')), may hold values from 0 to 63, all different within a row
Outputs:
- fock: float32 [8192, 8192], P(('aux', 'orb'))
- mm_potential: float32 [32768], P(('grp', 'aux', 'orb'))
The draws below stay inside these ranges and needn't reach their ends.
Inputs may be any that keep to these rules, and one draw needn't show every extreme that they name: `neighbours`: each row names 2 different blocks; every block is named by some row.
All inputs are finite; a program needn't handle non-finite values. No bound on the sum of `block_mask` on one device may be relied on, other than what follows from the above.
Results may differ from the reference program's by a relative error of at most 0.01.
Values may be sent and summed in bfloat16 or wider, within the bound.
A program may use at most 128 MiB of HBM per device.

```python
import jax
import jax.numpy as jnp
from jax import lax

BLK = 128
NBF = 8192
NBLK = 64
PH = 2
SLABS = 2
NAUX = 4
NOCC = 256
MD = 1024
NMMBLK = 32
NMM = 32768
NB = 2


def plant(drawn, own_key, smallest, largest):
    spot = [jax.random.randint(jax.random.fold_in(own_key, axis), (), 0, length) for axis, length in enumerate(drawn.shape)]
    main_axis = drawn.shape.index(max(drawn.shape))
    next_to = spot[:main_axis] + [(spot[main_axis] + 1) % drawn.shape[main_axis]] + spot[main_axis + 1:]
    return drawn.at[tuple(spot)].set(smallest).at[tuple(next_to)].set(largest)


def level_of(stream_key, shape, split, low, largest):
    def one(position, parts):
        heights = jax.random.uniform(jax.random.fold_in(jax.random.fold_in(stream_key, 6), position), (parts,), jnp.float32, low / len(split), largest / len(split))
        return jnp.repeat(jnp.exp(heights), shape[position] // parts).reshape((-1,) + (1,) * (len(shape) - position - 1))

    factor_of = one(*split[0])
    for cut in split[1:]:
        factor_of = factor_of * one(*cut)
    return factor_of


def choose_distinct(key, rows, amount, top, lift):
    sequence = jax.random.permutation(jax.random.fold_in(key, 1), amount)
    pull = sequence
    for power in range(3):
        pull = pull * pull // amount
    pull = pull * lift // amount
    lots = jax.random.randint(jax.random.fold_in(key, 2), (rows, amount), 0, 4096) + pull
    sure = jax.random.permutation(jax.random.fold_in(key, 3), rows)[jnp.arange(amount) % rows]
    lots = jnp.where(jnp.arange(rows)[:, None] == sure[None, :], 1 << 14, lots)
    score = lots * amount + jnp.arange(amount)
    return lax.top_k(score.astype(jnp.int32), top)[1].astype(jnp.int32)


def normal_values(own_key, dims, width, limit, pieces=(), kind=jnp.bfloat16):
    gain = level_of(own_key, dims, pieces, -0.22, 0.18) if pieces else 1.0
    entries = jax.random.normal(own_key, dims, jnp.float32) * width * gain
    return jnp.minimum(jnp.maximum(entries, -limit), limit).astype(kind)


def setup_inputs(seed: int = 0) -> dict:
    key_list = jax.random.split(jax.random.key(seed), 9)
    return {
        "fitted_tensor": normal_values(key_list[0], (NAUX, NBF, NBF), 0.04, 0.23925781, ((0, 2), (1, 4), (2, 4))),
        "block_mask": plant((jax.random.randint(key_list[1], (SLABS, NBLK, NBLK), 0, 4) < 3).astype(jnp.int32), jax.random.fold_in(key_list[1], 1), 0, 1),
        "orbitals": normal_values(key_list[2], (NBF, NOCC), NBF ** -0.5, 0.0625, ((0, 4),)),
        "nuclear": jnp.clip(jax.random.uniform(key_list[3], (NBF,), jnp.float32, 0.5, 1.5), 0.5, 1.5),
        "centres": jnp.clip(jax.random.uniform(key_list[4], (3, NBF), jnp.float32, 0.0, 8.0), 0.0, 8.0),
        "mm_positions": jnp.clip(8.0 * jax.random.uniform(key_list[5], (3, NMM), jnp.float32) ** level_of(key_list[5], (3, NMM), ((1, 32),), -0.2, 0.2), 0.0, 8.0),
        "mm_charges": normal_values(key_list[6], (NMM,), 0.02, 0.12, ((0, 32),), jnp.float32),
        "neighbours": choose_distinct(key_list[7], NMMBLK, NBLK, NB, 256),
    }


softening = 1.0

def near_kernel(picker, centre_blocks, charge_blocks, atom_xyz):
    near_xyz = jnp.einsum('kb,cbj->ckj', picker, centre_blocks, precision=lax.Precision.HIGHEST)
    near_xyz = near_xyz.reshape(3, picker.shape[0] * centre_blocks.shape[2])
    near_q = jnp.dot(picker, charge_blocks, precision=lax.Precision.HIGHEST).reshape(-1)
    offsets = near_xyz[:, :, None] - atom_xyz[:, None, :]
    kernel = lax.rsqrt(lax.optimization_barrier(jnp.sum(offsets * offsets, axis=0)) + softening)
    return (kernel, near_q)

def reference(fitted_tensor, block_mask, orbitals, nuclear, centres, mm_positions, mm_charges, neighbours):
    c_full = orbitals.astype(jnp.float32)
    slab_ids = (jnp.arange(NAUX, dtype=jnp.int32) // PH).astype(jnp.int32)

    def aux_step(totals, inputs):
        coulomb, exchange_sum = totals
        tensor_row, slab = inputs
        block_bits = block_mask[slab]
        wide_mask = jnp.repeat(jnp.repeat(block_bits, BLK, axis=0), BLK, axis=1).astype(jnp.bfloat16)
        masked = tensor_row * wide_mask
        masked_f = masked.astype(jnp.float32)
        products = jnp.dot(masked_f, c_full, precision=lax.Precision.HIGHEST).astype(jnp.bfloat16)
        product_f = products.astype(jnp.float32)
        density = (2.0 * jnp.sum(product_f * c_full)).astype(jnp.bfloat16)
        coulomb = coulomb + masked_f * density.astype(jnp.float32)
        exchange_sum = exchange_sum + jnp.dot(product_f, product_f.T, precision=lax.Precision.HIGHEST)
        return ((coulomb, exchange_sum), None)
    zeros_fock = jnp.zeros((NBF, NBF), jnp.float32)
    (coulomb, exchange_sum), _ = lax.scan(aux_step, (zeros_fock, zeros_fock), (fitted_tensor, slab_ids))
    population = 2.0 * lax.optimization_barrier(jnp.sum(c_full * c_full, axis=1))
    qm_charge = nuclear - population
    centre_blocks = centres.reshape(3, NBLK, BLK)
    charge_blocks = qm_charge.reshape(NBLK, BLK)
    atom_blocks = jnp.transpose(mm_positions.reshape(3, NMMBLK, MD), (1, 0, 2))
    charge_rows = mm_charges.reshape(NMMBLK, MD)

    def mm_step(field_sum, inputs):
        atom_xyz, atom_charge, near_ids = inputs
        picker = (near_ids[:, None] == jnp.arange(NBLK, dtype=jnp.int32)[None, :]).astype(jnp.float32)
        kernel, near_q = near_kernel(picker, centre_blocks, charge_blocks, atom_xyz)
        potential = jnp.dot(near_q, kernel, precision=lax.Precision.HIGHEST)
        contrib = jnp.dot(kernel, atom_charge, precision=lax.Precision.HIGHEST).reshape(NB, BLK)
        field_sum = field_sum + jnp.dot(picker.T, contrib, precision=lax.Precision.HIGHEST)
        return (field_sum, potential)
    field_sum, potentials = lax.scan(mm_step, jnp.zeros((NBLK, BLK), jnp.float32), (atom_blocks, charge_rows, neighbours))
    field_vec = field_sum.reshape(NBF)
    fock = coulomb - 0.5 * exchange_sum + jnp.diag(field_vec)
    return (fock, potentials.reshape(NMM))
```

```python
import functools

import jax
import jax.numpy as jnp
from jax import lax
from jax.experimental import pallas as pl
from jax.experimental.pallas import tpu as pltpu
from jax.sharding import PartitionSpec as P

BLK = 128
VMEM_LIMIT = 48 * 1024 * 1024

softening = 1.0


def near_kernel(picker, centre_blocks, atom_xyz):
    near_xyz = jnp.einsum("kb,cbj->ckj", picker, centre_blocks, precision=lax.Precision.HIGHEST)
    near_xyz = near_xyz.reshape(3, picker.shape[0] * centre_blocks.shape[2])
    offsets = near_xyz[:, :, None] - atom_xyz[:, None, :]
    return lax.rsqrt(jnp.sum(offsets * offsets, axis=0) + softening)


def products_kernel(t_ref, mask_ref, win_ref, c_ref, x_ref, dens_ref):
    parts, rows, cols = t_ref.shape
    row_mask = mask_ref[0]

    @pl.when(pl.program_id(0) == 0)
    def _():
        dens_ref[...] = jnp.zeros_like(dens_ref)

    own = c_ref[...].astype(jnp.float32)
    for p in range(parts):
        prod = jnp.dot(t_ref[p] * row_mask, win_ref[...], preferred_element_type=jnp.float32)
        x_ref[p] = prod.astype(x_ref.dtype)
        dens_ref[p] += jnp.sum((prod * own).reshape(rows // 8, 8, prod.shape[1]), axis=0)


def products_call(fitted, mask_rows, window_c, own_c):
    parts, rows, cols = fitted.shape
    nocc = window_c.shape[1]
    return pl.pallas_call(
        products_kernel,
        grid=(rows // BLK,),
        in_specs=[
            pl.BlockSpec((parts, BLK, cols), lambda i: (0, i, 0)),
            pl.BlockSpec((1, 1, cols), lambda i: (i, 0, 0)),
            pl.BlockSpec((cols, nocc), lambda i: (0, 0)),
            pl.BlockSpec((BLK, nocc), lambda i: (i, 0)),
        ],
        out_specs=[
            pl.BlockSpec((parts, BLK, nocc), lambda i: (0, i, 0)),
            pl.BlockSpec((parts, 8, nocc), lambda i: (0, 0, 0)),
        ],
        out_shape=[
            jax.ShapeDtypeStruct((parts, rows, nocc), jnp.bfloat16),
            jax.ShapeDtypeStruct((parts, 8, nocc), jnp.float32),
        ],
        compiler_params=pltpu.CompilerParams(vmem_limit_bytes=VMEM_LIMIT),
        cost_estimate=pl.CostEstimate(
            flops=2 * parts * rows * cols * nocc,
            bytes_accessed=2 * parts * rows * (cols + nocc),
            transcendentals=0,
        ),
        name="products",
    )(fitted, mask_rows, window_c, own_c)


def coulomb_kernel(place_ref, dens_ref, ta_ref, ma_ref, tk_ref, mk_ref, away_ref, kept_ref):
    for t_ref, mask_ref, out_ref in ((ta_ref, ma_ref, away_ref), (tk_ref, mk_ref, kept_ref)):
        total = t_ref[0].astype(jnp.float32) * dens_ref[0]
        for p in range(1, t_ref.shape[0]):
            total += t_ref[p].astype(jnp.float32) * dens_ref[p]
        out_ref[...] = (total * mask_ref[0].astype(jnp.float32)).astype(out_ref.dtype)


def coulomb_call(place, densities, fitted, mask_rows, half):
    parts, rows, cols = fitted.shape
    tile = min(BLK, half)
    steps = half // tile

    def away_tile(i, place_ref):
        return (place_ref[1] * 2 + 1 - place_ref[0]) * steps + i

    def kept_tile(i, place_ref):
        return (place_ref[1] * 2 + place_ref[0]) * steps + i

    def tensor_spec(which):
        return pl.BlockSpec((parts, tile, cols), lambda i, place_ref, d: (0, which(i, place_ref), 0))

    def mask_spec(which):
        return pl.BlockSpec(
            (1, 1, cols), lambda i, place_ref, d: (which(i, place_ref) * tile // BLK, 0, 0)
        )

    return pl.pallas_call(
        coulomb_kernel,
        grid_spec=pltpu.PrefetchScalarGridSpec(
            num_scalar_prefetch=2,
            grid=(steps,),
            in_specs=[
                tensor_spec(away_tile),
                mask_spec(away_tile),
                tensor_spec(kept_tile),
                mask_spec(kept_tile),
            ],
            out_specs=[pl.BlockSpec((tile, cols), lambda i, place_ref, d: (i, 0))] * 2,
        ),
        out_shape=[jax.ShapeDtypeStruct((half, cols), jnp.bfloat16)] * 2,
        compiler_params=pltpu.CompilerParams(vmem_limit_bytes=VMEM_LIMIT),
        cost_estimate=pl.CostEstimate(
            flops=4 * parts * half * cols,
            bytes_accessed=4 * half * cols * (parts + 1),
            transcendentals=0,
        ),
        name="coulomb",
    )(place, densities, fitted, mask_rows, fitted, mask_rows)


def fock_kernel(shifts, place_ref, own_ref, mate_ref, all_ref, mate_all_ref, field_ref, *refs):
    mine, theirs, out_ref = refs[:shifts], refs[shifts : 2 * shifts], refs[2 * shifts]
    parts = own_ref.shape[0]
    rows, cols = out_ref.shape
    half = rows // 2
    per_src = mine[0].shape[1] // cols
    dims = (((1,), (1,)), ((), ()))
    grp_id, row0, orb_id = place_ref[0], place_ref[1], place_ref[2]

    def slab(a, b):
        total = lax.dot_general(a[0], b[0], dims, preferred_element_type=jnp.float32)
        for p in range(1, parts):
            total += lax.dot_general(a[p], b[p], dims, preferred_element_type=jnp.float32)
        return total

    out_ref[...] = -0.5 * (slab(own_ref, all_ref) + slab(mate_ref, mate_all_ref))

    step = pl.program_id(0)
    shift = lax.rem(orb_id - step // per_src + shifts, shifts)
    col_in = pl.multiple_of(lax.rem(step, per_src) * cols, cols)
    own_row = pl.multiple_of(grp_id * half, half)
    mate_row = pl.multiple_of((1 - grp_id) * half, half)
    for k in range(shifts):

        @pl.when(shift == k)
        def _():
            out_ref[pl.ds(own_row, half), :] += mine[k][:, pl.ds(col_in, cols)].astype(jnp.float32)
            out_ref[pl.ds(mate_row, half), :] += theirs[k][:, pl.ds(col_in, cols)].astype(jnp.float32)

    col0 = step * cols

    @pl.when((row0 < col0 + cols) & (row0 + rows > col0))
    def _():
        row_ids = row0 + lax.broadcasted_iota(jnp.int32, (rows, cols), 0)
        col_ids = col0 + lax.broadcasted_iota(jnp.int32, (rows, cols), 1)
        out_ref[...] += jnp.where(row_ids == col_ids, field_ref[...], jnp.float32(0.0))


def fock_call(place, x_own, x_mate, x_all, x_mate_all, field_col, mine, theirs):
    parts, rows, nocc = x_own.shape
    total = x_all.shape[1]
    half, per_src = mine[0].shape
    cols = min(1024, per_src)
    own_spec = pl.BlockSpec((parts, rows, nocc), lambda j: (0, 0, 0))
    all_spec = pl.BlockSpec((parts, cols, nocc), lambda j: (0, j, 0))
    return pl.pallas_call(
        functools.partial(fock_kernel, len(mine)),
        grid=(total // cols,),
        in_specs=[
            pl.BlockSpec(memory_space=pltpu.SMEM),
            own_spec,
            own_spec,
            all_spec,
            all_spec,
            pl.BlockSpec((rows, 1), lambda j: (0, 0)),
        ]
        + [pl.BlockSpec((half, per_src), lambda j: (0, 0))] * (2 * len(mine)),
        out_specs=pl.BlockSpec((rows, cols), lambda j: (0, j)),
        out_shape=jax.ShapeDtypeStruct((rows, total), jnp.float32),
        compiler_params=pltpu.CompilerParams(vmem_limit_bytes=VMEM_LIMIT),
        cost_estimate=pl.CostEstimate(
            flops=4 * parts * rows * total * nocc,
            bytes_accessed=4 * parts * total * nocc + 4 * rows * total + 2 * rows * total,
            transcendentals=0,
        ),
        name="fock",
    )(place, x_own, x_mate, x_all, x_mate_all, field_col, *mine, *theirs)


def swap(value):
    return lax.ppermute(value, "grp", [(0, 1), (1, 0)])


def per_device(
    fitted_tensor, block_mask, orbitals, nuclear, centres, mm_positions, mm_charges, neighbours
):
    parts, row_span, col_span = fitted_tensor.shape
    nocc = orbitals.shape[1]
    orb_count = lax.axis_size("orb")
    aux_count = lax.axis_size("aux")
    grp_count = lax.axis_size("grp")
    grp_id = lax.axis_index("grp")
    aux_id = lax.axis_index("aux")
    orb_id = lax.axis_index("orb")
    own_span = row_span // orb_count
    half = own_span // 2
    block_total = block_mask.shape[1]
    row_start = aux_id * row_span
    col_start = orb_id * col_span

    if aux_count == orb_count:
        perm = [
            (a * orb_count + o, o * orb_count + a)
            for a in range(aux_count)
            for o in range(orb_count)
        ]
        c_half = lax.dynamic_slice_in_dim(orbitals, grp_id * (row_span // 2), row_span // 2, 0)
        c_half = lax.ppermute(c_half, ("aux", "orb"), perm)
        c_mate = swap(c_half)
        window_c = jnp.where(
            grp_id == 0, jnp.stack([c_half, c_mate]), jnp.stack([c_mate, c_half])
        ).reshape(col_span, nocc)
    else:
        whole_c = lax.all_gather(orbitals, "aux", axis=0, tiled=True)
        window_c = lax.dynamic_slice_in_dim(whole_c, col_start, col_span, 0)

    bits = lax.dynamic_slice(
        block_mask[0],
        (row_start // BLK, col_start // BLK),
        (row_span // BLK, col_span // BLK),
    ).astype(jnp.bfloat16)
    mask_rows = jnp.repeat(bits, BLK, axis=1)[:, None, :]

    own_float = orbitals.astype(jnp.float32)
    own_population = 2.0 * jnp.sum(own_float * own_float, axis=1)
    population = lax.all_gather(own_population, "aux", axis=0, tiled=True)
    centre_blocks = centres.reshape(3, block_total, BLK)
    picker = (neighbours[0][:, None] == jnp.arange(block_total, dtype=jnp.int32)[None, :]).astype(
        jnp.float32
    )
    kernel = near_kernel(picker, centre_blocks, mm_positions)
    contrib = jnp.dot(kernel, mm_charges, precision=lax.Precision.HIGHEST).reshape(
        picker.shape[0], BLK
    )
    field_part = jnp.dot(picker.T, contrib, precision=lax.Precision.HIGHEST)

    window_c, population = lax.optimization_barrier((window_c, population))
    qm_charge = nuclear - population
    charge_blocks = qm_charge.reshape(block_total, BLK)
    near_q = jnp.dot(picker, charge_blocks, precision=lax.Precision.HIGHEST).reshape(-1)
    mm_potential = jnp.dot(near_q, kernel, precision=lax.Precision.HIGHEST)

    x_part, dens_lanes = products_call(fitted_tensor, mask_rows, window_c, orbitals)
    dens_part = 2.0 * jnp.sum(dens_lanes, axis=(1, 2))
    dens_slots = jnp.zeros((grp_count, BLK), jnp.float32)
    dens_slots = lax.dynamic_update_slice(dens_slots, dens_part[None, :], (grp_id, 0))
    sums = lax.psum(jnp.concatenate([field_part, dens_slots], axis=0), ("grp", "aux", "orb"))

    x_blocks = x_part.reshape(parts, orb_count, own_span, nocc)
    targets = [lax.rem(orb_id + k, orb_count) for k in range(orb_count)]
    moves = [[(s, (s + k) % orb_count) for s in range(orb_count)] for k in range(orb_count)]
    arrived = []
    for k in range(1, orb_count):
        block = lax.dynamic_index_in_dim(x_blocks, targets[k], 1, keepdims=False)
        arrived.append(lax.ppermute(block, "orb", moves[k]))
    sums, *arrived = lax.optimization_barrier((sums, *arrived))
    field_vec = sums[:block_total].reshape(-1)
    densities = lax.dynamic_slice(sums, (block_total + grp_id, 0), (1, parts))[0]
    x_sum = lax.dynamic_index_in_dim(x_blocks, orb_id, 1, keepdims=False).astype(jnp.float32)
    for block in arrived:
        x_sum += block.astype(jnp.float32)
    x_own = x_sum.astype(jnp.bfloat16)
    x_mate = swap(x_own)
    x_all = lax.all_gather(x_own, ("aux", "orb"), axis=1, tiled=True)

    mine = [None] * orb_count
    for k in list(range(1, orb_count)) + [0]:
        at = jnp.stack([grp_id, targets[k]]).astype(jnp.int32)
        away, kept = coulomb_call(at, densities, fitted_tensor, mask_rows, half)
        both = (kept.astype(jnp.float32) + swap(away).astype(jnp.float32)).astype(jnp.bfloat16)
        mine[k] = lax.ppermute(both, "orb", moves[k]) if k else both
    x_all, *mine = lax.optimization_barrier((x_all, *mine))
    theirs = [swap(block) for block in mine]
    x_mate_all = swap(x_all)

    own_first = row_start + orb_id * own_span
    field_col = lax.dynamic_slice_in_dim(field_vec, own_first, own_span, 0)[:, None]
    place = jnp.stack([grp_id, own_first, orb_id]).astype(jnp.int32)
    fock = fock_call(place, x_own, x_mate, x_all, x_mate_all, field_col, mine, theirs)
    return (fock, mm_potential)


MESH = pl.DeviceIdType.MESH
CHUNKS = 8
GRID_VMEM = 58 * 1024 * 1024


def grid_kernel(
    t_hbm, mask_ref, c_ref, small_ref, out_ref, sums_ref,
    t_ref, cw_ref, xp_ref, ra_ref, rb_ref, xa_ref, xm_ref, xo_ref, mr_ref, cr_ref, eb_ref,
    s_ref, sr_ref, dens_ref,
    t_sem, c_send, c_recv, ra_send, ra_recv, rb_send, rb_recv, xe_send, xe_recv,
    pl_send, pl_recv, xm_send, xm_recv, xo_send, xo_recv, s_send, s_recv,
    mr_send, mr_recv, cr_send, cr_recv, om_send, om_recv, ol_sem,
):
    parts, rows, cols = t_ref.shape
    nocc = c_ref.shape[1]
    chunk = rows // CHUNKS
    own = rows // 4
    half = cols // 2
    quarter = cols // 4
    per = CHUNKS // 2
    g, a, z = lax.axis_index("grp"), lax.axis_index("aux"), lax.axis_index("orb")
    mate = (1 - g, a, z)
    is_mid = (z == 1) | (z == 2)
    is_end = (z == 0) | (z == 3)
    inner = jnp.where(z == 0, 1, 2)
    outer = jnp.where(z == 1, 0, 3)
    rel = lax.bitwise_xor(a, z)

    def plane(k):
        return (g, lax.bitwise_xor(a, k), z)

    def remote(src, dst, send, recv, device):
        return pltpu.make_async_remote_copy(
            src_ref=src, dst_ref=dst, send_sem=send, recv_sem=recv,
            device_id=device, device_id_type=MESH,
        )

    def t_copy(c):
        span = pl.ds(c * chunk, chunk)
        return pltpu.make_async_copy(t_hbm.at[:, span], t_ref.at[:, span], t_sem.at[c])

    for c in range(CHUNKS):
        t_copy(c).start()

    barrier = pltpu.get_barrier_semaphore()
    for peer in (
        mate, plane(1), plane(2), plane(3),
        (g, a, lax.rem(z + 1, 4)), (g, a, lax.rem(z + 2, 4)), (g, a, lax.rem(z + 3, 4)),
    ):
        pl.semaphore_signal(barrier, inc=1, device_id=peer, device_id_type=MESH)
    pl.semaphore_wait(barrier, 7)

    def quarter_copy(src_ref, q, slot, device):
        span = pl.ds(pl.multiple_of(q * quarter, quarter), quarter)
        return remote(src_ref.at[span], cw_ref.at[span], c_send.at[slot], c_recv.at[q], device)

    first, second = 2 * g, 2 * g + 1

    @pl.when(rel == 0)
    def _():
        quarter_copy(c_ref, first, 0, plane(1)).start()
        quarter_copy(c_ref, second, 1, plane(2)).start()
        quarter_copy(c_ref, second, 2, plane(1)).start()
        quarter_copy(c_ref, first, 3, plane(2)).start()
        cw_ref[...] = c_ref[...]

    @pl.when(rel != 0)
    def _():
        for rank in range(2):
            q = jnp.where(rel == 2, 2 * g + 1 - rank, 2 * g + rank)
            quarter_copy(cw_ref, q, 0, mate).wait_recv()
            if rank == 0:

                @pl.when(rel == 1)
                def _():
                    quarter_copy(cw_ref, q, 2, plane(2)).start()

                @pl.when(rel == 2)
                def _():
                    quarter_copy(cw_ref, q, 2, plane(1)).start()

            quarter_copy(cw_ref, q, rank, mate).start()
        for rank in range(2):
            quarter_copy(cw_ref, 2 * (1 - g) + rank, 0, mate).wait_recv()

    def x_span(c):
        return pl.ds(pl.multiple_of(c * chunk, chunk), chunk)

    def ra_copy(c):
        return remote(
            xp_ref.at[:, x_span(c)], ra_ref.at[:, x_span(c)], ra_send.at[c], ra_recv.at[c], (g, a, inner)
        )

    dens_ref[...] = jnp.zeros_like(dens_ref)

    def products_step(c, carry):
        t_copy(c).wait()
        span = x_span(c)
        c_rows = c_ref[span, :].astype(jnp.float32)
        blocks = chunk // BLK
        for p in range(parts):
            masked = jnp.concatenate(
                [
                    t_ref[p, pl.ds(pl.multiple_of(c * chunk + j * BLK, BLK), BLK), :]
                    * mask_ref[c * blocks + j]
                    for j in range(blocks)
                ],
                axis=0,
            )
            prod = jnp.dot(masked, cw_ref[...], preferred_element_type=jnp.float32)
            xp_ref[p, span, :] = prod.astype(jnp.bfloat16)
            dens_ref[p] += jnp.sum((prod * c_rows).reshape(chunk // 8, 8, nocc), axis=0)

        @pl.when(is_end)
        def _():
            ra_copy(c).start()

        return carry

    lax.fori_loop(0, CHUNKS, products_step, 0)

    small = s_ref.shape[0]
    s_ref[...] = small_ref[...]
    tile_rows = lax.broadcasted_iota(jnp.int32, (8, 128), 0)
    tile = jnp.zeros((8, 128), jnp.float32)
    for p in range(parts):
        lanes = jnp.sum(dens_ref[p], axis=0, keepdims=True)
        folded = lanes[:, :128]
        for j in range(1, nocc // 128):
            folded = folded + lanes[:, j * 128 : (j + 1) * 128]
        tile = tile + jnp.where(tile_rows == parts * g + p, folded, 0.0)
    s_ref[small - 8 :, :] = tile

    def s_copy(i):
        device = (mate, plane(1), plane(2))[i] if i < 3 else (g, a, lax.rem(z + i - 2, 4))
        return remote(s_ref, sr_ref.at[i], s_send.at[i], s_recv.at[i], device)

    def s_start(r):
        for i in ((0,), (1,), (2,), (3, 4, 5))[r]:
            s_copy(i).start()

    def s_finish(r):
        batch = ((0,), (1,), (2,), (3, 4, 5))[r]
        for i in batch:
            s_copy(i).wait()
        for i in batch:
            s_ref[...] += sr_ref[i]

    def rb_copy(c):
        return remote(
            xp_ref.at[:, x_span(c)], rb_ref.at[:, x_span(c)], rb_send.at[c], rb_recv.at[c], (g, a, 3 - z)
        )

    def xa_at(block, c):
        return xa_ref.at[:, pl.ds(pl.multiple_of(block * rows + c * chunk, chunk), chunk)]

    def xe_copy(c):
        return remote(xa_at(a, c), xa_at(a, c), xe_send.at[c], xe_recv.at[c], (g, a, outer))

    def pl_copy(c, k):
        return remote(
            xa_at(a, c), xa_at(a, c), pl_send.at[k - 1, c], pl_recv.at[k - 1, c], plane(k)
        )

    def pl_wait(c, k):
        block = lax.bitwise_xor(a, k)
        remote(
            xa_at(block, c), xa_at(block, c), pl_send.at[k - 1, c], pl_recv.at[k - 1, c], plane(k)
        ).wait_recv()

    def xm_copy(block, c):
        i = block * per + lax.rem(c, per)
        dst = xm_ref.at[:, pl.ds(pl.multiple_of(i * chunk, chunk), chunk)]
        return remote(xa_at(block, c), dst, xm_send.at[i], xm_recv.at[i], mate)

    def xo_copy(c):
        i = lax.rem(c, 2)
        dst = xo_ref.at[:, pl.ds(pl.multiple_of(i * chunk, chunk), chunk)]
        return remote(xa_at(a, c), dst, xo_send.at[i], xo_recv.at[i], mate)

    def for_mate(c):
        return c // per == 1 - g

    def publish(c):
        for k in (1, 2, 3):
            pl_copy(c, k).start()

        @pl.when(for_mate(c))
        def _():
            xm_copy(a, c).start()

        @pl.when(z == c // 2)
        def _():
            xo_copy(c).start()

    def stage_one(c):
        ra_copy(c).wait_recv()
        for p in range(parts):
            both = xp_ref[p, x_span(c), :].astype(jnp.float32) + ra_ref[p, x_span(c), :].astype(jnp.float32)
            xp_ref[p, x_span(c), :] = both.astype(jnp.bfloat16)
        rb_copy(c).start()

    def stage_two(c):
        rb_copy(c).wait_recv()
        for p in range(parts):
            both = xp_ref[p, x_span(c), :].astype(jnp.float32) + rb_ref[p, x_span(c), :].astype(jnp.float32)
            xa_ref[p, pl.ds(pl.multiple_of(a * rows + c * chunk, chunk), chunk), :] = both.astype(jnp.bfloat16)
        xe_copy(c).start()
        publish(c)

    def slot(t):
        @pl.when(is_mid & (t < CHUNKS))
        def _():
            stage_one(t)

        @pl.when(is_mid & (t >= 1) & (t <= CHUNKS))
        def _():
            stage_two(t - 1)

        @pl.when(is_end & (t >= 3))
        def _():
            xe_copy(t - 3).wait_recv()
            publish(t - 3)

    own_cols = pl.ds(pl.multiple_of(g * half, half), half)
    mate_cols = pl.ds(pl.multiple_of((1 - g) * half, half), half)

    def mr_copy(dest):
        span = pl.ds(pl.multiple_of(dest * own, own), own)
        return remote(
            t_ref.at[0, span, mate_cols], mr_ref.at[dest], mr_send.at[dest], mr_recv.at[dest], mate
        )

    def cr_copy(k):
        dest = lax.rem(z + k, 4)
        span = pl.ds(pl.multiple_of(dest * own, own), own)
        return remote(
            t_ref.at[1, span, own_cols], cr_ref.at[z], cr_send.at[k - 1], cr_recv.at[k - 1], (g, a, dest)
        )

    def cr_wait(k):
        src = lax.rem(z + 4 - k, 4)
        remote(
            t_ref.at[1, pl.ds(0, own), own_cols], cr_ref.at[src], cr_send.at[k - 1], cr_recv.at[k - 1], mate
        ).wait_recv()
        return src

    def coulomb_part(k, d):
        dest = lax.rem(z + k, 4)
        step = 32

        def body(i, carry):
            row = pl.multiple_of(dest * own + i * step, step)
            span = pl.ds(row, step)
            total = t_ref[0, span, :].astype(jnp.float32) * d[0]
            for p in range(1, parts):
                total += t_ref[p, span, :].astype(jnp.float32) * d[p]
            total = total * mask_ref[row // BLK].astype(jnp.float32)
            t_ref[0, span, :] = total.astype(jnp.bfloat16)
            return carry

        lax.fori_loop(0, own // step, body, 0)
        mr_copy(dest).start()

    def coulomb_sum(k):
        dest = lax.rem(z + k, 4)
        mr_copy(dest).wait_recv()
        step = 64

        def body(i, carry):
            span = pl.ds(pl.multiple_of(dest * own + i * step, step), step)
            piece = pl.ds(pl.multiple_of(i * step, step), step)
            both = t_ref[0, span, own_cols].astype(jnp.float32) + mr_ref[dest, piece, :].astype(jnp.float32)
            if k:
                t_ref[1, span, own_cols] = both.astype(jnp.bfloat16)
            else:
                cr_ref[dest, piece, :] = both.astype(jnp.bfloat16)
            return carry

        lax.fori_loop(0, own // step, body, 0)
        if k:
            cr_copy(k).start()

    s_start(0)
    slot(0)
    s_finish(0)
    s_start(1)
    s_finish(1)
    s_start(2)
    slot(1)
    s_finish(2)
    s_start(3)
    slot(2)
    s_finish(3)
    sums_ref[...] = s_ref[...]
    dens_tile = s_ref[small - 8 :, :]
    d = []
    for p in range(parts):
        row = jnp.where(tile_rows == parts * g + p, dens_tile, 0.0)
        value = 2.0 * jnp.sum(jnp.sum(row, axis=1, keepdims=True), axis=0, keepdims=True)
        d.append(value.astype(jnp.bfloat16).astype(jnp.float32))
    order = (2, 1, 3, 0)
    slot(3)
    coulomb_part(order[0], d)
    for i in range(1, 4):
        coulomb_part(order[i], d)
        coulomb_sum(order[i - 1])
        slot(3 + i)
    coulomb_sum(order[3])
    for t in range(7, CHUNKS + 3):
        slot(t)

    def arrive(c, carry):
        for k in (1, 2, 3):
            pl_wait(c, k)

            @pl.when(for_mate(c))
            def _():
                xm_copy(lax.bitwise_xor(a, k), c).start()

        return carry

    lax.fori_loop(0, CHUNKS, arrive, 0)

    for i in range(2):
        xo_copy(i).wait_recv()
    dims = (((1,), (1,)), ((), ()))
    own_rows = pl.ds(pl.multiple_of(a * rows + z * own, own), own)

    def exchange(block, carry):
        def body(j, inside):
            i = block * per + j
            xm_copy(block, j).wait_recv()
            total = jnp.zeros((own, chunk), jnp.float32)
            near = pl.ds(pl.multiple_of(block * rows + g * half + j * chunk, chunk), chunk)
            far = pl.ds(pl.multiple_of(i * chunk, chunk), chunk)
            for p in range(parts):
                total += lax.dot_general(
                    xa_ref[p, own_rows, :], xa_ref[p, near, :], dims, preferred_element_type=jnp.float32
                )
                total += lax.dot_general(
                    xo_ref[p], xm_ref[p, far, :], dims, preferred_element_type=jnp.float32
                )
            eb_ref[block, :, pl.ds(pl.multiple_of(j * chunk, chunk), chunk)] = (-0.5 * total).astype(jnp.bfloat16)
            return inside

        return lax.fori_loop(0, per, body, carry)

    lax.fori_loop(0, 4, exchange, 0)

    def out_cols(block, core):
        return pl.ds(pl.multiple_of(block * cols + core * half, half), half)

    def om_copy(block):
        return remote(
            eb_ref.at[block], out_ref.at[:, out_cols(block, g)], om_send.at[block], om_recv.at[block], mate
        )

    def ol_copy(block):
        return pltpu.make_async_copy(eb_ref.at[block], out_ref.at[:, out_cols(block, g)], ol_sem.at[block])

    for k in (0, 1, 3, 2):
        src = cr_wait(k) if k else z
        step = 64

        def body(i, carry):
            piece = pl.ds(pl.multiple_of(i * step, step), step)
            both = eb_ref[src, piece, :].astype(jnp.float32) + cr_ref[src, piece, :].astype(jnp.float32)
            eb_ref[src, piece, :] = both.astype(jnp.bfloat16)
            return carry

        lax.fori_loop(0, own // step, body, 0)
        om_copy(src).start()
        ol_copy(src).start()

    for block in range(4):
        remote(
            eb_ref.at[block], out_ref.at[:, out_cols(block, 1 - g)], om_send.at[block], om_recv.at[block], mate
        ).wait()
        ol_copy(block).wait()
        mr_copy(block).wait_send()
    for k in (1, 2, 3):
        cr_copy(k).wait_send()

    @pl.when(rel == 0)
    def _():
        for i in range(4):
            quarter_copy(c_ref, first, i, mate).wait_send()

    @pl.when(rel != 0)
    def _():
        for i in range(2):
            quarter_copy(cw_ref, first, i, mate).wait_send()

    @pl.when((rel == 1) | (rel == 2))
    def _():
        quarter_copy(cw_ref, first, 2, mate).wait_send()

    def drain(c, carry):
        @pl.when(is_end)
        def _():
            ra_copy(c).wait_send()

        @pl.when(is_mid)
        def _():
            rb_copy(c).wait_send()
            xe_copy(c).wait_send()

        for k in (1, 2, 3):
            pl_copy(c, k).wait_send()

        @pl.when(for_mate(c))
        def _():
            for block in range(4):
                xm_copy(block, c).wait_send()

        return carry

    lax.fori_loop(0, CHUNKS, drain, 0)
    for i in range(2):
        xo_copy(i).wait_send()


def grid_call(fitted, mask_rows, own_c, small):
    parts, rows, cols = fitted.shape
    nocc = own_c.shape[1]
    own, half = rows // 4, cols // 2
    bf16, f32 = jnp.bfloat16, jnp.float32
    vmem = pl.BlockSpec(memory_space=pltpu.VMEM)
    hbm = pl.BlockSpec(memory_space=pl.ANY)
    dma = pltpu.SemaphoreType.DMA
    return pl.pallas_call(
        grid_kernel,
        in_specs=[hbm, vmem, vmem, vmem],
        out_specs=[hbm, vmem],
        out_shape=[
            jax.ShapeDtypeStruct((own, 4 * cols), bf16),
            jax.ShapeDtypeStruct(small.shape, f32),
        ],
        scratch_shapes=[
            pltpu.VMEM((parts, rows, cols), bf16),
            pltpu.VMEM((cols, nocc), bf16),
            pltpu.VMEM((parts, rows, nocc), bf16),
            pltpu.VMEM((parts, rows, nocc), bf16),
            pltpu.VMEM((parts, rows, nocc), bf16),
            pltpu.VMEM((parts, 4 * rows, nocc), bf16),
            pltpu.VMEM((parts, 2 * rows, nocc), bf16),
            pltpu.VMEM((parts, own, nocc), bf16),
            pltpu.VMEM((4, own, half), bf16),
            pltpu.VMEM((4, own, half), bf16),
            pltpu.VMEM((4, own, half), bf16),
            pltpu.VMEM(small.shape, f32),
            pltpu.VMEM((6,) + small.shape, f32),
            pltpu.VMEM((parts, 8, nocc), f32),
            dma((CHUNKS,)),
            dma((4,)), dma((4,)),
            dma((CHUNKS,)), dma((CHUNKS,)),
            dma((CHUNKS,)), dma((CHUNKS,)),
            dma((CHUNKS,)), dma((CHUNKS,)),
            dma((3, CHUNKS)), dma((3, CHUNKS)),
            dma((2 * CHUNKS,)), dma((2 * CHUNKS,)),
            dma((2,)), dma((2,)),
            dma((6,)), dma((6,)),
            dma((4,)), dma((4,)),
            dma((3,)), dma((3,)),
            dma((4,)), dma((4,)),
            dma((4,)),
        ],
        compiler_params=pltpu.CompilerParams(
            collective_id=0, has_side_effects=True, vmem_limit_bytes=GRID_VMEM
        ),
        cost_estimate=pl.CostEstimate(
            flops=2 * parts * rows * cols * nocc + 8 * parts * own * 2 * cols * nocc,
            bytes_accessed=2 * parts * rows * cols + 8 * own * cols,
            transcendentals=0,
        ),
        name="grid",
    )(fitted, mask_rows, own_c, small)


def per_device_grid(
    fitted_tensor, block_mask, orbitals, nuclear, centres, mm_positions, mm_charges, neighbours
):
    parts, row_span, col_span = fitted_tensor.shape
    grp_id = lax.axis_index("grp")
    aux_id = lax.axis_index("aux")
    orb_id = lax.axis_index("orb")
    own_span = row_span // 4
    block_total = block_mask.shape[1]
    row_start = aux_id * row_span
    bits = lax.dynamic_slice(
        block_mask[0],
        (row_start // BLK, orb_id * (col_span // BLK)),
        (row_span // BLK, col_span // BLK),
    ).astype(jnp.bfloat16)
    mask_rows = jnp.repeat(bits, BLK, axis=1)[:, None, :]

    own_float = orbitals.astype(jnp.float32)
    population = 2.0 * jnp.sum(own_float * own_float, axis=1)
    population = jnp.where((grp_id == 0) & (orb_id == 0), population, 0.0)
    population = lax.dynamic_update_slice(
        jnp.zeros((block_total, BLK), jnp.float32),
        population.reshape(row_span // BLK, BLK),
        (aux_id * (row_span // BLK), 0),
    )
    centre_blocks = centres.reshape(3, block_total, BLK)
    picker = (neighbours[0][:, None] == jnp.arange(block_total, dtype=jnp.int32)[None, :]).astype(
        jnp.float32
    )
    kernel = near_kernel(picker, centre_blocks, mm_positions)
    contrib = jnp.dot(kernel, mm_charges, precision=lax.Precision.HIGHEST).reshape(
        picker.shape[0], BLK
    )
    field_part = jnp.dot(picker.T, contrib, precision=lax.Precision.HIGHEST)
    small = jnp.concatenate([field_part, population, jnp.zeros((8, BLK), jnp.float32)], axis=0)

    fock16, sums = grid_call(fitted_tensor, mask_rows, orbitals, small)

    own_first = row_start + orb_id * own_span
    field_vec = sums[:block_total].reshape(-1)
    field_own = lax.dynamic_slice_in_dim(field_vec, own_first, own_span, 0)
    row_ids = own_first + lax.broadcasted_iota(jnp.int32, fock16.shape, 0)
    col_ids = lax.broadcasted_iota(jnp.int32, fock16.shape, 1)
    fock = fock16.astype(jnp.float32) + jnp.where(row_ids == col_ids, field_own[:, None], 0.0)

    charge_blocks = nuclear.reshape(block_total, BLK) - sums[block_total : 2 * block_total]
    near_q = jnp.dot(picker, charge_blocks, precision=lax.Precision.HIGHEST).reshape(-1)
    mm_potential = jnp.dot(near_q, kernel, precision=lax.Precision.HIGHEST)
    return (fock, mm_potential)


def grid_fits(mesh, fitted_tensor, orbitals):
    shape = mesh.shape
    parts = fitted_tensor.shape[0] // shape["grp"]
    rows = fitted_tensor.shape[1] // shape["aux"]
    cols = fitted_tensor.shape[2] // shape["orb"]
    return (
        shape["grp"] == 2
        and shape["aux"] == 4
        and shape["orb"] == 4
        and parts == 2
        and rows == cols
        and rows % (CHUNKS * BLK) == 0
        and orbitals.shape[1] % BLK == 0
        and 7 * rows * cols + 41 * rows * orbitals.shape[1] <= 52 * 2**20
    )


def solution(mesh):
    in_specs = (
        P("grp", "aux", "orb"),
        P("grp", None, None),
        P("aux", None),
        P(),
        P(),
        P(None, ("grp", "aux", "orb")),
        P(("grp", "aux", "orb")),
        P(("grp", "aux", "orb"), None),
    )
    out_specs = (P(("aux", "orb"), None), P(("grp", "aux", "orb")))
    def build(body):
        return jax.shard_map(
            body, mesh=mesh, in_specs=in_specs, out_specs=out_specs, check_vma=False
        )

    def run(fitted_tensor, block_mask, orbitals, *rest):
        body = per_device_grid if grid_fits(mesh, fitted_tensor, orbitals) else per_device
        return build(body)(fitted_tensor, block_mask, orbitals, *rest)

    return run
```

```python
import functools

import jax
import jax.numpy as jnp
from jax import lax
from jax.experimental import pallas as pl
from jax.experimental.pallas import tpu as pltpu
from jax.sharding import PartitionSpec as P

BLK = 128
VMEM_LIMIT = 48 * 1024 * 1024

softening = 1.0


def near_kernel(picker, centre_blocks, atom_xyz):
    near_xyz = jnp.einsum("kb,cbj->ckj", picker, centre_blocks, precision=lax.Precision.HIGHEST)
    near_xyz = near_xyz.reshape(3, picker.shape[0] * centre_blocks.shape[2])
    offsets = near_xyz[:, :, None] - atom_xyz[:, None, :]
    return lax.rsqrt(jnp.sum(offsets * offsets, axis=0) + softening)


def products_kernel(t_ref, mask_ref, win_ref, c_ref, x_ref, dens_ref):
    parts, rows, cols = t_ref.shape
    row_mask = mask_ref[0]

    @pl.when(pl.program_id(0) == 0)
    def _():
        dens_ref[...] = jnp.zeros_like(dens_ref)

    own = c_ref[...].astype(jnp.float32)
    for p in range(parts):
        prod = jnp.dot(t_ref[p] * row_mask, win_ref[...], preferred_element_type=jnp.float32)
        x_ref[p] = prod.astype(x_ref.dtype)
        dens_ref[p] += jnp.sum((prod * own).reshape(rows // 8, 8, prod.shape[1]), axis=0)


def products_call(fitted, mask_rows, window_c, own_c):
    parts, rows, cols = fitted.shape
    nocc = window_c.shape[1]
    return pl.pallas_call(
        products_kernel,
        grid=(rows // BLK,),
        in_specs=[
            pl.BlockSpec((parts, BLK, cols), lambda i: (0, i, 0)),
            pl.BlockSpec((1, 1, cols), lambda i: (i, 0, 0)),
            pl.BlockSpec((cols, nocc), lambda i: (0, 0)),
            pl.BlockSpec((BLK, nocc), lambda i: (i, 0)),
        ],
        out_specs=[
            pl.BlockSpec((parts, BLK, nocc), lambda i: (0, i, 0)),
            pl.BlockSpec((parts, 8, nocc), lambda i: (0, 0, 0)),
        ],
        out_shape=[
            jax.ShapeDtypeStruct((parts, rows, nocc), jnp.bfloat16),
            jax.ShapeDtypeStruct((parts, 8, nocc), jnp.float32),
        ],
        compiler_params=pltpu.CompilerParams(vmem_limit_bytes=VMEM_LIMIT),
        cost_estimate=pl.CostEstimate(
            flops=2 * parts * rows * cols * nocc,
            bytes_accessed=2 * parts * rows * (cols + nocc),
            transcendentals=0,
        ),
        name="products",
    )(fitted, mask_rows, window_c, own_c)


def coulomb_kernel(place_ref, dens_ref, ta_ref, ma_ref, tk_ref, mk_ref, away_ref, kept_ref):
    for t_ref, mask_ref, out_ref in ((ta_ref, ma_ref, away_ref), (tk_ref, mk_ref, kept_ref)):
        total = t_ref[0].astype(jnp.float32) * dens_ref[0]
        for p in range(1, t_ref.shape[0]):
            total += t_ref[p].astype(jnp.float32) * dens_ref[p]
        out_ref[...] = (total * mask_ref[0].astype(jnp.float32)).astype(out_ref.dtype)


def coulomb_call(place, densities, fitted, mask_rows, half):
    parts, rows, cols = fitted.shape
    tile = min(BLK, half)
    steps = half // tile

    def away_tile(i, place_ref):
        return (place_ref[1] * 2 + 1 - place_ref[0]) * steps + i

    def kept_tile(i, place_ref):
        return (place_ref[1] * 2 + place_ref[0]) * steps + i

    def tensor_spec(which):
        return pl.BlockSpec((parts, tile, cols), lambda i, place_ref, d: (0, which(i, place_ref), 0))

    def mask_spec(which):
        return pl.BlockSpec(
            (1, 1, cols), lambda i, place_ref, d: (which(i, place_ref) * tile // BLK, 0, 0)
        )

    return pl.pallas_call(
        coulomb_kernel,
        grid_spec=pltpu.PrefetchScalarGridSpec(
            num_scalar_prefetch=2,
            grid=(steps,),
            in_specs=[
                tensor_spec(away_tile),
                mask_spec(away_tile),
                tensor_spec(kept_tile),
                mask_spec(kept_tile),
            ],
            out_specs=[pl.BlockSpec((tile, cols), lambda i, place_ref, d: (i, 0))] * 2,
        ),
        out_shape=[jax.ShapeDtypeStruct((half, cols), jnp.bfloat16)] * 2,
        compiler_params=pltpu.CompilerParams(vmem_limit_bytes=VMEM_LIMIT),
        cost_estimate=pl.CostEstimate(
            flops=4 * parts * half * cols,
            bytes_accessed=4 * half * cols * (parts + 1),
            transcendentals=0,
        ),
        name="coulomb",
    )(place, densities, fitted, mask_rows, fitted, mask_rows)


def fock_kernel(shifts, place_ref, own_ref, mate_ref, all_ref, mate_all_ref, field_ref, *refs):
    mine, theirs, out_ref = refs[:shifts], refs[shifts : 2 * shifts], refs[2 * shifts]
    parts = own_ref.shape[0]
    rows, cols = out_ref.shape
    half = rows // 2
    per_src = mine[0].shape[1] // cols
    dims = (((1,), (1,)), ((), ()))
    grp_id, row0, orb_id = place_ref[0], place_ref[1], place_ref[2]

    def slab(a, b):
        total = lax.dot_general(a[0], b[0], dims, preferred_element_type=jnp.float32)
        for p in range(1, parts):
            total += lax.dot_general(a[p], b[p], dims, preferred_element_type=jnp.float32)
        return total

    out_ref[...] = -0.5 * (slab(own_ref, all_ref) + slab(mate_ref, mate_all_ref))

    step = pl.program_id(0)
    shift = lax.rem(orb_id - step // per_src + shifts, shifts)
    col_in = pl.multiple_of(lax.rem(step, per_src) * cols, cols)
    own_row = pl.multiple_of(grp_id * half, half)
    mate_row = pl.multiple_of((1 - grp_id) * half, half)
    for k in range(shifts):

        @pl.when(shift == k)
        def _():
            out_ref[pl.ds(own_row, half), :] += mine[k][:, pl.ds(col_in, cols)].astype(jnp.float32)
            out_ref[pl.ds(mate_row, half), :] += theirs[k][:, pl.ds(col_in, cols)].astype(jnp.float32)

    col0 = step * cols

    @pl.when((row0 < col0 + cols) & (row0 + rows > col0))
    def _():
        row_ids = row0 + lax.broadcasted_iota(jnp.int32, (rows, cols), 0)
        col_ids = col0 + lax.broadcasted_iota(jnp.int32, (rows, cols), 1)
        out_ref[...] += jnp.where(row_ids == col_ids, field_ref[...], jnp.float32(0.0))


def fock_call(place, x_own, x_mate, x_all, x_mate_all, field_col, mine, theirs):
    parts, rows, nocc = x_own.shape
    total = x_all.shape[1]
    half, per_src = mine[0].shape
    cols = min(1024, per_src)
    own_spec = pl.BlockSpec((parts, rows, nocc), lambda j: (0, 0, 0))
    all_spec = pl.BlockSpec((parts, cols, nocc), lambda j: (0, j, 0))
    return pl.pallas_call(
        functools.partial(fock_kernel, len(mine)),
        grid=(total // cols,),
        in_specs=[
            pl.BlockSpec(memory_space=pltpu.SMEM),
            own_spec,
            own_spec,
            all_spec,
            all_spec,
            pl.BlockSpec((rows, 1), lambda j: (0, 0)),
        ]
        + [pl.BlockSpec((half, per_src), lambda j: (0, 0))] * (2 * len(mine)),
        out_specs=pl.BlockSpec((rows, cols), lambda j: (0, j)),
        out_shape=jax.ShapeDtypeStruct((rows, total), jnp.float32),
        compiler_params=pltpu.CompilerParams(vmem_limit_bytes=VMEM_LIMIT),
        cost_estimate=pl.CostEstimate(
            flops=4 * parts * rows * total * nocc,
            bytes_accessed=4 * parts * total * nocc + 4 * rows * total + 2 * rows * total,
            transcendentals=0,
        ),
        name="fock",
    )(place, x_own, x_mate, x_all, x_mate_all, field_col, *mine, *theirs)


def swap(value):
    return lax.ppermute(value, "grp", [(0, 1), (1, 0)])


def per_device(
    fitted_tensor, block_mask, orbitals, nuclear, centres, mm_positions, mm_charges, neighbours
):
    parts, row_span, col_span = fitted_tensor.shape
    nocc = orbitals.shape[1]
    orb_count = lax.axis_size("orb")
    aux_count = lax.axis_size("aux")
    grp_count = lax.axis_size("grp")
    grp_id = lax.axis_index("grp")
    aux_id = lax.axis_index("aux")
    orb_id = lax.axis_index("orb")
    own_span = row_span // orb_count
    half = own_span // 2
    block_total = block_mask.shape[1]
    row_start = aux_id * row_span
    col_start = orb_id * col_span

    if aux_count == orb_count:
        perm = [
            (a * orb_count + o, o * orb_count + a)
            for a in range(aux_count)
            for o in range(orb_count)
        ]
        c_half = lax.dynamic_slice_in_dim(orbitals, grp_id * (row_span // 2), row_span // 2, 0)
        c_half = lax.ppermute(c_half, ("aux", "orb"), perm)
        c_mate = swap(c_half)
        window_c = jnp.where(
            grp_id == 0, jnp.stack([c_half, c_mate]), jnp.stack([c_mate, c_half])
        ).reshape(col_span, nocc)
    else:
        whole_c = lax.all_gather(orbitals, "aux", axis=0, tiled=True)
        window_c = lax.dynamic_slice_in_dim(whole_c, col_start, col_span, 0)

    bits = lax.dynamic_slice(
        block_mask[0],
        (row_start // BLK, col_start // BLK),
        (row_span // BLK, col_span // BLK),
    ).astype(jnp.bfloat16)
    mask_rows = jnp.repeat(bits, BLK, axis=1)[:, None, :]

    own_float = orbitals.astype(jnp.float32)
    own_population = 2.0 * jnp.sum(own_float * own_float, axis=1)
    population = lax.all_gather(own_population, "aux", axis=0, tiled=True)
    centre_blocks = centres.reshape(3, block_total, BLK)
    picker = (neighbours[0][:, None] == jnp.arange(block_total, dtype=jnp.int32)[None, :]).astype(
        jnp.float32
    )
    kernel = near_kernel(picker, centre_blocks, mm_positions)
    contrib = jnp.dot(kernel, mm_charges, precision=lax.Precision.HIGHEST).reshape(
        picker.shape[0], BLK
    )
    field_part = jnp.dot(picker.T, contrib, precision=lax.Precision.HIGHEST)

    window_c, population = lax.optimization_barrier((window_c, population))
    qm_charge = nuclear - population
    charge_blocks = qm_charge.reshape(block_total, BLK)
    near_q = jnp.dot(picker, charge_blocks, precision=lax.Precision.HIGHEST).reshape(-1)
    mm_potential = jnp.dot(near_q, kernel, precision=lax.Precision.HIGHEST)

    x_part, dens_lanes = products_call(fitted_tensor, mask_rows, window_c, orbitals)
    dens_part = 2.0 * jnp.sum(dens_lanes, axis=(1, 2))
    dens_slots = jnp.zeros((grp_count, BLK), jnp.float32)
    dens_slots = lax.dynamic_update_slice(dens_slots, dens_part[None, :], (grp_id, 0))
    sums = lax.psum(jnp.concatenate([field_part, dens_slots], axis=0), ("grp", "aux", "orb"))

    x_blocks = x_part.reshape(parts, orb_count, own_span, nocc)
    targets = [lax.rem(orb_id + k, orb_count) for k in range(orb_count)]
    moves = [[(s, (s + k) % orb_count) for s in range(orb_count)] for k in range(orb_count)]
    arrived = []
    for k in range(1, orb_count):
        block = lax.dynamic_index_in_dim(x_blocks, targets[k], 1, keepdims=False)
        arrived.append(lax.ppermute(block, "orb", moves[k]))
    sums, *arrived = lax.optimization_barrier((sums, *arrived))
    field_vec = sums[:block_total].reshape(-1)
    densities = lax.dynamic_slice(sums, (block_total + grp_id, 0), (1, parts))[0]
    x_sum = lax.dynamic_index_in_dim(x_blocks, orb_id, 1, keepdims=False).astype(jnp.float32)
    for block in arrived:
        x_sum += block.astype(jnp.float32)
    x_own = x_sum.astype(jnp.bfloat16)
    x_mate = swap(x_own)
    x_all = lax.all_gather(x_own, ("aux", "orb"), axis=1, tiled=True)

    mine = [None] * orb_count
    for k in list(range(1, orb_count)) + [0]:
        at = jnp.stack([grp_id, targets[k]]).astype(jnp.int32)
        away, kept = coulomb_call(at, densities, fitted_tensor, mask_rows, half)
        both = (kept.astype(jnp.float32) + swap(away).astype(jnp.float32)).astype(jnp.bfloat16)
        mine[k] = lax.ppermute(both, "orb", moves[k]) if k else both
    x_all, *mine = lax.optimization_barrier((x_all, *mine))
    theirs = [swap(block) for block in mine]
    x_mate_all = swap(x_all)

    own_first = row_start + orb_id * own_span
    field_col = lax.dynamic_slice_in_dim(field_vec, own_first, own_span, 0)[:, None]
    place = jnp.stack([grp_id, own_first, orb_id]).astype(jnp.int32)
    fock = fock_call(place, x_own, x_mate, x_all, x_mate_all, field_col, mine, theirs)
    return (fock, mm_potential)


MESH = pl.DeviceIdType.MESH
CHUNKS = 8
AHEAD = 2
GRID_VMEM = 58 * 1024 * 1024


def grid_kernel(
    t_hbm, mask_ref, c_ref, small_ref, out_ref, sums_ref,
    t_ref, cw_ref, xp_ref, ra_ref, rb_ref, xa_ref, xm_ref, xo_ref, mr_ref, cr_ref, eb_ref,
    s_ref, sr_ref, dens_ref,
    t_sem, c_send, c_recv, ra_send, ra_recv, rb_send, rb_recv, xe_send, xe_recv,
    pl_send, pl_recv, xm_send, xm_recv, xo_send, xo_recv, s_send, s_recv,
    mr_send, mr_recv, cr_send, cr_recv, om_send, om_recv, ol_sem,
):
    parts, rows, cols = t_ref.shape
    nocc = c_ref.shape[1]
    chunk = rows // CHUNKS
    own = rows // 4
    half = cols // 2
    quarter = cols // 4
    per = CHUNKS // 2
    g, a, z = lax.axis_index("grp"), lax.axis_index("aux"), lax.axis_index("orb")
    mate = (1 - g, a, z)
    is_mid = (z == 1) | (z == 2)
    is_end = (z == 0) | (z == 3)
    inner = jnp.where(z == 0, 1, 2)
    outer = jnp.where(z == 1, 0, 3)
    rel = lax.bitwise_xor(a, z)

    def plane(k):
        return (g, lax.bitwise_xor(a, k), z)

    def remote(src, dst, send, recv, device):
        return pltpu.make_async_remote_copy(
            src_ref=src, dst_ref=dst, send_sem=send, recv_sem=recv,
            device_id=device, device_id_type=MESH,
        )

    def t_copy(c):
        span = pl.ds(c * chunk, chunk)
        return pltpu.make_async_copy(t_hbm.at[:, span], t_ref.at[:, span], t_sem.at[c])

    for c in range(CHUNKS):
        t_copy(c).start()

    barrier = pltpu.get_barrier_semaphore()
    for peer in (
        mate, plane(1), plane(2), plane(3),
        (g, a, lax.rem(z + 1, 4)), (g, a, lax.rem(z + 2, 4)), (g, a, lax.rem(z + 3, 4)),
    ):
        pl.semaphore_signal(barrier, inc=1, device_id=peer, device_id_type=MESH)
    pl.semaphore_wait(barrier, 7)

    def quarter_copy(src_ref, q, slot, device):
        span = pl.ds(pl.multiple_of(q * quarter, quarter), quarter)
        return remote(src_ref.at[span], cw_ref.at[span], c_send.at[slot], c_recv.at[q], device)

    first, second = 2 * g, 2 * g + 1

    @pl.when(rel == 0)
    def _():
        quarter_copy(c_ref, first, 0, plane(1)).start()
        quarter_copy(c_ref, second, 1, plane(2)).start()
        quarter_copy(c_ref, second, 2, plane(1)).start()
        quarter_copy(c_ref, first, 3, plane(2)).start()
        cw_ref[...] = c_ref[...]

    @pl.when(rel != 0)
    def _():
        for rank in range(2):
            q = jnp.where(rel == 2, 2 * g + 1 - rank, 2 * g + rank)
            quarter_copy(cw_ref, q, 0, mate).wait_recv()
            if rank == 0:

                @pl.when(rel == 1)
                def _():
                    quarter_copy(cw_ref, q, 2, plane(2)).start()

                @pl.when(rel == 2)
                def _():
                    quarter_copy(cw_ref, q, 2, plane(1)).start()

            quarter_copy(cw_ref, q, rank, mate).start()
        for rank in range(2):
            quarter_copy(cw_ref, 2 * (1 - g) + rank, 0, mate).wait_recv()

    def x_span(c):
        return pl.ds(pl.multiple_of(c * chunk, chunk), chunk)

    def ra_copy(c):
        return remote(
            xp_ref.at[:, x_span(c)], ra_ref.at[:, x_span(c)], ra_send.at[c], ra_recv.at[c], (g, a, inner)
        )

    dens_ref[...] = jnp.zeros_like(dens_ref)

    def products_step(c, carry):
        t_copy(c).wait()
        span = x_span(c)
        c_rows = c_ref[span, :].astype(jnp.float32)
        blocks = chunk // BLK
        for p in range(parts):
            masked = jnp.concatenate(
                [
                    t_ref[p, pl.ds(pl.multiple_of(c * chunk + j * BLK, BLK), BLK), :]
                    * mask_ref[c * blocks + j]
                    for j in range(blocks)
                ],
                axis=0,
            )
            prod = jnp.dot(masked, cw_ref[...], preferred_element_type=jnp.float32)
            xp_ref[p, span, :] = prod.astype(jnp.bfloat16)
            dens_ref[p] += jnp.sum((prod * c_rows).reshape(chunk // 8, 8, nocc), axis=0)

        @pl.when(is_end & (c < AHEAD))
        def _():
            ra_copy(c).start()

        return carry

    lax.fori_loop(0, CHUNKS, products_step, 0)

    small = s_ref.shape[0]
    s_ref[...] = small_ref[...]
    tile_rows = lax.broadcasted_iota(jnp.int32, (8, 128), 0)
    tile = jnp.zeros((8, 128), jnp.float32)
    for p in range(parts):
        lanes = jnp.sum(dens_ref[p], axis=0, keepdims=True)
        folded = lanes[:, :128]
        for j in range(1, nocc // 128):
            folded = folded + lanes[:, j * 128 : (j + 1) * 128]
        tile = tile + jnp.where(tile_rows == parts * g + p, folded, 0.0)
    s_ref[small - 8 :, :] = tile

    def s_copy(i):
        device = (mate, plane(1), plane(2))[i] if i < 3 else (g, a, lax.rem(z + i - 2, 4))
        return remote(s_ref, sr_ref.at[i], s_send.at[i], s_recv.at[i], device)

    def s_start(r):
        for i in ((0,), (1,), (2,), (3, 4, 5))[r]:
            s_copy(i).start()

    def s_finish(r):
        batch = ((0,), (1,), (2,), (3, 4, 5))[r]
        for i in batch:
            s_copy(i).wait()
        for i in batch:
            s_ref[...] += sr_ref[i]

    def rb_copy(c):
        return remote(
            xp_ref.at[:, x_span(c)], rb_ref.at[:, x_span(c)], rb_send.at[c], rb_recv.at[c], (g, a, 3 - z)
        )

    def xa_at(block, c):
        return xa_ref.at[:, pl.ds(pl.multiple_of(block * rows + c * chunk, chunk), chunk)]

    def xe_copy(c):
        return remote(xa_at(a, c), xa_at(a, c), xe_send.at[c], xe_recv.at[c], (g, a, outer))

    def pl_copy(c, k):
        return remote(
            xa_at(a, c), xa_at(a, c), pl_send.at[k - 1, c], pl_recv.at[k - 1, c], plane(k)
        )

    def pl_wait(c, k):
        block = lax.bitwise_xor(a, k)
        remote(
            xa_at(block, c), xa_at(block, c), pl_send.at[k - 1, c], pl_recv.at[k - 1, c], plane(k)
        ).wait_recv()

    def xm_copy(block, c):
        i = block * per + lax.rem(c, per)
        dst = xm_ref.at[:, pl.ds(pl.multiple_of(i * chunk, chunk), chunk)]
        return remote(xa_at(block, c), dst, xm_send.at[i], xm_recv.at[i], mate)

    def xo_copy(c):
        i = lax.rem(c, 2)
        dst = xo_ref.at[:, pl.ds(pl.multiple_of(i * chunk, chunk), chunk)]
        return remote(xa_at(a, c), dst, xo_send.at[i], xo_recv.at[i], mate)

    def for_mate(c):
        return c // per == 1 - g

    def publish(c):
        for k in (1, 2, 3):
            pl_copy(c, k).start()

        @pl.when(for_mate(c))
        def _():
            xm_copy(a, c).start()

        @pl.when(z == c // 2)
        def _():
            xo_copy(c).start()

    def stage_one(c):
        ra_copy(c).wait_recv()
        for p in range(parts):
            both = xp_ref[p, x_span(c), :].astype(jnp.float32) + ra_ref[p, x_span(c), :].astype(jnp.float32)
            xp_ref[p, x_span(c), :] = both.astype(jnp.bfloat16)
        rb_copy(c).start()

    def stage_two(c):
        rb_copy(c).wait_recv()
        for p in range(parts):
            both = xp_ref[p, x_span(c), :].astype(jnp.float32) + rb_ref[p, x_span(c), :].astype(jnp.float32)
            xa_ref[p, pl.ds(pl.multiple_of(a * rows + c * chunk, chunk), chunk), :] = both.astype(jnp.bfloat16)
        xe_copy(c).start()
        publish(c)

    def late_slot(t):
        if t == CHUNKS:

            @pl.when(is_mid)
            def _():
                stage_two(t - 1)

        @pl.when(is_end)
        def _():
            xe_copy(t - 3).wait_recv()
            publish(t - 3)

    def slot(t):
        if t >= CHUNKS:
            late_slot(t)
            return

        @pl.when(is_mid)
        def _():
            stage_one(t)
            if t >= 1:
                stage_two(t - 1)

        @pl.when(is_end)
        def _():
            ra_copy(t).wait_send()
            if t < CHUNKS - AHEAD:
                ra_copy(t + AHEAD).start()
            if t >= 3:
                xe_copy(t - 3).wait_recv()
                publish(t - 3)

    own_cols = pl.ds(pl.multiple_of(g * half, half), half)
    mate_cols = pl.ds(pl.multiple_of((1 - g) * half, half), half)

    def mr_copy(dest):
        span = pl.ds(pl.multiple_of(dest * own, own), own)
        return remote(
            t_ref.at[0, span, mate_cols], mr_ref.at[dest], mr_send.at[dest], mr_recv.at[dest], mate
        )

    def cr_copy(k):
        dest = lax.rem(z + k, 4)
        span = pl.ds(pl.multiple_of(dest * own, own), own)
        return remote(
            t_ref.at[1, span, own_cols], cr_ref.at[z], cr_send.at[k - 1], cr_recv.at[k - 1], (g, a, dest)
        )

    def cr_wait(k):
        src = lax.rem(z + 4 - k, 4)
        remote(
            t_ref.at[1, pl.ds(0, own), own_cols], cr_ref.at[src], cr_send.at[k - 1], cr_recv.at[k - 1], mate
        ).wait_recv()
        return src

    def coulomb_part(k, d):
        dest = lax.rem(z + k, 4)
        step = 32

        def body(i, carry):
            row = pl.multiple_of(dest * own + i * step, step)
            span = pl.ds(row, step)
            total = t_ref[0, span, :].astype(jnp.float32) * d[0]
            for p in range(1, parts):
                total += t_ref[p, span, :].astype(jnp.float32) * d[p]
            total = total * mask_ref[row // BLK].astype(jnp.float32)
            t_ref[0, span, :] = total.astype(jnp.bfloat16)
            return carry

        lax.fori_loop(0, own // step, body, 0)
        mr_copy(dest).start()

    def coulomb_sum(k):
        dest = lax.rem(z + k, 4)
        mr_copy(dest).wait_recv()
        step = 64

        def body(i, carry):
            span = pl.ds(pl.multiple_of(dest * own + i * step, step), step)
            piece = pl.ds(pl.multiple_of(i * step, step), step)
            both = t_ref[0, span, own_cols].astype(jnp.float32) + mr_ref[dest, piece, :].astype(jnp.float32)
            if k:
                t_ref[1, span, own_cols] = both.astype(jnp.bfloat16)
            else:
                cr_ref[dest, piece, :] = both.astype(jnp.bfloat16)
            return carry

        lax.fori_loop(0, own // step, body, 0)

    s_start(0)
    s_finish(0)
    s_start(1)
    slot(0)
    s_finish(1)
    s_start(2)
    s_finish(2)
    s_start(3)
    slot(1)
    slot(2)
    s_finish(3)
    sums_ref[...] = s_ref[...]
    dens_tile = s_ref[small - 8 :, :]
    d = []
    for p in range(parts):
        row = jnp.where(tile_rows == parts * g + p, dens_tile, 0.0)
        value = 2.0 * jnp.sum(jnp.sum(row, axis=1, keepdims=True), axis=0, keepdims=True)
        d.append(value.astype(jnp.bfloat16).astype(jnp.float32))
    order = (2, 1, 3, 0)
    slot(3)
    coulomb_part(order[0], d)
    for i in range(1, 4):
        coulomb_part(order[i], d)
        coulomb_sum(order[i - 1])
        slot(3 + i)
    coulomb_sum(order[3])
    slot(7)

    @pl.when(is_end)
    def _():
        for k in order[:3]:
            cr_copy(k).start()

    slot(8)

    @pl.when(is_mid)
    def _():
        for k in order[:3]:
            cr_copy(k).start()

    slot(9)
    slot(10)

    def arrive(c, carry):
        for k in (1, 2, 3):
            pl_wait(c, k)

            @pl.when(for_mate(c))
            def _():
                xm_copy(lax.bitwise_xor(a, k), c).start()

        return carry

    lax.fori_loop(0, CHUNKS, arrive, 0)

    for i in range(2):
        xo_copy(i).wait_recv()
    dims = (((1,), (1,)), ((), ()))
    own_rows = pl.ds(pl.multiple_of(a * rows + z * own, own), own)

    def exchange(block, carry):
        def body(j, inside):
            i = block * per + j
            xm_copy(block, j).wait_recv()
            total = jnp.zeros((own, chunk), jnp.float32)
            near = pl.ds(pl.multiple_of(block * rows + g * half + j * chunk, chunk), chunk)
            far = pl.ds(pl.multiple_of(i * chunk, chunk), chunk)
            for p in range(parts):
                total += lax.dot_general(
                    xa_ref[p, own_rows, :], xa_ref[p, near, :], dims, preferred_element_type=jnp.float32
                )
                total += lax.dot_general(
                    xo_ref[p], xm_ref[p, far, :], dims, preferred_element_type=jnp.float32
                )
            eb_ref[block, :, pl.ds(pl.multiple_of(j * chunk, chunk), chunk)] = (-0.5 * total).astype(jnp.bfloat16)
            return inside

        return lax.fori_loop(0, per, body, carry)

    lax.fori_loop(0, 4, exchange, 0)

    def out_cols(block, core):
        return pl.ds(pl.multiple_of(block * cols + core * half, half), half)

    def om_copy(block):
        return remote(
            eb_ref.at[block], out_ref.at[:, out_cols(block, g)], om_send.at[block], om_recv.at[block], mate
        )

    def ol_copy(block):
        return pltpu.make_async_copy(eb_ref.at[block], out_ref.at[:, out_cols(block, g)], ol_sem.at[block])

    for k in (0, 1, 3, 2):
        src = cr_wait(k) if k else z
        step = 64

        def body(i, carry):
            piece = pl.ds(pl.multiple_of(i * step, step), step)
            both = eb_ref[src, piece, :].astype(jnp.float32) + cr_ref[src, piece, :].astype(jnp.float32)
            eb_ref[src, piece, :] = both.astype(jnp.bfloat16)
            return carry

        lax.fori_loop(0, own // step, body, 0)
        om_copy(src).start()
        ol_copy(src).start()

    for block in range(4):
        remote(
            eb_ref.at[block], out_ref.at[:, out_cols(block, 1 - g)], om_send.at[block], om_recv.at[block], mate
        ).wait()
        ol_copy(block).wait()
        mr_copy(block).wait_send()
    for k in (1, 2, 3):
        cr_copy(k).wait_send()

    @pl.when(rel == 0)
    def _():
        for i in range(4):
            quarter_copy(c_ref, first, i, mate).wait_send()

    @pl.when(rel != 0)
    def _():
        for i in range(2):
            quarter_copy(cw_ref, first, i, mate).wait_send()

    @pl.when((rel == 1) | (rel == 2))
    def _():
        quarter_copy(cw_ref, first, 2, mate).wait_send()

    def drain(c, carry):
        @pl.when(is_mid)
        def _():
            rb_copy(c).wait_send()
            xe_copy(c).wait_send()

        for k in (1, 2, 3):
            pl_copy(c, k).wait_send()

        @pl.when(for_mate(c))
        def _():
            for block in range(4):
                xm_copy(block, c).wait_send()

        return carry

    lax.fori_loop(0, CHUNKS, drain, 0)
    for i in range(2):
        xo_copy(i).wait_send()


def grid_call(fitted, mask_rows, own_c, small):
    parts, rows, cols = fitted.shape
    nocc = own_c.shape[1]
    own, half = rows // 4, cols // 2
    bf16, f32 = jnp.bfloat16, jnp.float32
    vmem = pl.BlockSpec(memory_space=pltpu.VMEM)
    hbm = pl.BlockSpec(memory_space=pl.ANY)
    dma = pltpu.SemaphoreType.DMA
    return pl.pallas_call(
        grid_kernel,
        in_specs=[hbm, vmem, vmem, vmem],
        out_specs=[hbm, vmem],
        out_shape=[
            jax.ShapeDtypeStruct((own, 4 * cols), bf16),
            jax.ShapeDtypeStruct(small.shape, f32),
        ],
        scratch_shapes=[
            pltpu.VMEM((parts, rows, cols), bf16),
            pltpu.VMEM((cols, nocc), bf16),
            pltpu.VMEM((parts, rows, nocc), bf16),
            pltpu.VMEM((parts, rows, nocc), bf16),
            pltpu.VMEM((parts, rows, nocc), bf16),
            pltpu.VMEM((parts, 4 * rows, nocc), bf16),
            pltpu.VMEM((parts, 2 * rows, nocc), bf16),
            pltpu.VMEM((parts, own, nocc), bf16),
            pltpu.VMEM((4, own, half), bf16),
            pltpu.VMEM((4, own, half), bf16),
            pltpu.VMEM((4, own, half), bf16),
            pltpu.VMEM(small.shape, f32),
            pltpu.VMEM((6,) + small.shape, f32),
            pltpu.VMEM((parts, 8, nocc), f32),
            dma((CHUNKS,)),
            dma((4,)), dma((4,)),
            dma((CHUNKS,)), dma((CHUNKS,)),
            dma((CHUNKS,)), dma((CHUNKS,)),
            dma((CHUNKS,)), dma((CHUNKS,)),
            dma((3, CHUNKS)), dma((3, CHUNKS)),
            dma((2 * CHUNKS,)), dma((2 * CHUNKS,)),
            dma((2,)), dma((2,)),
            dma((6,)), dma((6,)),
            dma((4,)), dma((4,)),
            dma((3,)), dma((3,)),
            dma((4,)), dma((4,)),
            dma((4,)),
        ],
        compiler_params=pltpu.CompilerParams(
            collective_id=0, has_side_effects=True, vmem_limit_bytes=GRID_VMEM
        ),
        cost_estimate=pl.CostEstimate(
            flops=2 * parts * rows * cols * nocc + 8 * parts * own * 2 * cols * nocc,
            bytes_accessed=2 * parts * rows * cols + 8 * own * cols,
            transcendentals=0,
        ),
        name="grid",
    )(fitted, mask_rows, own_c, small)


def per_device_grid(
    fitted_tensor, block_mask, orbitals, nuclear, centres, mm_positions, mm_charges, neighbours
):
    parts, row_span, col_span = fitted_tensor.shape
    grp_id = lax.axis_index("grp")
    aux_id = lax.axis_index("aux")
    orb_id = lax.axis_index("orb")
    own_span = row_span // 4
    block_total = block_mask.shape[1]
    row_start = aux_id * row_span
    bits = lax.dynamic_slice(
        block_mask[0],
        (row_start // BLK, orb_id * (col_span // BLK)),
        (row_span // BLK, col_span // BLK),
    ).astype(jnp.bfloat16)
    mask_rows = jnp.repeat(bits, BLK, axis=1)[:, None, :]

    own_float = orbitals.astype(jnp.float32)
    population = 2.0 * jnp.sum(own_float * own_float, axis=1)
    population = jnp.where((grp_id == 0) & (orb_id == 0), population, 0.0)
    population = lax.dynamic_update_slice(
        jnp.zeros((block_total, BLK), jnp.float32),
        population.reshape(row_span // BLK, BLK),
        (aux_id * (row_span // BLK), 0),
    )
    centre_blocks = centres.reshape(3, block_total, BLK)
    picker = (neighbours[0][:, None] == jnp.arange(block_total, dtype=jnp.int32)[None, :]).astype(
        jnp.float32
    )
    kernel = near_kernel(picker, centre_blocks, mm_positions)
    contrib = jnp.dot(kernel, mm_charges, precision=lax.Precision.HIGHEST).reshape(
        picker.shape[0], BLK
    )
    field_part = jnp.dot(picker.T, contrib, precision=lax.Precision.HIGHEST)
    small = jnp.concatenate([field_part, population, jnp.zeros((8, BLK), jnp.float32)], axis=0)

    fock16, sums = grid_call(fitted_tensor, mask_rows, orbitals, small)

    own_first = row_start + orb_id * own_span
    field_vec = sums[:block_total].reshape(-1)
    field_own = lax.dynamic_slice_in_dim(field_vec, own_first, own_span, 0)
    row_ids = own_first + lax.broadcasted_iota(jnp.int32, fock16.shape, 0)
    col_ids = lax.broadcasted_iota(jnp.int32, fock16.shape, 1)
    fock = fock16.astype(jnp.float32) + jnp.where(row_ids == col_ids, field_own[:, None], 0.0)

    charge_blocks = nuclear.reshape(block_total, BLK) - sums[block_total : 2 * block_total]
    near_q = jnp.dot(picker, charge_blocks, precision=lax.Precision.HIGHEST).reshape(-1)
    mm_potential = jnp.dot(near_q, kernel, precision=lax.Precision.HIGHEST)
    return (fock, mm_potential)


def grid_fits(mesh, fitted_tensor, orbitals):
    shape = mesh.shape
    parts = fitted_tensor.shape[0] // shape["grp"]
    rows = fitted_tensor.shape[1] // shape["aux"]
    cols = fitted_tensor.shape[2] // shape["orb"]
    return (
        shape["grp"] == 2
        and shape["aux"] == 4
        and shape["orb"] == 4
        and parts == 2
        and rows == cols
        and rows % (CHUNKS * BLK) == 0
        and orbitals.shape[1] % BLK == 0
        and 7 * rows * cols + 41 * rows * orbitals.shape[1] <= 52 * 2**20
    )


def solution(mesh):
    in_specs = (
        P("grp", "aux", "orb"),
        P("grp", None, None),
        P("aux", None),
        P(),
        P(),
        P(None, ("grp", "aux", "orb")),
        P(("grp", "aux", "orb")),
        P(("grp", "aux", "orb"), None),
    )
    out_specs = (P(("aux", "orb"), None), P(("grp", "aux", "orb")))
    def build(body):
        return jax.shard_map(
            body, mesh=mesh, in_specs=in_specs, out_specs=out_specs, check_vma=False
        )

    def run(fitted_tensor, block_mask, orbitals, *rest):
        body = per_device_grid if grid_fits(mesh, fitted_tensor, orbitals) else per_device
        return build(body)(fitted_tensor, block_mask, orbitals, *rest)

    return run
```

```python
import functools

import jax
import jax.numpy as jnp
from jax import lax
from jax.experimental import pallas as pl
from jax.experimental.pallas import tpu as pltpu
from jax.sharding import PartitionSpec as P

BLK = 128
VMEM_LIMIT = 48 * 1024 * 1024

softening = 1.0


def near_kernel(picker, centre_blocks, atom_xyz):
    near_xyz = jnp.einsum("kb,cbj->ckj", picker, centre_blocks, precision=lax.Precision.HIGHEST)
    near_xyz = near_xyz.reshape(3, picker.shape[0] * centre_blocks.shape[2])
    offsets = near_xyz[:, :, None] - atom_xyz[:, None, :]
    return lax.rsqrt(jnp.sum(offsets * offsets, axis=0) + softening)


def products_kernel(t_ref, mask_ref, win_ref, c_ref, x_ref, dens_ref):
    parts, rows, cols = t_ref.shape
    row_mask = mask_ref[0]

    @pl.when(pl.program_id(0) == 0)
    def _():
        dens_ref[...] = jnp.zeros_like(dens_ref)

    own = c_ref[...].astype(jnp.float32)
    for p in range(parts):
        prod = jnp.dot(t_ref[p] * row_mask, win_ref[...], preferred_element_type=jnp.float32)
        x_ref[p] = prod.astype(x_ref.dtype)
        dens_ref[p] += jnp.sum((prod * own).reshape(rows // 8, 8, prod.shape[1]), axis=0)


def products_call(fitted, mask_rows, window_c, own_c):
    parts, rows, cols = fitted.shape
    nocc = window_c.shape[1]
    return pl.pallas_call(
        products_kernel,
        grid=(rows // BLK,),
        in_specs=[
            pl.BlockSpec((parts, BLK, cols), lambda i: (0, i, 0)),
            pl.BlockSpec((1, 1, cols), lambda i: (i, 0, 0)),
            pl.BlockSpec((cols, nocc), lambda i: (0, 0)),
            pl.BlockSpec((BLK, nocc), lambda i: (i, 0)),
        ],
        out_specs=[
            pl.BlockSpec((parts, BLK, nocc), lambda i: (0, i, 0)),
            pl.BlockSpec((parts, 8, nocc), lambda i: (0, 0, 0)),
        ],
        out_shape=[
            jax.ShapeDtypeStruct((parts, rows, nocc), jnp.bfloat16),
            jax.ShapeDtypeStruct((parts, 8, nocc), jnp.float32),
        ],
        compiler_params=pltpu.CompilerParams(vmem_limit_bytes=VMEM_LIMIT),
        cost_estimate=pl.CostEstimate(
            flops=2 * parts * rows * cols * nocc,
            bytes_accessed=2 * parts * rows * (cols + nocc),
            transcendentals=0,
        ),
        name="products",
    )(fitted, mask_rows, window_c, own_c)


def coulomb_kernel(place_ref, dens_ref, ta_ref, ma_ref, tk_ref, mk_ref, away_ref, kept_ref):
    for t_ref, mask_ref, out_ref in ((ta_ref, ma_ref, away_ref), (tk_ref, mk_ref, kept_ref)):
        total = t_ref[0].astype(jnp.float32) * dens_ref[0]
        for p in range(1, t_ref.shape[0]):
            total += t_ref[p].astype(jnp.float32) * dens_ref[p]
        out_ref[...] = (total * mask_ref[0].astype(jnp.float32)).astype(out_ref.dtype)


def coulomb_call(place, densities, fitted, mask_rows, half):
    parts, rows, cols = fitted.shape
    tile = min(BLK, half)
    steps = half // tile

    def away_tile(i, place_ref):
        return (place_ref[1] * 2 + 1 - place_ref[0]) * steps + i

    def kept_tile(i, place_ref):
        return (place_ref[1] * 2 + place_ref[0]) * steps + i

    def tensor_spec(which):
        return pl.BlockSpec((parts, tile, cols), lambda i, place_ref, d: (0, which(i, place_ref), 0))

    def mask_spec(which):
        return pl.BlockSpec(
            (1, 1, cols), lambda i, place_ref, d: (which(i, place_ref) * tile // BLK, 0, 0)
        )

    return pl.pallas_call(
        coulomb_kernel,
        grid_spec=pltpu.PrefetchScalarGridSpec(
            num_scalar_prefetch=2,
            grid=(steps,),
            in_specs=[
                tensor_spec(away_tile),
                mask_spec(away_tile),
                tensor_spec(kept_tile),
                mask_spec(kept_tile),
            ],
            out_specs=[pl.BlockSpec((tile, cols), lambda i, place_ref, d: (i, 0))] * 2,
        ),
        out_shape=[jax.ShapeDtypeStruct((half, cols), jnp.bfloat16)] * 2,
        compiler_params=pltpu.CompilerParams(vmem_limit_bytes=VMEM_LIMIT),
        cost_estimate=pl.CostEstimate(
            flops=4 * parts * half * cols,
            bytes_accessed=4 * half * cols * (parts + 1),
            transcendentals=0,
        ),
        name="coulomb",
    )(place, densities, fitted, mask_rows, fitted, mask_rows)


def fock_kernel(shifts, place_ref, own_ref, mate_ref, all_ref, mate_all_ref, field_ref, *refs):
    mine, theirs, out_ref = refs[:shifts], refs[shifts : 2 * shifts], refs[2 * shifts]
    parts = own_ref.shape[0]
    rows, cols = out_ref.shape
    half = rows // 2
    per_src = mine[0].shape[1] // cols
    dims = (((1,), (1,)), ((), ()))
    grp_id, row0, orb_id = place_ref[0], place_ref[1], place_ref[2]

    def slab(a, b):
        total = lax.dot_general(a[0], b[0], dims, preferred_element_type=jnp.float32)
        for p in range(1, parts):
            total += lax.dot_general(a[p], b[p], dims, preferred_element_type=jnp.float32)
        return total

    out_ref[...] = -0.5 * (slab(own_ref, all_ref) + slab(mate_ref, mate_all_ref))

    step = pl.program_id(0)
    shift = lax.rem(orb_id - step // per_src + shifts, shifts)
    col_in = pl.multiple_of(lax.rem(step, per_src) * cols, cols)
    own_row = pl.multiple_of(grp_id * half, half)
    mate_row = pl.multiple_of((1 - grp_id) * half, half)
    for k in range(shifts):

        @pl.when(shift == k)
        def _():
            out_ref[pl.ds(own_row, half), :] += mine[k][:, pl.ds(col_in, cols)].astype(jnp.float32)
            out_ref[pl.ds(mate_row, half), :] += theirs[k][:, pl.ds(col_in, cols)].astype(jnp.float32)

    col0 = step * cols

    @pl.when((row0 < col0 + cols) & (row0 + rows > col0))
    def _():
        row_ids = row0 + lax.broadcasted_iota(jnp.int32, (rows, cols), 0)
        col_ids = col0 + lax.broadcasted_iota(jnp.int32, (rows, cols), 1)
        out_ref[...] += jnp.where(row_ids == col_ids, field_ref[...], jnp.float32(0.0))


def fock_call(place, x_own, x_mate, x_all, x_mate_all, field_col, mine, theirs):
    parts, rows, nocc = x_own.shape
    total = x_all.shape[1]
    half, per_src = mine[0].shape
    cols = min(1024, per_src)
    own_spec = pl.BlockSpec((parts, rows, nocc), lambda j: (0, 0, 0))
    all_spec = pl.BlockSpec((parts, cols, nocc), lambda j: (0, j, 0))
    return pl.pallas_call(
        functools.partial(fock_kernel, len(mine)),
        grid=(total // cols,),
        in_specs=[
            pl.BlockSpec(memory_space=pltpu.SMEM),
            own_spec,
            own_spec,
            all_spec,
            all_spec,
            pl.BlockSpec((rows, 1), lambda j: (0, 0)),
        ]
        + [pl.BlockSpec((half, per_src), lambda j: (0, 0))] * (2 * len(mine)),
        out_specs=pl.BlockSpec((rows, cols), lambda j: (0, j)),
        out_shape=jax.ShapeDtypeStruct((rows, total), jnp.float32),
        compiler_params=pltpu.CompilerParams(vmem_limit_bytes=VMEM_LIMIT),
        cost_estimate=pl.CostEstimate(
            flops=4 * parts * rows * total * nocc,
            bytes_accessed=4 * parts * total * nocc + 4 * rows * total + 2 * rows * total,
            transcendentals=0,
        ),
        name="fock",
    )(place, x_own, x_mate, x_all, x_mate_all, field_col, *mine, *theirs)


def swap(value):
    return lax.ppermute(value, "grp", [(0, 1), (1, 0)])


def per_device(
    fitted_tensor, block_mask, orbitals, nuclear, centres, mm_positions, mm_charges, neighbours
):
    parts, row_span, col_span = fitted_tensor.shape
    nocc = orbitals.shape[1]
    orb_count = lax.axis_size("orb")
    aux_count = lax.axis_size("aux")
    grp_count = lax.axis_size("grp")
    grp_id = lax.axis_index("grp")
    aux_id = lax.axis_index("aux")
    orb_id = lax.axis_index("orb")
    own_span = row_span // orb_count
    half = own_span // 2
    block_total = block_mask.shape[1]
    row_start = aux_id * row_span
    col_start = orb_id * col_span

    if aux_count == orb_count:
        perm = [
            (a * orb_count + o, o * orb_count + a)
            for a in range(aux_count)
            for o in range(orb_count)
        ]
        c_half = lax.dynamic_slice_in_dim(orbitals, grp_id * (row_span // 2), row_span // 2, 0)
        c_half = lax.ppermute(c_half, ("aux", "orb"), perm)
        c_mate = swap(c_half)
        window_c = jnp.where(
            grp_id == 0, jnp.stack([c_half, c_mate]), jnp.stack([c_mate, c_half])
        ).reshape(col_span, nocc)
    else:
        whole_c = lax.all_gather(orbitals, "aux", axis=0, tiled=True)
        window_c = lax.dynamic_slice_in_dim(whole_c, col_start, col_span, 0)

    bits = lax.dynamic_slice(
        block_mask[0],
        (row_start // BLK, col_start // BLK),
        (row_span // BLK, col_span // BLK),
    ).astype(jnp.bfloat16)
    mask_rows = jnp.repeat(bits, BLK, axis=1)[:, None, :]

    own_float = orbitals.astype(jnp.float32)
    own_population = 2.0 * jnp.sum(own_float * own_float, axis=1)
    population = lax.all_gather(own_population, "aux", axis=0, tiled=True)
    centre_blocks = centres.reshape(3, block_total, BLK)
    picker = (neighbours[0][:, None] == jnp.arange(block_total, dtype=jnp.int32)[None, :]).astype(
        jnp.float32
    )
    kernel = near_kernel(picker, centre_blocks, mm_positions)
    contrib = jnp.dot(kernel, mm_charges, precision=lax.Precision.HIGHEST).reshape(
        picker.shape[0], BLK
    )
    field_part = jnp.dot(picker.T, contrib, precision=lax.Precision.HIGHEST)

    window_c, population = lax.optimization_barrier((window_c, population))
    qm_charge = nuclear - population
    charge_blocks = qm_charge.reshape(block_total, BLK)
    near_q = jnp.dot(picker, charge_blocks, precision=lax.Precision.HIGHEST).reshape(-1)
    mm_potential = jnp.dot(near_q, kernel, precision=lax.Precision.HIGHEST)

    x_part, dens_lanes = products_call(fitted_tensor, mask_rows, window_c, orbitals)
    dens_part = 2.0 * jnp.sum(dens_lanes, axis=(1, 2))
    dens_slots = jnp.zeros((grp_count, BLK), jnp.float32)
    dens_slots = lax.dynamic_update_slice(dens_slots, dens_part[None, :], (grp_id, 0))
    sums = lax.psum(jnp.concatenate([field_part, dens_slots], axis=0), ("grp", "aux", "orb"))

    x_blocks = x_part.reshape(parts, orb_count, own_span, nocc)
    targets = [lax.rem(orb_id + k, orb_count) for k in range(orb_count)]
    moves = [[(s, (s + k) % orb_count) for s in range(orb_count)] for k in range(orb_count)]
    arrived = []
    for k in range(1, orb_count):
        block = lax.dynamic_index_in_dim(x_blocks, targets[k], 1, keepdims=False)
        arrived.append(lax.ppermute(block, "orb", moves[k]))
    sums, *arrived = lax.optimization_barrier((sums, *arrived))
    field_vec = sums[:block_total].reshape(-1)
    densities = lax.dynamic_slice(sums, (block_total + grp_id, 0), (1, parts))[0]
    x_sum = lax.dynamic_index_in_dim(x_blocks, orb_id, 1, keepdims=False).astype(jnp.float32)
    for block in arrived:
        x_sum += block.astype(jnp.float32)
    x_own = x_sum.astype(jnp.bfloat16)
    x_mate = swap(x_own)
    x_all = lax.all_gather(x_own, ("aux", "orb"), axis=1, tiled=True)

    mine = [None] * orb_count
    for k in list(range(1, orb_count)) + [0]:
        at = jnp.stack([grp_id, targets[k]]).astype(jnp.int32)
        away, kept = coulomb_call(at, densities, fitted_tensor, mask_rows, half)
        both = (kept.astype(jnp.float32) + swap(away).astype(jnp.float32)).astype(jnp.bfloat16)
        mine[k] = lax.ppermute(both, "orb", moves[k]) if k else both
    x_all, *mine = lax.optimization_barrier((x_all, *mine))
    theirs = [swap(block) for block in mine]
    x_mate_all = swap(x_all)

    own_first = row_start + orb_id * own_span
    field_col = lax.dynamic_slice_in_dim(field_vec, own_first, own_span, 0)[:, None]
    place = jnp.stack([grp_id, own_first, orb_id]).astype(jnp.int32)
    fock = fock_call(place, x_own, x_mate, x_all, x_mate_all, field_col, mine, theirs)
    return (fock, mm_potential)


MESH = pl.DeviceIdType.MESH
CHUNKS = 8
AHEAD = 2
GRID_VMEM = 58 * 1024 * 1024


def grid_kernel(
    t_hbm, bits_ref, c_ref, nuclear_ref, centres_ref, place_ref, charge_ref, near_ref,
    out_ref, potential_ref,
    t_ref, mask_ref, kern_ref, cw_ref, xp_ref, ra_ref, rb_ref, xa_ref, xm_ref, xo_ref, mr_ref, cr_ref, eb_ref,
    s_ref, sr_ref, dens_ref,
    t_sem, c_send, c_recv, ra_send, ra_recv, rb_send, rb_recv, xe_send, xe_recv,
    pl_send, pl_recv, xm_send, xm_recv, xo_send, xo_recv, s_send, s_recv,
    mr_send, mr_recv, cr_send, cr_recv, om_send, om_recv, ol_sem,
):
    parts, rows, cols = t_ref.shape
    nocc = c_ref.shape[1]
    chunk = rows // CHUNKS
    own = rows // 4
    half = cols // 2
    quarter = cols // 4
    per = CHUNKS // 2
    g, a, z = lax.axis_index("grp"), lax.axis_index("aux"), lax.axis_index("orb")
    mate = (1 - g, a, z)
    is_mid = (z == 1) | (z == 2)
    is_end = (z == 0) | (z == 3)
    inner = jnp.where(z == 0, 1, 2)
    outer = jnp.where(z == 1, 0, 3)
    rel = lax.bitwise_xor(a, z)

    def plane(k):
        return (g, lax.bitwise_xor(a, k), z)

    def remote(src, dst, send, recv, device):
        return pltpu.make_async_remote_copy(
            src_ref=src, dst_ref=dst, send_sem=send, recv_sem=recv,
            device_id=device, device_id_type=MESH,
        )

    def t_copy(c):
        span = pl.ds(c * chunk, chunk)
        return pltpu.make_async_copy(t_hbm.at[:, span], t_ref.at[:, span], t_sem.at[c])

    for c in range(CHUNKS):
        t_copy(c).start()

    barrier = pltpu.get_barrier_semaphore()
    for peer in (
        mate, plane(1), plane(2), plane(3),
        (g, a, lax.rem(z + 1, 4)), (g, a, lax.rem(z + 2, 4)), (g, a, lax.rem(z + 3, 4)),
    ):
        pl.semaphore_signal(barrier, inc=1, device_id=peer, device_id_type=MESH)
    pl.semaphore_wait(barrier, 7)

    def quarter_copy(src_ref, q, slot, device):
        span = pl.ds(pl.multiple_of(q * quarter, quarter), quarter)
        return remote(src_ref.at[span], cw_ref.at[span], c_send.at[slot], c_recv.at[q], device)

    first, second = 2 * g, 2 * g + 1

    @pl.when(rel == 0)
    def _():
        quarter_copy(c_ref, first, 0, plane(1)).start()
        quarter_copy(c_ref, second, 1, plane(2)).start()
        quarter_copy(c_ref, second, 2, plane(1)).start()
        quarter_copy(c_ref, first, 3, plane(2)).start()
        cw_ref[...] = c_ref[...]

    row_blocks, block_total = rows // BLK, bits_ref.shape[1]
    picked = lax.broadcasted_iota(jnp.int32, (block_total, cols), 1) // BLK + z * (cols // BLK)
    picked = (lax.broadcasted_iota(jnp.int32, (block_total, cols), 0) == picked).astype(jnp.float32)
    bits = bits_ref[0, pl.ds(pl.multiple_of(a * row_blocks, row_blocks), row_blocks), :].astype(jnp.float32)
    wide = jnp.dot(
        bits.astype(jnp.bfloat16), picked.astype(jnp.bfloat16), preferred_element_type=jnp.float32
    )
    for j in range(row_blocks):
        mask_ref[j] = wide[j : j + 1, :].astype(jnp.bfloat16)

    eye = lax.broadcasted_iota(jnp.int32, (BLK, BLK), 0) == lax.broadcasted_iota(jnp.int32, (BLK, BLK), 1)

    def to_row(column):
        return jnp.sum(jnp.where(eye, column, 0.0), axis=0, keepdims=True)

    def to_column(row):
        return jnp.sum(jnp.where(eye, row, 0.0), axis=1, keepdims=True)

    s_ref[...] = jnp.zeros_like(s_ref)
    share = jnp.where((g == 0) & (z == 0), 2.0, 0.0)

    def population_step(j, carry):
        block = c_ref[pl.ds(pl.multiple_of(j * BLK, BLK), BLK), :].astype(jnp.float32)
        row = to_row(jnp.sum(block * block, axis=1, keepdims=True))
        s_ref[pl.ds(block_total + a * row_blocks + j, 1), :] = share * row
        return carry

    lax.fori_loop(0, row_blocks, population_step, 0)

    near_count = near_ref.shape[1]
    block_ids = lax.broadcasted_iota(jnp.int32, (block_total, BLK), 0)
    for k in range(near_count):
        near_id = near_ref[:, k : k + 1]
        near_xyz = jnp.zeros((3, BLK), jnp.float32)
        for b in range(block_total):
            near_xyz = near_xyz + jnp.where(near_id == b, centres_ref[:, b * BLK : (b + 1) * BLK], 0.0)
        squares = None
        for axis in range(3):
            offset = to_column(near_xyz[axis : axis + 1, :]) - place_ref[axis : axis + 1, :]
            squares = offset * offset if squares is None else squares + offset * offset
        kern = lax.rsqrt(squares + softening)
        kern_ref[k] = kern
        contrib = to_row(jnp.sum(kern * charge_ref[...], axis=1, keepdims=True))
        s_ref[:block_total, :] += jnp.where(block_ids == near_id, contrib, 0.0)

    def potentials():
        charges = nuclear_ref[...] - s_ref[block_total : 2 * block_total, :]
        total = jnp.zeros(potential_ref.shape, jnp.float32)
        for k in range(near_count):
            near_q = jnp.sum(
                jnp.where(block_ids == near_ref[:, k : k + 1], charges, 0.0), axis=0, keepdims=True
            )
            total = total + jnp.sum(kern_ref[k] * to_column(near_q), axis=0, keepdims=True)
        potential_ref[...] = total

    @pl.when(rel != 0)
    def _():
        for rank in range(2):
            q = jnp.where(rel == 2, 2 * g + 1 - rank, 2 * g + rank)
            quarter_copy(cw_ref, q, 0, mate).wait_recv()
            if rank == 0:

                @pl.when(rel == 1)
                def _():
                    quarter_copy(cw_ref, q, 2, plane(2)).start()

                @pl.when(rel == 2)
                def _():
                    quarter_copy(cw_ref, q, 2, plane(1)).start()

            quarter_copy(cw_ref, q, rank, mate).start()
        for rank in range(2):
            quarter_copy(cw_ref, 2 * (1 - g) + rank, 0, mate).wait_recv()

    def x_span(c):
        return pl.ds(pl.multiple_of(c * chunk, chunk), chunk)

    def ra_copy(c):
        return remote(
            xp_ref.at[:, x_span(c)], ra_ref.at[:, x_span(c)], ra_send.at[c], ra_recv.at[c], (g, a, inner)
        )

    dens_ref[...] = jnp.zeros_like(dens_ref)

    def products_step(c, carry):
        t_copy(c).wait()
        span = x_span(c)
        c_rows = c_ref[span, :].astype(jnp.float32)
        blocks = chunk // BLK
        for p in range(parts):
            masked = jnp.concatenate(
                [
                    t_ref[p, pl.ds(pl.multiple_of(c * chunk + j * BLK, BLK), BLK), :]
                    * mask_ref[c * blocks + j]
                    for j in range(blocks)
                ],
                axis=0,
            )
            prod = jnp.dot(masked, cw_ref[...], preferred_element_type=jnp.float32)
            xp_ref[p, span, :] = prod.astype(jnp.bfloat16)
            dens_ref[p] += jnp.sum((prod * c_rows).reshape(chunk // 8, 8, nocc), axis=0)

        @pl.when(is_end & (c < AHEAD))
        def _():
            ra_copy(c).start()

        return carry

    lax.fori_loop(0, CHUNKS, products_step, 0)

    small = s_ref.shape[0]
    tile_rows = lax.broadcasted_iota(jnp.int32, (8, 128), 0)
    tile = jnp.zeros((8, 128), jnp.float32)
    for p in range(parts):
        lanes = jnp.sum(dens_ref[p], axis=0, keepdims=True)
        folded = lanes[:, :128]
        for j in range(1, nocc // 128):
            folded = folded + lanes[:, j * 128 : (j + 1) * 128]
        tile = tile + jnp.where(tile_rows == parts * g + p, folded, 0.0)
    s_ref[small - 8 :, :] = tile

    def s_copy(i):
        device = (mate, plane(1), plane(2))[i] if i < 3 else (g, a, lax.rem(z + i - 2, 4))
        return remote(s_ref, sr_ref.at[i], s_send.at[i], s_recv.at[i], device)

    def s_start(r):
        for i in ((0,), (1,), (2,), (3, 4, 5))[r]:
            s_copy(i).start()

    def s_finish(r):
        batch = ((0,), (1,), (2,), (3, 4, 5))[r]
        for i in batch:
            s_copy(i).wait()
        for i in batch:
            s_ref[...] += sr_ref[i]

    def rb_copy(c):
        return remote(
            xp_ref.at[:, x_span(c)], rb_ref.at[:, x_span(c)], rb_send.at[c], rb_recv.at[c], (g, a, 3 - z)
        )

    def xa_at(block, c):
        return xa_ref.at[:, pl.ds(pl.multiple_of(block * rows + c * chunk, chunk), chunk)]

    def xe_copy(c):
        return remote(xa_at(a, c), xa_at(a, c), xe_send.at[c], xe_recv.at[c], (g, a, outer))

    def pl_copy(c, k):
        return remote(
            xa_at(a, c), xa_at(a, c), pl_send.at[k - 1, c], pl_recv.at[k - 1, c], plane(k)
        )

    def pl_wait(c, k):
        block = lax.bitwise_xor(a, k)
        remote(
            xa_at(block, c), xa_at(block, c), pl_send.at[k - 1, c], pl_recv.at[k - 1, c], plane(k)
        ).wait_recv()

    def xm_copy(block, c):
        i = block * per + lax.rem(c, per)
        dst = xm_ref.at[:, pl.ds(pl.multiple_of(i * chunk, chunk), chunk)]
        return remote(xa_at(block, c), dst, xm_send.at[i], xm_recv.at[i], mate)

    def xo_copy(c):
        i = lax.rem(c, 2)
        dst = xo_ref.at[:, pl.ds(pl.multiple_of(i * chunk, chunk), chunk)]
        return remote(xa_at(a, c), dst, xo_send.at[i], xo_recv.at[i], mate)

    def for_mate(c):
        return c // per == 1 - g

    def publish(c):
        for k in (1, 2, 3):
            pl_copy(c, k).start()

        @pl.when(for_mate(c))
        def _():
            xm_copy(a, c).start()

        @pl.when(z == c // 2)
        def _():
            xo_copy(c).start()

    def stage_one(c):
        ra_copy(c).wait_recv()
        for p in range(parts):
            both = xp_ref[p, x_span(c), :].astype(jnp.float32) + ra_ref[p, x_span(c), :].astype(jnp.float32)
            xp_ref[p, x_span(c), :] = both.astype(jnp.bfloat16)
        rb_copy(c).start()

    def stage_two(c):
        rb_copy(c).wait_recv()
        for p in range(parts):
            both = xp_ref[p, x_span(c), :].astype(jnp.float32) + rb_ref[p, x_span(c), :].astype(jnp.float32)
            xa_ref[p, pl.ds(pl.multiple_of(a * rows + c * chunk, chunk), chunk), :] = both.astype(jnp.bfloat16)
        xe_copy(c).start()
        publish(c)

    def late_slot(t):
        if t == CHUNKS:

            @pl.when(is_mid)
            def _():
                stage_two(t - 1)

        @pl.when(is_end)
        def _():
            xe_copy(t - 3).wait_recv()
            publish(t - 3)

    def slot(t):
        if t >= CHUNKS:
            late_slot(t)
            return

        @pl.when(is_mid)
        def _():
            stage_one(t)
            if t >= 1:
                stage_two(t - 1)

        @pl.when(is_end)
        def _():
            ra_copy(t).wait_send()
            if t < CHUNKS - AHEAD:
                ra_copy(t + AHEAD).start()
            if t >= 3:
                xe_copy(t - 3).wait_recv()
                publish(t - 3)

    own_cols = pl.ds(pl.multiple_of(g * half, half), half)
    mate_cols = pl.ds(pl.multiple_of((1 - g) * half, half), half)

    def mr_copy(dest):
        span = pl.ds(pl.multiple_of(dest * own, own), own)
        return remote(
            t_ref.at[0, span, mate_cols], mr_ref.at[dest], mr_send.at[dest], mr_recv.at[dest], mate
        )

    def cr_copy(k):
        dest = lax.rem(z + k, 4)
        span = pl.ds(pl.multiple_of(dest * own, own), own)
        return remote(
            t_ref.at[1, span, own_cols], cr_ref.at[z], cr_send.at[k - 1], cr_recv.at[k - 1], (g, a, dest)
        )

    def cr_wait(k):
        src = lax.rem(z + 4 - k, 4)
        remote(
            t_ref.at[1, pl.ds(0, own), own_cols], cr_ref.at[src], cr_send.at[k - 1], cr_recv.at[k - 1], mate
        ).wait_recv()
        return src

    def coulomb_part(k, d):
        dest = lax.rem(z + k, 4)
        step = 32

        def body(i, carry):
            row = pl.multiple_of(dest * own + i * step, step)
            span = pl.ds(row, step)
            total = t_ref[0, span, :].astype(jnp.float32) * d[0]
            for p in range(1, parts):
                total += t_ref[p, span, :].astype(jnp.float32) * d[p]
            total = total * mask_ref[row // BLK].astype(jnp.float32)
            t_ref[0, span, :] = total.astype(jnp.bfloat16)
            return carry

        lax.fori_loop(0, own // step, body, 0)
        mr_copy(dest).start()

    def coulomb_sum(k):
        dest = lax.rem(z + k, 4)
        mr_copy(dest).wait_recv()
        step = 64

        def body(i, carry):
            span = pl.ds(pl.multiple_of(dest * own + i * step, step), step)
            piece = pl.ds(pl.multiple_of(i * step, step), step)
            both = t_ref[0, span, own_cols].astype(jnp.float32) + mr_ref[dest, piece, :].astype(jnp.float32)
            if k:
                t_ref[1, span, own_cols] = both.astype(jnp.bfloat16)
            else:
                cr_ref[dest, piece, :] = both.astype(jnp.bfloat16)
            return carry

        lax.fori_loop(0, own // step, body, 0)

    s_start(0)
    s_finish(0)
    s_start(1)
    slot(0)
    s_finish(1)
    s_start(2)
    s_finish(2)
    s_start(3)
    slot(1)
    slot(2)
    s_finish(3)
    dens_tile = s_ref[small - 8 :, :]
    d = []
    for p in range(parts):
        row = jnp.where(tile_rows == parts * g + p, dens_tile, 0.0)
        value = 2.0 * jnp.sum(jnp.sum(row, axis=1, keepdims=True), axis=0, keepdims=True)
        d.append(value.astype(jnp.bfloat16).astype(jnp.float32))
    order = (2, 1, 3, 0)
    slot(3)
    coulomb_part(order[0], d)
    potentials()
    for i in range(1, 4):
        coulomb_part(order[i], d)
        coulomb_sum(order[i - 1])
        slot(3 + i)
    coulomb_sum(order[3])
    slot(7)

    @pl.when(is_end)
    def _():
        for k in order[:3]:
            cr_copy(k).start()

    slot(8)

    @pl.when(is_mid)
    def _():
        for k in order[:3]:
            cr_copy(k).start()

    slot(9)
    slot(10)

    def arrive(c, carry):
        for k in (1, 2, 3):
            pl_wait(c, k)

            @pl.when(for_mate(c))
            def _():
                xm_copy(lax.bitwise_xor(a, k), c).start()

        return carry

    lax.fori_loop(0, CHUNKS, arrive, 0)

    for i in range(2):
        xo_copy(i).wait_recv()
    dims = (((1,), (1,)), ((), ()))
    own_rows = pl.ds(pl.multiple_of(a * rows + z * own, own), own)

    def exchange(block, carry):
        def body(j, inside):
            i = block * per + j
            xm_copy(block, j).wait_recv()
            total = jnp.zeros((own, chunk), jnp.float32)
            near = pl.ds(pl.multiple_of(block * rows + g * half + j * chunk, chunk), chunk)
            far = pl.ds(pl.multiple_of(i * chunk, chunk), chunk)
            for p in range(parts):
                total += lax.dot_general(
                    xa_ref[p, own_rows, :], xa_ref[p, near, :], dims, preferred_element_type=jnp.float32
                )
                total += lax.dot_general(
                    xo_ref[p], xm_ref[p, far, :], dims, preferred_element_type=jnp.float32
                )
            first = jnp.where(block == a, g * half + j * chunk - z * own, -4 * rows)
            field_row = a * row_blocks + g * (half // BLK) + j * (chunk // BLK)
            field = jnp.concatenate(
                [s_ref[pl.ds(field_row + i, 1), :] for i in range(chunk // BLK)], axis=1
            )
            diagonal = lax.broadcasted_iota(jnp.int32, (own, chunk), 0) == first + lax.broadcasted_iota(
                jnp.int32, (own, chunk), 1
            )
            total = jnp.where(diagonal, field, 0.0) - 0.5 * total
            eb_ref[block, :, pl.ds(pl.multiple_of(j * chunk, chunk), chunk)] = total.astype(jnp.bfloat16)
            return inside

        return lax.fori_loop(0, per, body, carry)

    lax.fori_loop(0, 4, exchange, 0)

    def out_cols(block, core):
        return pl.ds(pl.multiple_of(block * cols + core * half, half), half)

    def om_copy(block):
        return remote(
            eb_ref.at[block], out_ref.at[:, out_cols(block, g)], om_send.at[block], om_recv.at[block], mate
        )

    def ol_copy(block):
        return pltpu.make_async_copy(eb_ref.at[block], out_ref.at[:, out_cols(block, g)], ol_sem.at[block])

    for k in (0, 1, 3, 2):
        src = cr_wait(k) if k else z
        step = 64

        def body(i, carry):
            piece = pl.ds(pl.multiple_of(i * step, step), step)
            both = eb_ref[src, piece, :].astype(jnp.float32) + cr_ref[src, piece, :].astype(jnp.float32)
            eb_ref[src, piece, :] = both.astype(jnp.bfloat16)
            return carry

        lax.fori_loop(0, own // step, body, 0)
        om_copy(src).start()
        ol_copy(src).start()

    for block in range(4):
        remote(
            eb_ref.at[block], out_ref.at[:, out_cols(block, 1 - g)], om_send.at[block], om_recv.at[block], mate
        ).wait()
        ol_copy(block).wait()
        mr_copy(block).wait_send()
    for k in (1, 2, 3):
        cr_copy(k).wait_send()

    @pl.when(rel == 0)
    def _():
        for i in range(4):
            quarter_copy(c_ref, first, i, mate).wait_send()

    @pl.when(rel != 0)
    def _():
        for i in range(2):
            quarter_copy(cw_ref, first, i, mate).wait_send()

    @pl.when((rel == 1) | (rel == 2))
    def _():
        quarter_copy(cw_ref, first, 2, mate).wait_send()

    def drain(c, carry):
        @pl.when(is_mid)
        def _():
            rb_copy(c).wait_send()
            xe_copy(c).wait_send()

        for k in (1, 2, 3):
            pl_copy(c, k).wait_send()

        @pl.when(for_mate(c))
        def _():
            for block in range(4):
                xm_copy(block, c).wait_send()

        return carry

    lax.fori_loop(0, CHUNKS, drain, 0)
    for i in range(2):
        xo_copy(i).wait_send()


def grid_call(fitted, block_mask, own_c, nuclear, centres, positions, charges, neighbours):
    parts, rows, cols = fitted.shape
    nocc = own_c.shape[1]
    own, half = rows // 4, cols // 2
    block_total = block_mask.shape[1]
    small = (2 * block_total + 8, BLK)
    bf16, f32 = jnp.bfloat16, jnp.float32
    vmem = pl.BlockSpec(memory_space=pltpu.VMEM)
    hbm = pl.BlockSpec(memory_space=pl.ANY)
    dma = pltpu.SemaphoreType.DMA
    return pl.pallas_call(
        grid_kernel,
        in_specs=[hbm] + [vmem] * 7,
        out_specs=[hbm, vmem],
        out_shape=[
            jax.ShapeDtypeStruct((own, 4 * cols), bf16),
            jax.ShapeDtypeStruct((1, positions.shape[1]), f32),
        ],
        scratch_shapes=[
            pltpu.VMEM((parts, rows, cols), bf16),
            pltpu.VMEM((rows // BLK, 1, cols), bf16),
            pltpu.VMEM((neighbours.shape[1], BLK, positions.shape[1]), f32),
            pltpu.VMEM((cols, nocc), bf16),
            pltpu.VMEM((parts, rows, nocc), bf16),
            pltpu.VMEM((parts, rows, nocc), bf16),
            pltpu.VMEM((parts, rows, nocc), bf16),
            pltpu.VMEM((parts, 4 * rows, nocc), bf16),
            pltpu.VMEM((parts, 2 * rows, nocc), bf16),
            pltpu.VMEM((parts, own, nocc), bf16),
            pltpu.VMEM((4, own, half), bf16),
            pltpu.VMEM((4, own, half), bf16),
            pltpu.VMEM((4, own, half), bf16),
            pltpu.VMEM(small, f32),
            pltpu.VMEM((6,) + small, f32),
            pltpu.VMEM((parts, 8, nocc), f32),
            dma((CHUNKS,)),
            dma((4,)), dma((4,)),
            dma((CHUNKS,)), dma((CHUNKS,)),
            dma((CHUNKS,)), dma((CHUNKS,)),
            dma((CHUNKS,)), dma((CHUNKS,)),
            dma((3, CHUNKS)), dma((3, CHUNKS)),
            dma((2 * CHUNKS,)), dma((2 * CHUNKS,)),
            dma((2,)), dma((2,)),
            dma((6,)), dma((6,)),
            dma((4,)), dma((4,)),
            dma((3,)), dma((3,)),
            dma((4,)), dma((4,)),
            dma((4,)),
        ],
        compiler_params=pltpu.CompilerParams(
            collective_id=0, has_side_effects=True, vmem_limit_bytes=GRID_VMEM
        ),
        cost_estimate=pl.CostEstimate(
            flops=2 * parts * rows * cols * nocc + 8 * parts * own * 2 * cols * nocc,
            bytes_accessed=2 * parts * rows * cols + 8 * own * cols,
            transcendentals=0,
        ),
        name="grid",
    )(
        fitted, block_mask, own_c, nuclear.reshape(block_total, BLK), centres, positions,
        charges.reshape(1, -1), neighbours,
    )


def finish_kernel(in_ref, out_ref):
    out_ref[...] = in_ref[...].astype(jnp.float32)


def finish_call(fock16):
    rows, cols = fock16.shape
    step = 64
    spec = pl.BlockSpec((step, cols), lambda i: (i, 0))
    return pl.pallas_call(
        finish_kernel,
        grid=(rows // step,),
        in_specs=[spec],
        out_specs=spec,
        out_shape=jax.ShapeDtypeStruct((rows, cols), jnp.float32),
        compiler_params=pltpu.CompilerParams(vmem_limit_bytes=VMEM_LIMIT),
        cost_estimate=pl.CostEstimate(
            flops=rows * cols, bytes_accessed=6 * rows * cols, transcendentals=0
        ),
        name="finish",
    )(fock16)


def per_device_grid(
    fitted_tensor, block_mask, orbitals, nuclear, centres, mm_positions, mm_charges, neighbours
):
    fock16, potential = grid_call(
        fitted_tensor, block_mask, orbitals, nuclear, centres, mm_positions, mm_charges, neighbours
    )
    return (finish_call(fock16), potential.reshape(-1))


def grid_fits(mesh, fitted_tensor, orbitals):
    shape = mesh.shape
    parts = fitted_tensor.shape[0] // shape["grp"]
    rows = fitted_tensor.shape[1] // shape["aux"]
    cols = fitted_tensor.shape[2] // shape["orb"]
    return (
        shape["grp"] == 2
        and shape["aux"] == 4
        and shape["orb"] == 4
        and parts == 2
        and rows == cols
        and rows % (CHUNKS * BLK) == 0
        and orbitals.shape[1] % BLK == 0
        and 7 * rows * cols + 41 * rows * orbitals.shape[1] <= 52 * 2**20
    )


def solution(mesh):
    in_specs = (
        P("grp", "aux", "orb"),
        P("grp", None, None),
        P("aux", None),
        P(),
        P(),
        P(None, ("grp", "aux", "orb")),
        P(("grp", "aux", "orb")),
        P(("grp", "aux", "orb"), None),
    )
    out_specs = (P(("aux", "orb"), None), P(("grp", "aux", "orb")))
    def build(body):
        return jax.shard_map(
            body, mesh=mesh, in_specs=in_specs, out_specs=out_specs, check_vma=False
        )

    def run(fitted_tensor, block_mask, orbitals, *rest):
        body = per_device_grid if grid_fits(mesh, fitted_tensor, orbitals) else per_device
        return build(body)(fitted_tensor, block_mask, orbitals, *rest)

    return run
```

```python
import functools

import jax
import jax.numpy as jnp
from jax import lax
from jax.experimental import pallas as pl
from jax.experimental.pallas import tpu as pltpu
from jax.sharding import PartitionSpec as P

BLK = 128
VMEM_LIMIT = 48 * 1024 * 1024

softening = 1.0


def near_kernel(picker, centre_blocks, atom_xyz):
    near_xyz = jnp.einsum("kb,cbj->ckj", picker, centre_blocks, precision=lax.Precision.HIGHEST)
    near_xyz = near_xyz.reshape(3, picker.shape[0] * centre_blocks.shape[2])
    offsets = near_xyz[:, :, None] - atom_xyz[:, None, :]
    return lax.rsqrt(jnp.sum(offsets * offsets, axis=0) + softening)


def products_kernel(t_ref, mask_ref, win_ref, c_ref, x_ref, dens_ref):
    parts, rows, cols = t_ref.shape
    row_mask = mask_ref[0]

    @pl.when(pl.program_id(0) == 0)
    def _():
        dens_ref[...] = jnp.zeros_like(dens_ref)

    own = c_ref[...].astype(jnp.float32)
    for p in range(parts):
        prod = jnp.dot(t_ref[p] * row_mask, win_ref[...], preferred_element_type=jnp.float32)
        x_ref[p] = prod.astype(x_ref.dtype)
        dens_ref[p] += jnp.sum((prod * own).reshape(rows // 8, 8, prod.shape[1]), axis=0)


def products_call(fitted, mask_rows, window_c, own_c):
    parts, rows, cols = fitted.shape
    nocc = window_c.shape[1]
    return pl.pallas_call(
        products_kernel,
        grid=(rows // BLK,),
        in_specs=[
            pl.BlockSpec((parts, BLK, cols), lambda i: (0, i, 0)),
            pl.BlockSpec((1, 1, cols), lambda i: (i, 0, 0)),
            pl.BlockSpec((cols, nocc), lambda i: (0, 0)),
            pl.BlockSpec((BLK, nocc), lambda i: (i, 0)),
        ],
        out_specs=[
            pl.BlockSpec((parts, BLK, nocc), lambda i: (0, i, 0)),
            pl.BlockSpec((parts, 8, nocc), lambda i: (0, 0, 0)),
        ],
        out_shape=[
            jax.ShapeDtypeStruct((parts, rows, nocc), jnp.bfloat16),
            jax.ShapeDtypeStruct((parts, 8, nocc), jnp.float32),
        ],
        compiler_params=pltpu.CompilerParams(vmem_limit_bytes=VMEM_LIMIT),
        cost_estimate=pl.CostEstimate(
            flops=2 * parts * rows * cols * nocc,
            bytes_accessed=2 * parts * rows * (cols + nocc),
            transcendentals=0,
        ),
        name="products",
    )(fitted, mask_rows, window_c, own_c)


def coulomb_kernel(place_ref, dens_ref, ta_ref, ma_ref, tk_ref, mk_ref, away_ref, kept_ref):
    for t_ref, mask_ref, out_ref in ((ta_ref, ma_ref, away_ref), (tk_ref, mk_ref, kept_ref)):
        total = t_ref[0].astype(jnp.float32) * dens_ref[0]
        for p in range(1, t_ref.shape[0]):
            total += t_ref[p].astype(jnp.float32) * dens_ref[p]
        out_ref[...] = (total * mask_ref[0].astype(jnp.float32)).astype(out_ref.dtype)


def coulomb_call(place, densities, fitted, mask_rows, half):
    parts, rows, cols = fitted.shape
    tile = min(BLK, half)
    steps = half // tile

    def away_tile(i, place_ref):
        return (place_ref[1] * 2 + 1 - place_ref[0]) * steps + i

    def kept_tile(i, place_ref):
        return (place_ref[1] * 2 + place_ref[0]) * steps + i

    def tensor_spec(which):
        return pl.BlockSpec((parts, tile, cols), lambda i, place_ref, d: (0, which(i, place_ref), 0))

    def mask_spec(which):
        return pl.BlockSpec(
            (1, 1, cols), lambda i, place_ref, d: (which(i, place_ref) * tile // BLK, 0, 0)
        )

    return pl.pallas_call(
        coulomb_kernel,
        grid_spec=pltpu.PrefetchScalarGridSpec(
            num_scalar_prefetch=2,
            grid=(steps,),
            in_specs=[
                tensor_spec(away_tile),
                mask_spec(away_tile),
                tensor_spec(kept_tile),
                mask_spec(kept_tile),
            ],
            out_specs=[pl.BlockSpec((tile, cols), lambda i, place_ref, d: (i, 0))] * 2,
        ),
        out_shape=[jax.ShapeDtypeStruct((half, cols), jnp.bfloat16)] * 2,
        compiler_params=pltpu.CompilerParams(vmem_limit_bytes=VMEM_LIMIT),
        cost_estimate=pl.CostEstimate(
            flops=4 * parts * half * cols,
            bytes_accessed=4 * half * cols * (parts + 1),
            transcendentals=0,
        ),
        name="coulomb",
    )(place, densities, fitted, mask_rows, fitted, mask_rows)


def fock_kernel(shifts, place_ref, own_ref, mate_ref, all_ref, mate_all_ref, field_ref, *refs):
    mine, theirs, out_ref = refs[:shifts], refs[shifts : 2 * shifts], refs[2 * shifts]
    parts = own_ref.shape[0]
    rows, cols = out_ref.shape
    half = rows // 2
    per_src = mine[0].shape[1] // cols
    dims = (((1,), (1,)), ((), ()))
    grp_id, row0, orb_id = place_ref[0], place_ref[1], place_ref[2]

    def slab(a, b):
        total = lax.dot_general(a[0], b[0], dims, preferred_element_type=jnp.float32)
        for p in range(1, parts):
            total += lax.dot_general(a[p], b[p], dims, preferred_element_type=jnp.float32)
        return total

    out_ref[...] = -0.5 * (slab(own_ref, all_ref) + slab(mate_ref, mate_all_ref))

    step = pl.program_id(0)
    shift = lax.rem(orb_id - step // per_src + shifts, shifts)
    col_in = pl.multiple_of(lax.rem(step, per_src) * cols, cols)
    own_row = pl.multiple_of(grp_id * half, half)
    mate_row = pl.multiple_of((1 - grp_id) * half, half)
    for k in range(shifts):

        @pl.when(shift == k)
        def _():
            out_ref[pl.ds(own_row, half), :] += mine[k][:, pl.ds(col_in, cols)].astype(jnp.float32)
            out_ref[pl.ds(mate_row, half), :] += theirs[k][:, pl.ds(col_in, cols)].astype(jnp.float32)

    col0 = step * cols

    @pl.when((row0 < col0 + cols) & (row0 + rows > col0))
    def _():
        row_ids = row0 + lax.broadcasted_iota(jnp.int32, (rows, cols), 0)
        col_ids = col0 + lax.broadcasted_iota(jnp.int32, (rows, cols), 1)
        out_ref[...] += jnp.where(row_ids == col_ids, field_ref[...], jnp.float32(0.0))


def fock_call(place, x_own, x_mate, x_all, x_mate_all, field_col, mine, theirs):
    parts, rows, nocc = x_own.shape
    total = x_all.shape[1]
    half, per_src = mine[0].shape
    cols = min(1024, per_src)
    own_spec = pl.BlockSpec((parts, rows, nocc), lambda j: (0, 0, 0))
    all_spec = pl.BlockSpec((parts, cols, nocc), lambda j: (0, j, 0))
    return pl.pallas_call(
        functools.partial(fock_kernel, len(mine)),
        grid=(total // cols,),
        in_specs=[
            pl.BlockSpec(memory_space=pltpu.SMEM),
            own_spec,
            own_spec,
            all_spec,
            all_spec,
            pl.BlockSpec((rows, 1), lambda j: (0, 0)),
        ]
        + [pl.BlockSpec((half, per_src), lambda j: (0, 0))] * (2 * len(mine)),
        out_specs=pl.BlockSpec((rows, cols), lambda j: (0, j)),
        out_shape=jax.ShapeDtypeStruct((rows, total), jnp.float32),
        compiler_params=pltpu.CompilerParams(vmem_limit_bytes=VMEM_LIMIT),
        cost_estimate=pl.CostEstimate(
            flops=4 * parts * rows * total * nocc,
            bytes_accessed=4 * parts * total * nocc + 4 * rows * total + 2 * rows * total,
            transcendentals=0,
        ),
        name="fock",
    )(place, x_own, x_mate, x_all, x_mate_all, field_col, *mine, *theirs)


def swap(value):
    return lax.ppermute(value, "grp", [(0, 1), (1, 0)])


def per_device(
    fitted_tensor, block_mask, orbitals, nuclear, centres, mm_positions, mm_charges, neighbours
):
    parts, row_span, col_span = fitted_tensor.shape
    nocc = orbitals.shape[1]
    orb_count = lax.axis_size("orb")
    aux_count = lax.axis_size("aux")
    grp_count = lax.axis_size("grp")
    grp_id = lax.axis_index("grp")
    aux_id = lax.axis_index("aux")
    orb_id = lax.axis_index("orb")
    own_span = row_span // orb_count
    half = own_span // 2
    block_total = block_mask.shape[1]
    row_start = aux_id * row_span
    col_start = orb_id * col_span

    if aux_count == orb_count:
        perm = [
            (a * orb_count + o, o * orb_count + a)
            for a in range(aux_count)
            for o in range(orb_count)
        ]
        c_half = lax.dynamic_slice_in_dim(orbitals, grp_id * (row_span // 2), row_span // 2, 0)
        c_half = lax.ppermute(c_half, ("aux", "orb"), perm)
        c_mate = swap(c_half)
        window_c = jnp.where(
            grp_id == 0, jnp.stack([c_half, c_mate]), jnp.stack([c_mate, c_half])
        ).reshape(col_span, nocc)
    else:
        whole_c = lax.all_gather(orbitals, "aux", axis=0, tiled=True)
        window_c = lax.dynamic_slice_in_dim(whole_c, col_start, col_span, 0)

    bits = lax.dynamic_slice(
        block_mask[0],
        (row_start // BLK, col_start // BLK),
        (row_span // BLK, col_span // BLK),
    ).astype(jnp.bfloat16)
    mask_rows = jnp.repeat(bits, BLK, axis=1)[:, None, :]

    own_float = orbitals.astype(jnp.float32)
    own_population = 2.0 * jnp.sum(own_float * own_float, axis=1)
    population = lax.all_gather(own_population, "aux", axis=0, tiled=True)
    centre_blocks = centres.reshape(3, block_total, BLK)
    picker = (neighbours[0][:, None] == jnp.arange(block_total, dtype=jnp.int32)[None, :]).astype(
        jnp.float32
    )
    kernel = near_kernel(picker, centre_blocks, mm_positions)
    contrib = jnp.dot(kernel, mm_charges, precision=lax.Precision.HIGHEST).reshape(
        picker.shape[0], BLK
    )
    field_part = jnp.dot(picker.T, contrib, precision=lax.Precision.HIGHEST)

    window_c, population = lax.optimization_barrier((window_c, population))
    qm_charge = nuclear - population
    charge_blocks = qm_charge.reshape(block_total, BLK)
    near_q = jnp.dot(picker, charge_blocks, precision=lax.Precision.HIGHEST).reshape(-1)
    mm_potential = jnp.dot(near_q, kernel, precision=lax.Precision.HIGHEST)

    x_part, dens_lanes = products_call(fitted_tensor, mask_rows, window_c, orbitals)
    dens_part = 2.0 * jnp.sum(dens_lanes, axis=(1, 2))
    dens_slots = jnp.zeros((grp_count, BLK), jnp.float32)
    dens_slots = lax.dynamic_update_slice(dens_slots, dens_part[None, :], (grp_id, 0))
    sums = lax.psum(jnp.concatenate([field_part, dens_slots], axis=0), ("grp", "aux", "orb"))

    x_blocks = x_part.reshape(parts, orb_count, own_span, nocc)
    targets = [lax.rem(orb_id + k, orb_count) for k in range(orb_count)]
    moves = [[(s, (s + k) % orb_count) for s in range(orb_count)] for k in range(orb_count)]
    arrived = []
    for k in range(1, orb_count):
        block = lax.dynamic_index_in_dim(x_blocks, targets[k], 1, keepdims=False)
        arrived.append(lax.ppermute(block, "orb", moves[k]))
    sums, *arrived = lax.optimization_barrier((sums, *arrived))
    field_vec = sums[:block_total].reshape(-1)
    densities = lax.dynamic_slice(sums, (block_total + grp_id, 0), (1, parts))[0]
    x_sum = lax.dynamic_index_in_dim(x_blocks, orb_id, 1, keepdims=False).astype(jnp.float32)
    for block in arrived:
        x_sum += block.astype(jnp.float32)
    x_own = x_sum.astype(jnp.bfloat16)
    x_mate = swap(x_own)
    x_all = lax.all_gather(x_own, ("aux", "orb"), axis=1, tiled=True)

    mine = [None] * orb_count
    for k in list(range(1, orb_count)) + [0]:
        at = jnp.stack([grp_id, targets[k]]).astype(jnp.int32)
        away, kept = coulomb_call(at, densities, fitted_tensor, mask_rows, half)
        both = (kept.astype(jnp.float32) + swap(away).astype(jnp.float32)).astype(jnp.bfloat16)
        mine[k] = lax.ppermute(both, "orb", moves[k]) if k else both
    x_all, *mine = lax.optimization_barrier((x_all, *mine))
    theirs = [swap(block) for block in mine]
    x_mate_all = swap(x_all)

    own_first = row_start + orb_id * own_span
    field_col = lax.dynamic_slice_in_dim(field_vec, own_first, own_span, 0)[:, None]
    place = jnp.stack([grp_id, own_first, orb_id]).astype(jnp.int32)
    fock = fock_call(place, x_own, x_mate, x_all, x_mate_all, field_col, mine, theirs)
    return (fock, mm_potential)


MESH = pl.DeviceIdType.MESH
CHUNKS = 16
STEPS = 8
AHEAD = 2
LAG = 4
PIECES = 4
GRID_VMEM = 58 * 1024 * 1024


def grid_kernel(
    t_hbm, bits_ref, c_ref, nuclear_ref, centres_ref, place_ref, charge_ref, near_ref,
    out_ref, potential_ref,
    t_ref, mask_ref, kern_ref, cw_ref, xp_ref, ra_ref, rb_ref, xa_ref, xm_ref, xo_ref, mr_ref, cr_ref, eb_ref,
    s_ref, sr_ref, dens_ref,
    t_sem, c_send, c_recv, ra_send, ra_recv, rb_send, rb_recv, xe_send, xe_recv,
    pl_send, pl_recv, xm_send, xm_recv, xo_send, xo_recv, s_send, s_recv,
    mr_send, mr_recv, cr_send, cr_recv, om_send, om_recv, ol_sem,
):
    parts, rows, cols = t_ref.shape
    nocc = c_ref.shape[1]
    chunk = rows // CHUNKS
    load = rows // STEPS
    tile = 2 * BLK
    own = rows // 4
    piece = own // PIECES
    per_own = own // chunk
    half = cols // 2
    quarter = cols // 4
    per = CHUNKS // 2
    g, a, z = lax.axis_index("grp"), lax.axis_index("aux"), lax.axis_index("orb")
    mate = (1 - g, a, z)
    is_mid = (z == 1) | (z == 2)
    is_end = (z == 0) | (z == 3)
    inner = jnp.where(z == 0, 1, 2)
    outer = jnp.where(z == 1, 0, 3)
    rel = lax.bitwise_xor(a, z)

    def plane(k):
        return (g, lax.bitwise_xor(a, k), z)

    def remote(src, dst, send, recv, device):
        return pltpu.make_async_remote_copy(
            src_ref=src, dst_ref=dst, send_sem=send, recv_sem=recv,
            device_id=device, device_id_type=MESH,
        )

    def t_copy(c):
        span = pl.ds(c * load, load)
        return pltpu.make_async_copy(t_hbm.at[:, span], t_ref.at[:, span], t_sem.at[c])

    for c in range(STEPS):
        t_copy(c).start()

    barrier = pltpu.get_barrier_semaphore()
    for peer in (
        mate, plane(1), plane(2), plane(3),
        (g, a, lax.rem(z + 1, 4)), (g, a, lax.rem(z + 2, 4)), (g, a, lax.rem(z + 3, 4)),
    ):
        pl.semaphore_signal(barrier, inc=1, device_id=peer, device_id_type=MESH)
    pl.semaphore_wait(barrier, 7)

    def quarter_copy(src_ref, q, slot, device):
        span = pl.ds(pl.multiple_of(q * quarter, quarter), quarter)
        return remote(src_ref.at[span], cw_ref.at[span], c_send.at[slot], c_recv.at[q], device)

    first, second = 2 * g, 2 * g + 1

    @pl.when(rel == 0)
    def _():
        quarter_copy(c_ref, first, 0, plane(1)).start()
        quarter_copy(c_ref, second, 1, plane(2)).start()
        cw_ref[...] = c_ref[...]

    row_blocks, block_total = rows // BLK, bits_ref.shape[1]
    picked = lax.broadcasted_iota(jnp.int32, (block_total, cols), 1) // BLK + z * (cols // BLK)
    picked = (lax.broadcasted_iota(jnp.int32, (block_total, cols), 0) == picked).astype(jnp.float32)
    bits = bits_ref[0, pl.ds(pl.multiple_of(a * row_blocks, row_blocks), row_blocks), :].astype(jnp.float32)
    wide = jnp.dot(
        bits.astype(jnp.bfloat16), picked.astype(jnp.bfloat16), preferred_element_type=jnp.float32
    )
    for j in range(row_blocks):
        mask_ref[j] = wide[j : j + 1, :].astype(jnp.bfloat16)

    eye = lax.broadcasted_iota(jnp.int32, (BLK, BLK), 0) == lax.broadcasted_iota(jnp.int32, (BLK, BLK), 1)

    def to_row(column):
        return jnp.sum(jnp.where(eye, column, 0.0), axis=0, keepdims=True)

    def to_column(row):
        return jnp.sum(jnp.where(eye, row, 0.0), axis=1, keepdims=True)

    @pl.when(rel == 0)
    def _():
        quarter_copy(c_ref, first, 0, plane(1)).wait_send()
        quarter_copy(c_ref, second, 2, plane(1)).start()
        quarter_copy(c_ref, second, 1, plane(2)).wait_send()
        quarter_copy(c_ref, first, 3, plane(2)).start()

    s_ref[...] = jnp.zeros_like(s_ref)
    share = jnp.where((g == 0) & (z == 0), 2.0, 0.0)

    def population_step(j, carry):
        block = c_ref[pl.ds(pl.multiple_of(j * BLK, BLK), BLK), :].astype(jnp.float32)
        row = to_row(jnp.sum(block * block, axis=1, keepdims=True))
        s_ref[pl.ds(block_total + a * row_blocks + j, 1), :] = share * row
        return carry

    lax.fori_loop(0, row_blocks, population_step, 0)

    near_count = near_ref.shape[1]
    block_ids = lax.broadcasted_iota(jnp.int32, (block_total, BLK), 0)
    for k in range(near_count):
        near_id = near_ref[:, k : k + 1]
        near_xyz = jnp.zeros((3, BLK), jnp.float32)
        for b in range(block_total):
            near_xyz = near_xyz + jnp.where(near_id == b, centres_ref[:, b * BLK : (b + 1) * BLK], 0.0)
        squares = None
        for axis in range(3):
            offset = to_column(near_xyz[axis : axis + 1, :]) - place_ref[axis : axis + 1, :]
            squares = offset * offset if squares is None else squares + offset * offset
        kern = lax.rsqrt(squares + softening)
        kern_ref[k] = kern
        contrib = to_row(jnp.sum(kern * charge_ref[...], axis=1, keepdims=True))
        s_ref[:block_total, :] += jnp.where(block_ids == near_id, contrib, 0.0)

    def potentials():
        charges = nuclear_ref[...] - s_ref[block_total : 2 * block_total, :]
        total = jnp.zeros(potential_ref.shape, jnp.float32)
        for k in range(near_count):
            near_q = jnp.sum(
                jnp.where(block_ids == near_ref[:, k : k + 1], charges, 0.0), axis=0, keepdims=True
            )
            total = total + jnp.sum(kern_ref[k] * to_column(near_q), axis=0, keepdims=True)
        potential_ref[...] = total

    @pl.when(rel != 0)
    def _():
        for rank in range(2):
            q = jnp.where(rel == 2, 2 * g + 1 - rank, 2 * g + rank)
            quarter_copy(cw_ref, q, 0, mate).wait_recv()
            if rank == 0:

                @pl.when(rel == 1)
                def _():
                    quarter_copy(cw_ref, q, 2, plane(2)).start()

                @pl.when(rel == 2)
                def _():
                    quarter_copy(cw_ref, q, 2, plane(1)).start()

            quarter_copy(cw_ref, q, rank, mate).start()
        for rank in range(2):
            quarter_copy(cw_ref, 2 * (1 - g) + rank, 0, mate).wait_recv()

    def x_span(c):
        return pl.ds(pl.multiple_of(c * chunk, chunk), chunk)

    def ra_copy(c):
        return remote(
            xp_ref.at[:, x_span(c)], ra_ref.at[:, x_span(c)], ra_send.at[c], ra_recv.at[c], (g, a, inner)
        )

    dens_ref[...] = jnp.zeros_like(dens_ref)

    def products_step(c, carry):
        t_copy(c).wait()
        span = pl.ds(pl.multiple_of(c * load, load), load)
        c_rows = c_ref[span, :].astype(jnp.float32)
        blocks = load // BLK
        for p in range(parts):
            masked = jnp.concatenate(
                [
                    t_ref[p, pl.ds(pl.multiple_of(c * load + j * BLK, BLK), BLK), :]
                    * mask_ref[c * blocks + j]
                    for j in range(blocks)
                ],
                axis=0,
            )
            prod = jnp.dot(masked, cw_ref[...], preferred_element_type=jnp.float32)
            xp_ref[p, span, :] = prod.astype(jnp.bfloat16)
            dens_ref[p] += jnp.sum((prod * c_rows).reshape(load // 8, 8, nocc), axis=0)

        @pl.when(is_end & (c == 0))
        def _():
            for first_chunk in range(AHEAD):
                ra_copy(first_chunk).start()

        return carry

    lax.fori_loop(0, STEPS, products_step, 0)

    small = s_ref.shape[0]
    tile_rows = lax.broadcasted_iota(jnp.int32, (8, 128), 0)
    dens_rows = jnp.zeros((8, 128), jnp.float32)
    for p in range(parts):
        lanes = jnp.sum(dens_ref[p], axis=0, keepdims=True)
        folded = lanes[:, :128]
        for j in range(1, nocc // 128):
            folded = folded + lanes[:, j * 128 : (j + 1) * 128]
        dens_rows = dens_rows + jnp.where(tile_rows == parts * g + p, folded, 0.0)
    s_ref[small - 8 :, :] = dens_rows

    def s_copy(i):
        device = (mate, plane(1), plane(2))[i] if i < 3 else (g, a, lax.rem(z + i - 2, 4))
        return remote(s_ref, sr_ref.at[i], s_send.at[i], s_recv.at[i], device)

    def s_start(r):
        for i in ((0,), (1,), (2,), (3, 4, 5))[r]:
            s_copy(i).start()

    def s_finish(r):
        batch = ((0,), (1,), (2,), (3, 4, 5))[r]
        for i in batch:
            s_copy(i).wait()
        for i in batch:
            s_ref[...] += sr_ref[i]

    def rb_copy(c):
        return remote(
            xp_ref.at[:, x_span(c)], rb_ref.at[:, x_span(c)], rb_send.at[c], rb_recv.at[c], (g, a, 3 - z)
        )

    def xa_at(block, c):
        return xa_ref.at[:, pl.ds(pl.multiple_of(block * rows + c * chunk, chunk), chunk)]

    def xe_copy(c):
        return remote(xa_at(a, c), xa_at(a, c), xe_send.at[c], xe_recv.at[c], (g, a, outer))

    def pl_copy(c, k):
        return remote(
            xa_at(a, c), xa_at(a, c), pl_send.at[k - 1, c], pl_recv.at[k - 1, c], plane(k)
        )

    def pl_wait(c, k):
        block = lax.bitwise_xor(a, k)
        remote(
            xa_at(block, c), xa_at(block, c), pl_send.at[k - 1, c], pl_recv.at[k - 1, c], plane(k)
        ).wait_recv()

    def xm_copy(block, c):
        i = block * per + lax.rem(c, per)
        dst = xm_ref.at[:, pl.ds(pl.multiple_of(i * chunk, chunk), chunk)]
        return remote(xa_at(block, c), dst, xm_send.at[i], xm_recv.at[i], mate)

    def xo_copy(c):
        i = lax.rem(c, per_own)
        dst = xo_ref.at[:, pl.ds(pl.multiple_of(i * chunk, chunk), chunk)]
        return remote(xa_at(a, c), dst, xo_send.at[i], xo_recv.at[i], mate)

    def for_mate(c):
        return c // per == 1 - g

    def publish(c):
        for k in (1, 2, 3):
            pl_copy(c, k).start()

        @pl.when(for_mate(c))
        def _():
            xm_copy(a, c).start()

        @pl.when(z == c // per_own)
        def _():
            xo_copy(c).start()

    def stage_one(c):
        ra_copy(c).wait_recv()
        for p in range(parts):
            both = xp_ref[p, x_span(c), :].astype(jnp.float32) + ra_ref[p, x_span(c), :].astype(jnp.float32)
            xp_ref[p, x_span(c), :] = both.astype(jnp.bfloat16)
        rb_copy(c).start()

    def stage_two(c):
        rb_copy(c).wait_recv()
        for p in range(parts):
            both = xp_ref[p, x_span(c), :].astype(jnp.float32) + rb_ref[p, x_span(c), :].astype(jnp.float32)
            xa_ref[p, pl.ds(pl.multiple_of(a * rows + c * chunk, chunk), chunk), :] = both.astype(jnp.bfloat16)
        xe_copy(c).start()
        publish(c)

    def late_slot(t):
        if t == CHUNKS:

            @pl.when(is_mid)
            def _():
                stage_two(t - 1)

        @pl.when(is_end)
        def _():
            xe_copy(t - LAG).wait_recv()
            publish(t - LAG)

    def slot(t):
        if t >= CHUNKS:
            late_slot(t)
            return

        @pl.when(is_mid)
        def _():
            stage_one(t)
            if t >= 1:
                stage_two(t - 1)

        @pl.when(is_end)
        def _():
            ra_copy(t).wait_send()
            if t < CHUNKS - AHEAD:
                ra_copy(t + AHEAD).start()
            if t >= LAG:
                xe_copy(t - LAG).wait_recv()
                publish(t - LAG)

    own_cols = pl.ds(pl.multiple_of(g * half, half), half)
    mate_cols = pl.ds(pl.multiple_of((1 - g) * half, half), half)

    def mr_copy(dest):
        span = pl.ds(pl.multiple_of(dest * own, own), own)
        return remote(
            t_ref.at[0, span, mate_cols], mr_ref.at[dest], mr_send.at[dest], mr_recv.at[dest], mate
        )

    def cr_copy(k, n):
        dest = lax.bitwise_xor(z, k)
        span = pl.ds(pl.multiple_of(dest * own + n * piece, piece), piece)
        return remote(
            t_ref.at[1, span, own_cols], cr_ref.at[z, pl.ds(n * piece, piece)],
            cr_send.at[k - 1, n], cr_recv.at[k - 1, n], (g, a, dest),
        )

    def cr_wait(k, n):
        src = lax.bitwise_xor(z, k)
        remote(
            t_ref.at[1, pl.ds(0, piece), own_cols], cr_ref.at[src, pl.ds(n * piece, piece)],
            cr_send.at[k - 1, n], cr_recv.at[k - 1, n], (g, a, src),
        ).wait_recv()

    def coulomb_part(k, d):
        dest = lax.bitwise_xor(z, k)
        step = 32

        def body(i, carry):
            row = pl.multiple_of(dest * own + i * step, step)
            span = pl.ds(row, step)
            total = t_ref[0, span, :].astype(jnp.float32) * d[0]
            for p in range(1, parts):
                total += t_ref[p, span, :].astype(jnp.float32) * d[p]
            total = total * mask_ref[row // BLK].astype(jnp.float32)
            t_ref[0, span, :] = total.astype(jnp.bfloat16)
            return carry

        lax.fori_loop(0, own // step, body, 0)
        mr_copy(dest).start()

    def coulomb_sum(k):
        dest = lax.bitwise_xor(z, k)
        mr_copy(dest).wait_recv()
        step = 64

        def body(i, carry):
            span = pl.ds(pl.multiple_of(dest * own + i * step, step), step)
            part = pl.ds(pl.multiple_of(i * step, step), step)
            both = t_ref[0, span, own_cols].astype(jnp.float32) + mr_ref[dest, part, :].astype(jnp.float32)
            if k:
                t_ref[1, span, own_cols] = both.astype(jnp.bfloat16)
            else:
                cr_ref[dest, part, :] = both.astype(jnp.bfloat16)
            return carry

        lax.fori_loop(0, own // step, body, 0)

    s_start(0)
    s_finish(0)
    s_start(1)
    slot(0)
    s_finish(1)
    s_start(2)
    slot(1)
    s_finish(2)
    s_start(3)
    for t in range(2, 7):
        slot(t)
    s_finish(3)
    dens_tile = s_ref[small - 8 :, :]
    d = []
    for p in range(parts):
        row = jnp.where(tile_rows == parts * g + p, dens_tile, 0.0)
        value = 2.0 * jnp.sum(jnp.sum(row, axis=1, keepdims=True), axis=0, keepdims=True)
        d.append(value.astype(jnp.bfloat16).astype(jnp.float32))
    order = (2, 3, 1, 0)
    for i in range(4):
        slot(7 + 2 * i)
        coulomb_part(order[i], d)
        slot(8 + 2 * i)
        if i:
            coulomb_sum(order[i - 1])
    slot(15)
    cross = [(k, n) for n in range(PIECES) for k in (2, 3)]

    def coulomb_start():
        for n in range(PIECES):
            cr_copy(1, n).start()
        for k, n in cross[:2]:
            cr_copy(k, n).start()

    @pl.when(is_end)
    def _():
        coulomb_start()

    slot(CHUNKS)

    @pl.when(is_mid)
    def _():
        coulomb_start()

    coulomb_sum(order[3])
    potentials()
    for t in range(CHUNKS + 1, CHUNKS + LAG):
        slot(t)

    def arrive(c, carry):
        for k in (1, 2, 3):
            pl_wait(c, k)

            @pl.when(for_mate(c))
            def _():
                xm_copy(lax.bitwise_xor(a, k), c).start()

        return carry

    def next_cross(q):
        cr_copy(*cross[q - 2]).wait_send()
        cr_copy(*cross[q]).start()

    seen = 0
    for q, until in ((2, 8), (3, 11), (4, 14), (5, CHUNKS)):
        next_cross(q)
        lax.fori_loop(seen, until, arrive, 0)
        seen = until
    next_cross(6)
    for i in range(per_own):
        xo_copy(i).wait_recv()
    dims = (((1,), (1,)), ((), ()))
    own_rows = pl.ds(pl.multiple_of(a * rows + z * own, own), own)

    def exchange(block, carry):
        def body(j, inside):
            for i in range(tile // chunk):
                xm_copy(block, j * (tile // chunk) + i).wait_recv()
            total = jnp.zeros((own, tile), jnp.float32)
            near = pl.ds(pl.multiple_of(block * rows + g * half + j * tile, tile), tile)
            far = pl.ds(pl.multiple_of(block * half + j * tile, tile), tile)
            for p in range(parts):
                total += lax.dot_general(
                    xa_ref[p, own_rows, :], xa_ref[p, near, :], dims, preferred_element_type=jnp.float32
                )
                total += lax.dot_general(
                    xo_ref[p], xm_ref[p, far, :], dims, preferred_element_type=jnp.float32
                )
            first = jnp.where(block == a, g * half + j * tile - z * own, -4 * rows)
            field_row = a * row_blocks + g * (half // BLK) + j * (tile // BLK)
            field = jnp.concatenate(
                [s_ref[pl.ds(field_row + i, 1), :] for i in range(tile // BLK)], axis=1
            )
            diagonal = lax.broadcasted_iota(jnp.int32, (own, tile), 0) == first + lax.broadcasted_iota(
                jnp.int32, (own, tile), 1
            )
            total = jnp.where(diagonal, field, 0.0) - 0.5 * total
            eb_ref[block, :, pl.ds(pl.multiple_of(j * tile, tile), tile)] = total.astype(jnp.bfloat16)
            return inside

        return lax.fori_loop(0, half // tile, body, carry)

    lax.fori_loop(0, 2, exchange, 0)
    next_cross(7)
    lax.fori_loop(2, 4, exchange, 0)

    def out_cols(block, core):
        return pl.ds(pl.multiple_of(block * cols + core * half, half), half)

    def piece_at(n):
        return pl.ds(pl.multiple_of(n * piece, piece), piece)

    def om_copy(block, n, core):
        return remote(
            eb_ref.at[block, piece_at(n)], out_ref.at[piece_at(n), out_cols(block, core)],
            om_send.at[block, n], om_recv.at[block, n], mate,
        )

    def ol_copy(block, n):
        return pltpu.make_async_copy(
            eb_ref.at[block, piece_at(n)], out_ref.at[piece_at(n), out_cols(block, g)], ol_sem.at[block, n]
        )

    def finish_piece(block, n):
        step = 64

        def body(i, carry):
            part = pl.ds(pl.multiple_of(n * piece + i * step, step), step)
            both = eb_ref[block, part, :].astype(jnp.float32) + cr_ref[block, part, :].astype(jnp.float32)
            eb_ref[block, part, :] = both.astype(jnp.bfloat16)
            return carry

        lax.fori_loop(0, piece // step, body, 0)
        om_copy(block, n, g).start()
        ol_copy(block, n).start()

    def finish_near(n, carry):
        finish_piece(z, n)
        cr_wait(1, n)
        finish_piece(lax.bitwise_xor(z, 1), n)
        return carry

    lax.fori_loop(0, PIECES, finish_near, 0)

    def finish_cross(n, carry):
        for k in (2, 3):
            cr_wait(k, n)
            finish_piece(lax.bitwise_xor(z, k), n)
        return carry

    lax.fori_loop(0, PIECES, finish_cross, 0)

    for k, n in cross[-2:] + [(1, n) for n in range(PIECES)]:
        cr_copy(k, n).wait_send()

    def drain_out(block, carry):
        for n in range(PIECES):
            om_copy(block, n, 1 - g).wait()
            ol_copy(block, n).wait()
        mr_copy(block).wait_send()
        return carry

    lax.fori_loop(0, 4, drain_out, 0)

    @pl.when(rel == 0)
    def _():
        for i in range(2, 4):
            quarter_copy(c_ref, first, i, mate).wait_send()

    @pl.when(rel != 0)
    def _():
        for i in range(2):
            quarter_copy(cw_ref, first, i, mate).wait_send()

    @pl.when((rel == 1) | (rel == 2))
    def _():
        quarter_copy(cw_ref, first, 2, mate).wait_send()

    def drain(c, carry):
        @pl.when(is_mid)
        def _():
            rb_copy(c).wait_send()
            xe_copy(c).wait_send()

        for k in (1, 2, 3):
            pl_copy(c, k).wait_send()

        @pl.when(for_mate(c))
        def _():
            for block in range(4):
                xm_copy(block, c).wait_send()

        return carry

    lax.fori_loop(0, CHUNKS, drain, 0)
    for i in range(per_own):
        xo_copy(i).wait_send()


def grid_call(fitted, block_mask, own_c, nuclear, centres, positions, charges, neighbours):
    parts, rows, cols = fitted.shape
    nocc = own_c.shape[1]
    own, half = rows // 4, cols // 2
    block_total = block_mask.shape[1]
    small = (2 * block_total + 8, BLK)
    bf16, f32 = jnp.bfloat16, jnp.float32
    vmem = pl.BlockSpec(memory_space=pltpu.VMEM)
    hbm = pl.BlockSpec(memory_space=pl.ANY)
    dma = pltpu.SemaphoreType.DMA
    return pl.pallas_call(
        grid_kernel,
        in_specs=[hbm] + [vmem] * 7,
        out_specs=[hbm, vmem],
        out_shape=[
            jax.ShapeDtypeStruct((own, 4 * cols), bf16),
            jax.ShapeDtypeStruct((1, positions.shape[1]), f32),
        ],
        scratch_shapes=[
            pltpu.VMEM((parts, rows, cols), bf16),
            pltpu.VMEM((rows // BLK, 1, cols), bf16),
            pltpu.VMEM((neighbours.shape[1], BLK, positions.shape[1]), f32),
            pltpu.VMEM((cols, nocc), bf16),
            pltpu.VMEM((parts, rows, nocc), bf16),
            pltpu.VMEM((parts, rows, nocc), bf16),
            pltpu.VMEM((parts, rows, nocc), bf16),
            pltpu.VMEM((parts, 4 * rows, nocc), bf16),
            pltpu.VMEM((parts, 2 * rows, nocc), bf16),
            pltpu.VMEM((parts, own, nocc), bf16),
            pltpu.VMEM((4, own, half), bf16),
            pltpu.VMEM((4, own, half), bf16),
            pltpu.VMEM((4, own, half), bf16),
            pltpu.VMEM(small, f32),
            pltpu.VMEM((6,) + small, f32),
            pltpu.VMEM((parts, 8, nocc), f32),
            dma((STEPS,)),
            dma((4,)), dma((4,)),
            dma((CHUNKS,)), dma((CHUNKS,)),
            dma((CHUNKS,)), dma((CHUNKS,)),
            dma((CHUNKS,)), dma((CHUNKS,)),
            dma((3, CHUNKS)), dma((3, CHUNKS)),
            dma((2 * CHUNKS,)), dma((2 * CHUNKS,)),
            dma((own * CHUNKS // rows,)), dma((own * CHUNKS // rows,)),
            dma((6,)), dma((6,)),
            dma((4,)), dma((4,)),
            dma((3, PIECES)), dma((3, PIECES)),
            dma((4, PIECES)), dma((4, PIECES)),
            dma((4, PIECES)),
        ],
        compiler_params=pltpu.CompilerParams(
            collective_id=0, has_side_effects=True, vmem_limit_bytes=GRID_VMEM
        ),
        cost_estimate=pl.CostEstimate(
            flops=2 * parts * rows * cols * nocc + 8 * parts * own * 2 * cols * nocc,
            bytes_accessed=2 * parts * rows * cols + 8 * own * cols,
            transcendentals=0,
        ),
        name="grid",
    )(
        fitted, block_mask, own_c, nuclear.reshape(block_total, BLK), centres, positions,
        charges.reshape(1, -1), neighbours,
    )


def finish_kernel(in_ref, out_ref):
    out_ref[...] = in_ref[...].astype(jnp.float32)


def finish_call(fock16):
    rows, cols = fock16.shape
    step = 64
    spec = pl.BlockSpec((step, cols), lambda i: (i, 0))
    return pl.pallas_call(
        finish_kernel,
        grid=(rows // step,),
        in_specs=[spec],
        out_specs=spec,
        out_shape=jax.ShapeDtypeStruct((rows, cols), jnp.float32),
        compiler_params=pltpu.CompilerParams(vmem_limit_bytes=VMEM_LIMIT),
        cost_estimate=pl.CostEstimate(
            flops=rows * cols, bytes_accessed=6 * rows * cols, transcendentals=0
        ),
        name="finish",
    )(fock16)


def per_device_grid(
    fitted_tensor, block_mask, orbitals, nuclear, centres, mm_positions, mm_charges, neighbours
):
    fock16, potential = grid_call(
        fitted_tensor, block_mask, orbitals, nuclear, centres, mm_positions, mm_charges, neighbours
    )
    return (finish_call(fock16), potential.reshape(-1))


def grid_fits(mesh, fitted_tensor, orbitals):
    shape = mesh.shape
    parts = fitted_tensor.shape[0] // shape["grp"]
    rows = fitted_tensor.shape[1] // shape["aux"]
    cols = fitted_tensor.shape[2] // shape["orb"]
    return (
        shape["grp"] == 2
        and shape["aux"] == 4
        and shape["orb"] == 4
        and parts == 2
        and rows == cols
        and rows % (CHUNKS * BLK) == 0
        and rows % (2 * STEPS * BLK) == 0
        and orbitals.shape[1] % BLK == 0
        and 7 * rows * cols + 41 * rows * orbitals.shape[1] <= 52 * 2**20
    )


def solution(mesh):
    in_specs = (
        P("grp", "aux", "orb"),
        P("grp", None, None),
        P("aux", None),
        P(),
        P(),
        P(None, ("grp", "aux", "orb")),
        P(("grp", "aux", "orb")),
        P(("grp", "aux", "orb"), None),
    )
    out_specs = (P(("aux", "orb"), None), P(("grp", "aux", "orb")))
    def build(body):
        return jax.shard_map(
            body, mesh=mesh, in_specs=in_specs, out_specs=out_specs, check_vma=False
        )

    def run(fitted_tensor, block_mask, orbitals, *rest):
        body = per_device_grid if grid_fits(mesh, fitted_tensor, orbitals) else per_device
        return build(body)(fitted_tensor, block_mask, orbitals, *rest)

    return run
```

```python
import functools

import jax
import jax.numpy as jnp
from jax import lax
from jax.experimental import pallas as pl
from jax.experimental.pallas import tpu as pltpu
from jax.sharding import PartitionSpec as P

BLK = 128
VMEM_LIMIT = 48 * 1024 * 1024

softening = 1.0


def near_kernel(picker, centre_blocks, atom_xyz):
    near_xyz = jnp.einsum("kb,cbj->ckj", picker, centre_blocks, precision=lax.Precision.HIGHEST)
    near_xyz = near_xyz.reshape(3, picker.shape[0] * centre_blocks.shape[2])
    offsets = near_xyz[:, :, None] - atom_xyz[:, None, :]
    return lax.rsqrt(jnp.sum(offsets * offsets, axis=0) + softening)


def products_kernel(t_ref, mask_ref, win_ref, c_ref, x_ref, dens_ref):
    parts, rows, cols = t_ref.shape
    row_mask = mask_ref[0]

    @pl.when(pl.program_id(0) == 0)
    def _():
        dens_ref[...] = jnp.zeros_like(dens_ref)

    own = c_ref[...].astype(jnp.float32)
    for p in range(parts):
        prod = jnp.dot(t_ref[p] * row_mask, win_ref[...], preferred_element_type=jnp.float32)
        x_ref[p] = prod.astype(x_ref.dtype)
        dens_ref[p] += jnp.sum((prod * own).reshape(rows // 8, 8, prod.shape[1]), axis=0)


def products_call(fitted, mask_rows, window_c, own_c):
    parts, rows, cols = fitted.shape
    nocc = window_c.shape[1]
    return pl.pallas_call(
        products_kernel,
        grid=(rows // BLK,),
        in_specs=[
            pl.BlockSpec((parts, BLK, cols), lambda i: (0, i, 0)),
            pl.BlockSpec((1, 1, cols), lambda i: (i, 0, 0)),
            pl.BlockSpec((cols, nocc), lambda i: (0, 0)),
            pl.BlockSpec((BLK, nocc), lambda i: (i, 0)),
        ],
        out_specs=[
            pl.BlockSpec((parts, BLK, nocc), lambda i: (0, i, 0)),
            pl.BlockSpec((parts, 8, nocc), lambda i: (0, 0, 0)),
        ],
        out_shape=[
            jax.ShapeDtypeStruct((parts, rows, nocc), jnp.bfloat16),
            jax.ShapeDtypeStruct((parts, 8, nocc), jnp.float32),
        ],
        compiler_params=pltpu.CompilerParams(vmem_limit_bytes=VMEM_LIMIT),
        cost_estimate=pl.CostEstimate(
            flops=2 * parts * rows * cols * nocc,
            bytes_accessed=2 * parts * rows * (cols + nocc),
            transcendentals=0,
        ),
        name="products",
    )(fitted, mask_rows, window_c, own_c)


def coulomb_kernel(place_ref, dens_ref, ta_ref, ma_ref, tk_ref, mk_ref, away_ref, kept_ref):
    for t_ref, mask_ref, out_ref in ((ta_ref, ma_ref, away_ref), (tk_ref, mk_ref, kept_ref)):
        total = t_ref[0].astype(jnp.float32) * dens_ref[0]
        for p in range(1, t_ref.shape[0]):
            total += t_ref[p].astype(jnp.float32) * dens_ref[p]
        out_ref[...] = (total * mask_ref[0].astype(jnp.float32)).astype(out_ref.dtype)


def coulomb_call(place, densities, fitted, mask_rows, half):
    parts, rows, cols = fitted.shape
    tile = min(BLK, half)
    steps = half // tile

    def away_tile(i, place_ref):
        return (place_ref[1] * 2 + 1 - place_ref[0]) * steps + i

    def kept_tile(i, place_ref):
        return (place_ref[1] * 2 + place_ref[0]) * steps + i

    def tensor_spec(which):
        return pl.BlockSpec((parts, tile, cols), lambda i, place_ref, d: (0, which(i, place_ref), 0))

    def mask_spec(which):
        return pl.BlockSpec(
            (1, 1, cols), lambda i, place_ref, d: (which(i, place_ref) * tile // BLK, 0, 0)
        )

    return pl.pallas_call(
        coulomb_kernel,
        grid_spec=pltpu.PrefetchScalarGridSpec(
            num_scalar_prefetch=2,
            grid=(steps,),
            in_specs=[
                tensor_spec(away_tile),
                mask_spec(away_tile),
                tensor_spec(kept_tile),
                mask_spec(kept_tile),
            ],
            out_specs=[pl.BlockSpec((tile, cols), lambda i, place_ref, d: (i, 0))] * 2,
        ),
        out_shape=[jax.ShapeDtypeStruct((half, cols), jnp.bfloat16)] * 2,
        compiler_params=pltpu.CompilerParams(vmem_limit_bytes=VMEM_LIMIT),
        cost_estimate=pl.CostEstimate(
            flops=4 * parts * half * cols,
            bytes_accessed=4 * half * cols * (parts + 1),
            transcendentals=0,
        ),
        name="coulomb",
    )(place, densities, fitted, mask_rows, fitted, mask_rows)


def fock_kernel(shifts, place_ref, own_ref, mate_ref, all_ref, mate_all_ref, field_ref, *refs):
    mine, theirs, out_ref = refs[:shifts], refs[shifts : 2 * shifts], refs[2 * shifts]
    parts = own_ref.shape[0]
    rows, cols = out_ref.shape
    half = rows // 2
    per_src = mine[0].shape[1] // cols
    dims = (((1,), (1,)), ((), ()))
    grp_id, row0, orb_id = place_ref[0], place_ref[1], place_ref[2]

    def slab(a, b):
        total = lax.dot_general(a[0], b[0], dims, preferred_element_type=jnp.float32)
        for p in range(1, parts):
            total += lax.dot_general(a[p], b[p], dims, preferred_element_type=jnp.float32)
        return total

    out_ref[...] = -0.5 * (slab(own_ref, all_ref) + slab(mate_ref, mate_all_ref))

    step = pl.program_id(0)
    shift = lax.rem(orb_id - step // per_src + shifts, shifts)
    col_in = pl.multiple_of(lax.rem(step, per_src) * cols, cols)
    own_row = pl.multiple_of(grp_id * half, half)
    mate_row = pl.multiple_of((1 - grp_id) * half, half)
    for k in range(shifts):

        @pl.when(shift == k)
        def _():
            out_ref[pl.ds(own_row, half), :] += mine[k][:, pl.ds(col_in, cols)].astype(jnp.float32)
            out_ref[pl.ds(mate_row, half), :] += theirs[k][:, pl.ds(col_in, cols)].astype(jnp.float32)

    col0 = step * cols

    @pl.when((row0 < col0 + cols) & (row0 + rows > col0))
    def _():
        row_ids = row0 + lax.broadcasted_iota(jnp.int32, (rows, cols), 0)
        col_ids = col0 + lax.broadcasted_iota(jnp.int32, (rows, cols), 1)
        out_ref[...] += jnp.where(row_ids == col_ids, field_ref[...], jnp.float32(0.0))


def fock_call(place, x_own, x_mate, x_all, x_mate_all, field_col, mine, theirs):
    parts, rows, nocc = x_own.shape
    total = x_all.shape[1]
    half, per_src = mine[0].shape
    cols = min(1024, per_src)
    own_spec = pl.BlockSpec((parts, rows, nocc), lambda j: (0, 0, 0))
    all_spec = pl.BlockSpec((parts, cols, nocc), lambda j: (0, j, 0))
    return pl.pallas_call(
        functools.partial(fock_kernel, len(mine)),
        grid=(total // cols,),
        in_specs=[
            pl.BlockSpec(memory_space=pltpu.SMEM),
            own_spec,
            own_spec,
            all_spec,
            all_spec,
            pl.BlockSpec((rows, 1), lambda j: (0, 0)),
        ]
        + [pl.BlockSpec((half, per_src), lambda j: (0, 0))] * (2 * len(mine)),
        out_specs=pl.BlockSpec((rows, cols), lambda j: (0, j)),
        out_shape=jax.ShapeDtypeStruct((rows, total), jnp.float32),
        compiler_params=pltpu.CompilerParams(vmem_limit_bytes=VMEM_LIMIT),
        cost_estimate=pl.CostEstimate(
            flops=4 * parts * rows * total * nocc,
            bytes_accessed=4 * parts * total * nocc + 4 * rows * total + 2 * rows * total,
            transcendentals=0,
        ),
        name="fock",
    )(place, x_own, x_mate, x_all, x_mate_all, field_col, *mine, *theirs)


def swap(value):
    return lax.ppermute(value, "grp", [(0, 1), (1, 0)])


def per_device(
    fitted_tensor, block_mask, orbitals, nuclear, centres, mm_positions, mm_charges, neighbours
):
    parts, row_span, col_span = fitted_tensor.shape
    nocc = orbitals.shape[1]
    orb_count = lax.axis_size("orb")
    aux_count = lax.axis_size("aux")
    grp_count = lax.axis_size("grp")
    grp_id = lax.axis_index("grp")
    aux_id = lax.axis_index("aux")
    orb_id = lax.axis_index("orb")
    own_span = row_span // orb_count
    half = own_span // 2
    block_total = block_mask.shape[1]
    row_start = aux_id * row_span
    col_start = orb_id * col_span

    if aux_count == orb_count:
        perm = [
            (a * orb_count + o, o * orb_count + a)
            for a in range(aux_count)
            for o in range(orb_count)
        ]
        c_half = lax.dynamic_slice_in_dim(orbitals, grp_id * (row_span // 2), row_span // 2, 0)
        c_half = lax.ppermute(c_half, ("aux", "orb"), perm)
        c_mate = swap(c_half)
        window_c = jnp.where(
            grp_id == 0, jnp.stack([c_half, c_mate]), jnp.stack([c_mate, c_half])
        ).reshape(col_span, nocc)
    else:
        whole_c = lax.all_gather(orbitals, "aux", axis=0, tiled=True)
        window_c = lax.dynamic_slice_in_dim(whole_c, col_start, col_span, 0)

    bits = lax.dynamic_slice(
        block_mask[0],
        (row_start // BLK, col_start // BLK),
        (row_span // BLK, col_span // BLK),
    ).astype(jnp.bfloat16)
    mask_rows = jnp.repeat(bits, BLK, axis=1)[:, None, :]

    own_float = orbitals.astype(jnp.float32)
    own_population = 2.0 * jnp.sum(own_float * own_float, axis=1)
    population = lax.all_gather(own_population, "aux", axis=0, tiled=True)
    centre_blocks = centres.reshape(3, block_total, BLK)
    picker = (neighbours[0][:, None] == jnp.arange(block_total, dtype=jnp.int32)[None, :]).astype(
        jnp.float32
    )
    kernel = near_kernel(picker, centre_blocks, mm_positions)
    contrib = jnp.dot(kernel, mm_charges, precision=lax.Precision.HIGHEST).reshape(
        picker.shape[0], BLK
    )
    field_part = jnp.dot(picker.T, contrib, precision=lax.Precision.HIGHEST)

    window_c, population = lax.optimization_barrier((window_c, population))
    qm_charge = nuclear - population
    charge_blocks = qm_charge.reshape(block_total, BLK)
    near_q = jnp.dot(picker, charge_blocks, precision=lax.Precision.HIGHEST).reshape(-1)
    mm_potential = jnp.dot(near_q, kernel, precision=lax.Precision.HIGHEST)

    x_part, dens_lanes = products_call(fitted_tensor, mask_rows, window_c, orbitals)
    dens_part = 2.0 * jnp.sum(dens_lanes, axis=(1, 2))
    dens_slots = jnp.zeros((grp_count, BLK), jnp.float32)
    dens_slots = lax.dynamic_update_slice(dens_slots, dens_part[None, :], (grp_id, 0))
    sums = lax.psum(jnp.concatenate([field_part, dens_slots], axis=0), ("grp", "aux", "orb"))

    x_blocks = x_part.reshape(parts, orb_count, own_span, nocc)
    targets = [lax.rem(orb_id + k, orb_count) for k in range(orb_count)]
    moves = [[(s, (s + k) % orb_count) for s in range(orb_count)] for k in range(orb_count)]
    arrived = []
    for k in range(1, orb_count):
        block = lax.dynamic_index_in_dim(x_blocks, targets[k], 1, keepdims=False)
        arrived.append(lax.ppermute(block, "orb", moves[k]))
    sums, *arrived = lax.optimization_barrier((sums, *arrived))
    field_vec = sums[:block_total].reshape(-1)
    densities = lax.dynamic_slice(sums, (block_total + grp_id, 0), (1, parts))[0]
    x_sum = lax.dynamic_index_in_dim(x_blocks, orb_id, 1, keepdims=False).astype(jnp.float32)
    for block in arrived:
        x_sum += block.astype(jnp.float32)
    x_own = x_sum.astype(jnp.bfloat16)
    x_mate = swap(x_own)
    x_all = lax.all_gather(x_own, ("aux", "orb"), axis=1, tiled=True)

    mine = [None] * orb_count
    for k in list(range(1, orb_count)) + [0]:
        at = jnp.stack([grp_id, targets[k]]).astype(jnp.int32)
        away, kept = coulomb_call(at, densities, fitted_tensor, mask_rows, half)
        both = (kept.astype(jnp.float32) + swap(away).astype(jnp.float32)).astype(jnp.bfloat16)
        mine[k] = lax.ppermute(both, "orb", moves[k]) if k else both
    x_all, *mine = lax.optimization_barrier((x_all, *mine))
    theirs = [swap(block) for block in mine]
    x_mate_all = swap(x_all)

    own_first = row_start + orb_id * own_span
    field_col = lax.dynamic_slice_in_dim(field_vec, own_first, own_span, 0)[:, None]
    place = jnp.stack([grp_id, own_first, orb_id]).astype(jnp.int32)
    fock = fock_call(place, x_own, x_mate, x_all, x_mate_all, field_col, mine, theirs)
    return (fock, mm_potential)


MESH = pl.DeviceIdType.MESH
CHUNKS = 16
STEPS = 8
AHEAD = 2
LAG = 4
PIECES = 4
FLIGHT = 4
GRID_VMEM = 58 * 1024 * 1024


def grid_kernel(
    t_hbm, bits_ref, c_ref, nuclear_ref, centres_ref, place_ref, charge_ref, near_ref,
    out_ref, potential_ref,
    t_ref, mask_ref, kern_ref, cw_ref, xp_ref, ra_ref, rb_ref, xa_ref, xm_ref, xo_ref, mr_ref, cr_ref, eb_ref,
    s_ref, sr_ref, dens_ref,
    t_sem, c_send, c_recv, ra_send, ra_recv, rb_send, rb_recv, xe_send, xe_recv,
    pl_send, pl_recv, xm_send, xm_recv, xo_send, xo_recv, s_send, s_recv,
    mr_send, mr_recv, cr_send, cr_recv, om_send, om_recv, ol_sem,
):
    parts, rows, cols = t_ref.shape
    nocc = c_ref.shape[1]
    chunk = rows // CHUNKS
    load = rows // STEPS
    tile = 2 * BLK
    own = rows // 4
    piece = own // PIECES
    per_own = own // chunk
    half = cols // 2
    quarter = cols // 4
    per = CHUNKS // 2
    g, a, z = lax.axis_index("grp"), lax.axis_index("aux"), lax.axis_index("orb")
    mate = (1 - g, a, z)
    is_mid = (z == 1) | (z == 2)
    is_end = (z == 0) | (z == 3)
    inner = jnp.where(z == 0, 1, 2)
    outer = jnp.where(z == 1, 0, 3)
    rel = lax.bitwise_xor(a, z)

    def plane(k):
        return (g, lax.bitwise_xor(a, k), z)

    def remote(src, dst, send, recv, device):
        return pltpu.make_async_remote_copy(
            src_ref=src, dst_ref=dst, send_sem=send, recv_sem=recv,
            device_id=device, device_id_type=MESH,
        )

    def t_copy(c):
        span = pl.ds(c * load, load)
        return pltpu.make_async_copy(t_hbm.at[:, span], t_ref.at[:, span], t_sem.at[c])

    for c in range(STEPS):
        t_copy(c).start()

    barrier = pltpu.get_barrier_semaphore()
    for peer in (
        mate, plane(1), plane(2), plane(3),
        (g, a, lax.rem(z + 1, 4)), (g, a, lax.rem(z + 2, 4)), (g, a, lax.rem(z + 3, 4)),
    ):
        pl.semaphore_signal(barrier, inc=1, device_id=peer, device_id_type=MESH)
    pl.semaphore_wait(barrier, 7)

    def quarter_copy(src_ref, q, slot, device):
        span = pl.ds(pl.multiple_of(q * quarter, quarter), quarter)
        return remote(src_ref.at[span], cw_ref.at[span], c_send.at[slot], c_recv.at[q], device)

    first, second = 2 * g, 2 * g + 1

    @pl.when(rel == 0)
    def _():
        quarter_copy(c_ref, first, 0, plane(1)).start()
        quarter_copy(c_ref, second, 1, plane(2)).start()
        cw_ref[...] = c_ref[...]

    row_blocks, block_total = rows // BLK, bits_ref.shape[1]
    picked = lax.broadcasted_iota(jnp.int32, (block_total, cols), 1) // BLK + z * (cols // BLK)
    picked = (lax.broadcasted_iota(jnp.int32, (block_total, cols), 0) == picked).astype(jnp.float32)
    bits = bits_ref[0, pl.ds(pl.multiple_of(a * row_blocks, row_blocks), row_blocks), :].astype(jnp.float32)
    wide = jnp.dot(
        bits.astype(jnp.bfloat16), picked.astype(jnp.bfloat16), preferred_element_type=jnp.float32
    )
    for j in range(row_blocks):
        mask_ref[j] = wide[j : j + 1, :].astype(jnp.bfloat16)

    eye = lax.broadcasted_iota(jnp.int32, (BLK, BLK), 0) == lax.broadcasted_iota(jnp.int32, (BLK, BLK), 1)

    def to_row(column):
        return jnp.sum(jnp.where(eye, column, 0.0), axis=0, keepdims=True)

    def to_column(row):
        return jnp.sum(jnp.where(eye, row, 0.0), axis=1, keepdims=True)

    @pl.when(rel == 0)
    def _():
        quarter_copy(c_ref, first, 0, plane(1)).wait_send()
        quarter_copy(c_ref, second, 2, plane(1)).start()
        quarter_copy(c_ref, second, 1, plane(2)).wait_send()
        quarter_copy(c_ref, first, 3, plane(2)).start()

    s_ref[...] = jnp.zeros_like(s_ref)
    share = jnp.where((g == 0) & (z == 0), 2.0, 0.0)

    def population_step(j, carry):
        block = c_ref[pl.ds(pl.multiple_of(j * BLK, BLK), BLK), :].astype(jnp.float32)
        row = to_row(jnp.sum(block * block, axis=1, keepdims=True))
        s_ref[pl.ds(block_total + a * row_blocks + j, 1), :] = share * row
        return carry

    lax.fori_loop(0, row_blocks, population_step, 0)

    near_count = near_ref.shape[1]
    block_ids = lax.broadcasted_iota(jnp.int32, (block_total, BLK), 0)
    for k in range(near_count):
        near_id = near_ref[:, k : k + 1]
        near_xyz = jnp.zeros((3, BLK), jnp.float32)
        for b in range(block_total):
            near_xyz = near_xyz + jnp.where(near_id == b, centres_ref[:, b * BLK : (b + 1) * BLK], 0.0)
        squares = None
        for axis in range(3):
            offset = to_column(near_xyz[axis : axis + 1, :]) - place_ref[axis : axis + 1, :]
            squares = offset * offset if squares is None else squares + offset * offset
        kern = lax.rsqrt(squares + softening)
        kern_ref[k] = kern
        contrib = to_row(jnp.sum(kern * charge_ref[...], axis=1, keepdims=True))
        s_ref[:block_total, :] += jnp.where(block_ids == near_id, contrib, 0.0)

    def potentials():
        charges = nuclear_ref[...] - s_ref[block_total : 2 * block_total, :]
        total = jnp.zeros(potential_ref.shape, jnp.float32)
        for k in range(near_count):
            near_q = jnp.sum(
                jnp.where(block_ids == near_ref[:, k : k + 1], charges, 0.0), axis=0, keepdims=True
            )
            total = total + jnp.sum(kern_ref[k] * to_column(near_q), axis=0, keepdims=True)
        potential_ref[...] = total

    @pl.when(rel != 0)
    def _():
        for rank in range(2):
            q = jnp.where(rel == 2, 2 * g + 1 - rank, 2 * g + rank)
            quarter_copy(cw_ref, q, 0, mate).wait_recv()
            if rank == 0:

                @pl.when(rel == 1)
                def _():
                    quarter_copy(cw_ref, q, 2, plane(2)).start()

                @pl.when(rel == 2)
                def _():
                    quarter_copy(cw_ref, q, 2, plane(1)).start()

            quarter_copy(cw_ref, q, rank, mate).start()
        for rank in range(2):
            quarter_copy(cw_ref, 2 * (1 - g) + rank, 0, mate).wait_recv()

    def x_span(c):
        return pl.ds(pl.multiple_of(c * chunk, chunk), chunk)

    def ra_copy(c):
        return remote(
            xp_ref.at[:, x_span(c)], ra_ref.at[:, x_span(c)], ra_send.at[c], ra_recv.at[c], (g, a, inner)
        )

    dens_ref[...] = jnp.zeros_like(dens_ref)

    def products_step(c, carry):
        t_copy(c).wait()
        span = pl.ds(pl.multiple_of(c * load, load), load)
        c_rows = c_ref[span, :].astype(jnp.float32)
        blocks = load // BLK
        for p in range(parts):
            masked = jnp.concatenate(
                [
                    t_ref[p, pl.ds(pl.multiple_of(c * load + j * BLK, BLK), BLK), :]
                    * mask_ref[c * blocks + j]
                    for j in range(blocks)
                ],
                axis=0,
            )
            prod = jnp.dot(masked, cw_ref[...], preferred_element_type=jnp.float32)
            xp_ref[p, span, :] = prod.astype(jnp.bfloat16)
            dens_ref[p] += jnp.sum((prod * c_rows).reshape(load // 8, 8, nocc), axis=0)

        for first_chunk in range(AHEAD):

            @pl.when(is_end & (c == 3 * first_chunk))
            def _():
                ra_copy(first_chunk).start()

        return carry

    lax.fori_loop(0, STEPS, products_step, 0)

    small = s_ref.shape[0]
    tile_rows = lax.broadcasted_iota(jnp.int32, (8, 128), 0)
    dens_rows = jnp.zeros((8, 128), jnp.float32)
    for p in range(parts):
        lanes = jnp.sum(dens_ref[p], axis=0, keepdims=True)
        folded = lanes[:, :128]
        for j in range(1, nocc // 128):
            folded = folded + lanes[:, j * 128 : (j + 1) * 128]
        dens_rows = dens_rows + jnp.where(tile_rows == parts * g + p, folded, 0.0)
    s_ref[small - 8 :, :] = dens_rows

    def s_copy(i):
        device = (mate, plane(1), plane(2))[i] if i < 3 else (g, a, lax.rem(z + i - 2, 4))
        return remote(s_ref, sr_ref.at[i], s_send.at[i], s_recv.at[i], device)

    def s_start(r):
        for i in ((0,), (1,), (2,), (3, 4, 5))[r]:
            s_copy(i).start()

    def s_finish(r):
        batch = ((0,), (1,), (2,), (3, 4, 5))[r]
        for i in batch:
            s_copy(i).wait()
        for i in batch:
            s_ref[...] += sr_ref[i]

    def rb_copy(c):
        return remote(
            xp_ref.at[:, x_span(c)], rb_ref.at[:, x_span(c)], rb_send.at[c], rb_recv.at[c], (g, a, 3 - z)
        )

    def xa_at(block, c):
        return xa_ref.at[:, pl.ds(pl.multiple_of(block * rows + c * chunk, chunk), chunk)]

    def xe_copy(c):
        return remote(xa_at(a, c), xa_at(a, c), xe_send.at[c], xe_recv.at[c], (g, a, outer))

    def pl_copy(c, k):
        return remote(
            xa_at(a, c), xa_at(a, c), pl_send.at[k - 1, c], pl_recv.at[k - 1, c], plane(k)
        )

    def pl_wait(c, k):
        block = lax.bitwise_xor(a, k)
        remote(
            xa_at(block, c), xa_at(block, c), pl_send.at[k - 1, c], pl_recv.at[k - 1, c], plane(k)
        ).wait_recv()

    def xm_copy(block, c):
        i = block * per + lax.rem(c, per)
        dst = xm_ref.at[:, pl.ds(pl.multiple_of(i * chunk, chunk), chunk)]
        return remote(xa_at(block, c), dst, xm_send.at[i], xm_recv.at[i], mate)

    def xo_copy(c):
        i = lax.rem(c, per_own)
        dst = xo_ref.at[:, pl.ds(pl.multiple_of(i * chunk, chunk), chunk)]
        return remote(xa_at(a, c), dst, xo_send.at[i], xo_recv.at[i], mate)

    def for_mate(c):
        return c // per == 1 - g

    def publish(c):
        for k in (1, 2, 3):
            pl_copy(c, k).start()

        @pl.when(for_mate(c))
        def _():
            xm_copy(a, c).start()

        @pl.when(z == c // per_own)
        def _():
            xo_copy(c).start()

    def stage_one(c):
        ra_copy(c).wait_recv()
        for p in range(parts):
            both = xp_ref[p, x_span(c), :].astype(jnp.float32) + ra_ref[p, x_span(c), :].astype(jnp.float32)
            xp_ref[p, x_span(c), :] = both.astype(jnp.bfloat16)
        rb_copy(c).start()

    def stage_two(c):
        rb_copy(c).wait_recv()
        for p in range(parts):
            both = xp_ref[p, x_span(c), :].astype(jnp.float32) + rb_ref[p, x_span(c), :].astype(jnp.float32)
            xa_ref[p, pl.ds(pl.multiple_of(a * rows + c * chunk, chunk), chunk), :] = both.astype(jnp.bfloat16)
        xe_copy(c).start()
        publish(c)

    def late_slot(t):
        if t == CHUNKS:

            @pl.when(is_mid)
            def _():
                stage_two(t - 1)

        @pl.when(is_end)
        def _():
            xe_copy(t - LAG).wait_recv()
            publish(t - LAG)

    def slot(t):
        if t >= CHUNKS:
            late_slot(t)
            return

        @pl.when(is_mid)
        def _():
            stage_one(t)
            if t >= 1:
                stage_two(t - 1)

        @pl.when(is_end)
        def _():
            ra_copy(t).wait_send()
            if t < CHUNKS - AHEAD:
                ra_copy(t + AHEAD).start()
            if t >= LAG:
                xe_copy(t - LAG).wait_recv()
                publish(t - LAG)

    own_cols = pl.ds(pl.multiple_of(g * half, half), half)
    mate_cols = pl.ds(pl.multiple_of((1 - g) * half, half), half)

    def mr_copy(dest):
        span = pl.ds(pl.multiple_of(dest * own, own), own)
        return remote(
            t_ref.at[0, span, mate_cols], mr_ref.at[dest], mr_send.at[dest], mr_recv.at[dest], mate
        )

    def cr_copy(k, n):
        dest = lax.bitwise_xor(z, k)
        span = pl.ds(pl.multiple_of(dest * own + n * piece, piece), piece)
        return remote(
            t_ref.at[1, span, own_cols], cr_ref.at[z, pl.ds(n * piece, piece)],
            cr_send.at[k - 1, n], cr_recv.at[k - 1, n], (g, a, dest),
        )

    def cr_wait(k, n):
        src = lax.bitwise_xor(z, k)
        remote(
            t_ref.at[1, pl.ds(0, piece), own_cols], cr_ref.at[src, pl.ds(n * piece, piece)],
            cr_send.at[k - 1, n], cr_recv.at[k - 1, n], (g, a, src),
        ).wait_recv()

    def coulomb_part(k, d):
        dest = lax.bitwise_xor(z, k)
        step = 32

        def body(i, carry):
            row = pl.multiple_of(dest * own + i * step, step)
            span = pl.ds(row, step)
            total = t_ref[0, span, :].astype(jnp.float32) * d[0]
            for p in range(1, parts):
                total += t_ref[p, span, :].astype(jnp.float32) * d[p]
            total = total * mask_ref[row // BLK].astype(jnp.float32)
            t_ref[0, span, :] = total.astype(jnp.bfloat16)
            return carry

        lax.fori_loop(0, own // step, body, 0)
        mr_copy(dest).start()

    def coulomb_sum(k):
        dest = lax.bitwise_xor(z, k)
        mr_copy(dest).wait_recv()
        step = 64

        def body(i, carry):
            span = pl.ds(pl.multiple_of(dest * own + i * step, step), step)
            part = pl.ds(pl.multiple_of(i * step, step), step)
            both = t_ref[0, span, own_cols].astype(jnp.float32) + mr_ref[dest, part, :].astype(jnp.float32)
            if k:
                t_ref[1, span, own_cols] = both.astype(jnp.bfloat16)
            else:
                cr_ref[dest, part, :] = both.astype(jnp.bfloat16)
            return carry

        lax.fori_loop(0, own // step, body, 0)

    s_start(0)
    s_finish(0)
    s_start(1)
    slot(0)
    s_finish(1)
    s_start(2)
    slot(1)
    s_finish(2)
    s_start(3)
    for t in range(2, 5):
        slot(t)
    s_finish(3)
    dens_tile = s_ref[small - 8 :, :]
    d = []
    for p in range(parts):
        row = jnp.where(tile_rows == parts * g + p, dens_tile, 0.0)
        value = 2.0 * jnp.sum(jnp.sum(row, axis=1, keepdims=True), axis=0, keepdims=True)
        d.append(value.astype(jnp.bfloat16).astype(jnp.float32))
    order = (2, 3, 1, 0)
    work = {}
    for i in range(4):
        work.setdefault(5 + 2 * i, []).append((coulomb_part, (order[i], d)))
        if i < 3:
            work.setdefault(5 + 2 * i + 3, []).append((coulomb_sum, (order[i],)))
    for t in range(5, CHUNKS - 1):
        for act, given in work.get(t, ()):
            act(*given)
        slot(t)
    for t in range(CHUNKS - 1, CHUNKS + 6):
        for act, given in work.get(t, ()):
            act(*given)
    slot(15)
    cross = [(k, n) for n in range(PIECES) for k in (2, 3)]

    def coulomb_start():
        for k, n in cross[:FLIGHT]:
            cr_copy(k, n).start()

    @pl.when(is_end)
    def _():
        coulomb_start()

    slot(CHUNKS)

    @pl.when(is_mid)
    def _():
        coulomb_start()

    coulomb_sum(order[3])
    potentials()
    for t in range(CHUNKS + 1, CHUNKS + LAG):
        slot(t)

    for n in range(PIECES):
        cr_copy(1, n).start()

    def arrive(c, carry):
        for k in (1, 2, 3):
            pl_wait(c, k)

            @pl.when(for_mate(c))
            def _():
                xm_copy(lax.bitwise_xor(a, k), c).start()

        return carry

    def next_cross(q):
        cr_copy(*cross[q - FLIGHT]).wait_send()
        cr_copy(*cross[q]).start()

    seen = 0
    for q, until in ((4, 13), (5, CHUNKS)):
        next_cross(q)
        lax.fori_loop(seen, until, arrive, 0)
        seen = until
    next_cross(6)
    for i in range(per_own):
        xo_copy(i).wait_recv()
    dims = (((1,), (1,)), ((), ()))
    own_rows = pl.ds(pl.multiple_of(a * rows + z * own, own), own)

    def exchange(block, carry):
        def body(j, inside):
            for i in range(tile // chunk):
                xm_copy(block, j * (tile // chunk) + i).wait_recv()
            total = jnp.zeros((own, tile), jnp.float32)
            near = pl.ds(pl.multiple_of(block * rows + g * half + j * tile, tile), tile)
            far = pl.ds(pl.multiple_of(block * half + j * tile, tile), tile)
            for p in range(parts):
                total += lax.dot_general(
                    xa_ref[p, own_rows, :], xa_ref[p, near, :], dims, preferred_element_type=jnp.float32
                )
                total += lax.dot_general(
                    xo_ref[p], xm_ref[p, far, :], dims, preferred_element_type=jnp.float32
                )
            first = jnp.where(block == a, g * half + j * tile - z * own, -4 * rows)
            field_row = a * row_blocks + g * (half // BLK) + j * (tile // BLK)
            field = jnp.concatenate(
                [s_ref[pl.ds(field_row + i, 1), :] for i in range(tile // BLK)], axis=1
            )
            diagonal = lax.broadcasted_iota(jnp.int32, (own, tile), 0) == first + lax.broadcasted_iota(
                jnp.int32, (own, tile), 1
            )
            total = jnp.where(diagonal, field, 0.0) - 0.5 * total
            eb_ref[block, :, pl.ds(pl.multiple_of(j * tile, tile), tile)] = total.astype(jnp.bfloat16)
            return inside

        return lax.fori_loop(0, half // tile, body, carry)

    lax.fori_loop(0, 2, exchange, 0)
    next_cross(7)
    lax.fori_loop(2, 4, exchange, 0)

    def out_cols(block, core):
        return pl.ds(pl.multiple_of(block * cols + core * half, half), half)

    def piece_at(n):
        return pl.ds(pl.multiple_of(n * piece, piece), piece)

    def om_copy(block, n, core):
        return remote(
            eb_ref.at[block, piece_at(n)], out_ref.at[piece_at(n), out_cols(block, core)],
            om_send.at[block, n], om_recv.at[block, n], mate,
        )

    def ol_copy(block, n):
        return pltpu.make_async_copy(
            eb_ref.at[block, piece_at(n)], out_ref.at[piece_at(n), out_cols(block, g)], ol_sem.at[block, n]
        )

    def finish_piece(block, n):
        step = 64

        def body(i, carry):
            part = pl.ds(pl.multiple_of(n * piece + i * step, step), step)
            both = eb_ref[block, part, :].astype(jnp.float32) + cr_ref[block, part, :].astype(jnp.float32)
            eb_ref[block, part, :] = both.astype(jnp.bfloat16)
            return carry

        lax.fori_loop(0, piece // step, body, 0)
        om_copy(block, n, g).start()
        ol_copy(block, n).start()

    def finish_near(n, carry):
        finish_piece(z, n)
        cr_wait(1, n)
        finish_piece(lax.bitwise_xor(z, 1), n)
        return carry

    lax.fori_loop(0, PIECES, finish_near, 0)

    def finish_cross(n, carry):
        for k in (2, 3):
            cr_wait(k, n)
            finish_piece(lax.bitwise_xor(z, k), n)
        return carry

    lax.fori_loop(0, PIECES, finish_cross, 0)

    for k, n in cross[-FLIGHT:] + [(1, n) for n in range(PIECES)]:
        cr_copy(k, n).wait_send()

    def drain_out(block, carry):
        for n in range(PIECES):
            om_copy(block, n, 1 - g).wait()
            ol_copy(block, n).wait()
        mr_copy(block).wait_send()
        return carry

    lax.fori_loop(0, 4, drain_out, 0)

    @pl.when(rel == 0)
    def _():
        for i in range(2, 4):
            quarter_copy(c_ref, first, i, mate).wait_send()

    @pl.when(rel != 0)
    def _():
        for i in range(2):
            quarter_copy(cw_ref, first, i, mate).wait_send()

    @pl.when((rel == 1) | (rel == 2))
    def _():
        quarter_copy(cw_ref, first, 2, mate).wait_send()

    def drain(c, carry):
        @pl.when(is_mid)
        def _():
            rb_copy(c).wait_send()
            xe_copy(c).wait_send()

        for k in (1, 2, 3):
            pl_copy(c, k).wait_send()

        @pl.when(for_mate(c))
        def _():
            for block in range(4):
                xm_copy(block, c).wait_send()

        return carry

    lax.fori_loop(0, CHUNKS, drain, 0)
    for i in range(per_own):
        xo_copy(i).wait_send()


def grid_call(fitted, block_mask, own_c, nuclear, centres, positions, charges, neighbours):
    parts, rows, cols = fitted.shape
    nocc = own_c.shape[1]
    own, half = rows // 4, cols // 2
    block_total = block_mask.shape[1]
    small = (2 * block_total + 8, BLK)
    bf16, f32 = jnp.bfloat16, jnp.float32
    vmem = pl.BlockSpec(memory_space=pltpu.VMEM)
    hbm = pl.BlockSpec(memory_space=pl.ANY)
    dma = pltpu.SemaphoreType.DMA
    return pl.pallas_call(
        grid_kernel,
        in_specs=[hbm] + [vmem] * 7,
        out_specs=[hbm, vmem],
        out_shape=[
            jax.ShapeDtypeStruct((own, 4 * cols), bf16),
            jax.ShapeDtypeStruct((1, positions.shape[1]), f32),
        ],
        scratch_shapes=[
            pltpu.VMEM((parts, rows, cols), bf16),
            pltpu.VMEM((rows // BLK, 1, cols), bf16),
            pltpu.VMEM((neighbours.shape[1], BLK, positions.shape[1]), f32),
            pltpu.VMEM((cols, nocc), bf16),
            pltpu.VMEM((parts, rows, nocc), bf16),
            pltpu.VMEM((parts, rows, nocc), bf16),
            pltpu.VMEM((parts, rows, nocc), bf16),
            pltpu.VMEM((parts, 4 * rows, nocc), bf16),
            pltpu.VMEM((parts, 2 * rows, nocc), bf16),
            pltpu.VMEM((parts, own, nocc), bf16),
            pltpu.VMEM((4, own, half), bf16),
            pltpu.VMEM((4, own, half), bf16),
            pltpu.VMEM((4, own, half), bf16),
            pltpu.VMEM(small, f32),
            pltpu.VMEM((6,) + small, f32),
            pltpu.VMEM((parts, 8, nocc), f32),
            dma((STEPS,)),
            dma((4,)), dma((4,)),
            dma((CHUNKS,)), dma((CHUNKS,)),
            dma((CHUNKS,)), dma((CHUNKS,)),
            dma((CHUNKS,)), dma((CHUNKS,)),
            dma((3, CHUNKS)), dma((3, CHUNKS)),
            dma((2 * CHUNKS,)), dma((2 * CHUNKS,)),
            dma((own * CHUNKS // rows,)), dma((own * CHUNKS // rows,)),
            dma((6,)), dma((6,)),
            dma((4,)), dma((4,)),
            dma((3, PIECES)), dma((3, PIECES)),
            dma((4, PIECES)), dma((4, PIECES)),
            dma((4, PIECES)),
        ],
        compiler_params=pltpu.CompilerParams(
            collective_id=0, has_side_effects=True, vmem_limit_bytes=GRID_VMEM
        ),
        cost_estimate=pl.CostEstimate(
            flops=2 * parts * rows * cols * nocc + 8 * parts * own * 2 * cols * nocc,
            bytes_accessed=2 * parts * rows * cols + 8 * own * cols,
            transcendentals=0,
        ),
        name="grid",
    )(
        fitted, block_mask, own_c, nuclear.reshape(block_total, BLK), centres, positions,
        charges.reshape(1, -1), neighbours,
    )


def finish_kernel(in_hbm, out_hbm, in_ref, out_ref, in_sem, out_sem):
    pieces = in_sem.shape[0]
    rows = in_ref.shape[0] // pieces

    def load(n):
        span = pl.ds(pl.multiple_of(n * rows, rows), rows)
        return pltpu.make_async_copy(in_hbm.at[span], in_ref.at[span], in_sem.at[n])

    def save(n):
        span = pl.ds(pl.multiple_of(n * rows, rows), rows)
        return pltpu.make_async_copy(out_ref.at[span], out_hbm.at[span], out_sem.at[n])

    for n in range(pieces):
        load(n).start()

    def widen(n, carry):
        load(n).wait()
        for r in range(rows // 16):
            span = pl.ds(pl.multiple_of(n * rows + r * 16, 16), 16)
            out_ref[span, :] = in_ref[span, :].astype(jnp.float32)
        save(n).start()
        return carry

    lax.fori_loop(0, pieces, widen, 0)
    for n in range(pieces):
        save(n).wait()


def finish_call(fock16):
    rows, cols = fock16.shape
    pieces = rows // 32
    hbm = pl.BlockSpec(memory_space=pl.ANY)
    return pl.pallas_call(
        finish_kernel,
        in_specs=[hbm],
        out_specs=hbm,
        out_shape=jax.ShapeDtypeStruct((rows, cols), jnp.float32),
        scratch_shapes=[
            pltpu.VMEM((rows, cols), jnp.bfloat16),
            pltpu.VMEM((rows, cols), jnp.float32),
            pltpu.SemaphoreType.DMA((pieces,)),
            pltpu.SemaphoreType.DMA((pieces,)),
        ],
        compiler_params=pltpu.CompilerParams(vmem_limit_bytes=VMEM_LIMIT),
        cost_estimate=pl.CostEstimate(
            flops=rows * cols, bytes_accessed=6 * rows * cols, transcendentals=0
        ),
        name="finish",
    )(fock16)


def per_device_grid(
    fitted_tensor, block_mask, orbitals, nuclear, centres, mm_positions, mm_charges, neighbours
):
    fock16, potential = grid_call(
        fitted_tensor, block_mask, orbitals, nuclear, centres, mm_positions, mm_charges, neighbours
    )
    return (finish_call(fock16), potential.reshape(-1))


def grid_fits(mesh, fitted_tensor, orbitals):
    shape = mesh.shape
    parts = fitted_tensor.shape[0] // shape["grp"]
    rows = fitted_tensor.shape[1] // shape["aux"]
    cols = fitted_tensor.shape[2] // shape["orb"]
    return (
        shape["grp"] == 2
        and shape["aux"] == 4
        and shape["orb"] == 4
        and parts == 2
        and rows == cols
        and rows % (CHUNKS * BLK) == 0
        and rows % (2 * STEPS * BLK) == 0
        and orbitals.shape[1] % BLK == 0
        and 7 * rows * cols + 41 * rows * orbitals.shape[1] <= 52 * 2**20
    )


def solution(mesh):
    in_specs = (
        P("grp", "aux", "orb"),
        P("grp", None, None),
        P("aux", None),
        P(),
        P(),
        P(None, ("grp", "aux", "orb")),
        P(("grp", "aux", "orb")),
        P(("grp", "aux", "orb"), None),
    )
    out_specs = (P(("aux", "orb"), None), P(("grp", "aux", "orb")))
    def build(body):
        return jax.shard_map(
            body, mesh=mesh, in_specs=in_specs, out_specs=out_specs, check_vma=False
        )

    def run(fitted_tensor, block_mask, orbitals, *rest):
        body = per_device_grid if grid_fits(mesh, fitted_tensor, orbitals) else per_device
        return build(body)(fitted_tensor, block_mask, orbitals, *rest)

    return run
```
